32 devices in a mesh: outer: 2 (over y), rep: 4 (over x, core), shard: 4 (over z).
Axes of the slice: x: 2, y: 2, z: 4, core: 2. Of those that a mesh axis runs over, the one named last changes fastest.
Arguments:
- hidden: bfloat16 [4096, 8192], P(('outer', 'rep'), 'shard'), parts along dimension 0, may hold values from -256 to 256
- norm_gain: bfloat16 [8192], P('shard'), may hold values from 0.099609375 to 1.8984375
- kv_weight: bfloat16 [8192, 2048], P('shard'), may hold values from -0.0625 to 0.0625
- restore_jobs: int32 [16, 3], P('outer'), parts along dimension 0, may hold values from 0 to 7, as said below
- page_table: int32 [64, 2, 4], P(('outer', 'rep'), None, 'shard'), parts along dimension 0, may hold values from 0 to 15, as said below
- context_lengths: int32 [64], P(('outer', 'rep')), parts along dimension 0, may hold values from 64 to 512, as said below
- queries: bfloat16 [64, 8192], P(('outer', 'rep')), parts along dimension 0, may hold values from -12 to 12
- kv_pool: bfloat16 [512, 64, 2048], P(('outer', 'rep', 'shard')), parts along dimension 0, may hold values from -10 to 10
Outputs:
- new_pool: bfloat16 [512, 64, 2048], P(('outer', 'rep', 'shard')), parts along dimension 0
- attention_out: bfloat16 [64, 8192], P(('outer', 'rep'), 'shard'), parts along dimension 0
The draws below stay inside these ranges and needn't reach their ends.
There are 2 independent parts, one for each index of `outer`. The reference program is written for one: setup_inputs(seed, part) draws one part's arguments, and reference() takes and returns one part's arrays. A program takes and returns all parts, laid end to end along the dimension named above; an argument that names none is the same for every part. Nothing has to cross between parts.
Inputs may be any that keep to these rules, and one draw needn't show every extreme that they name: `restore_jobs`: rows j * 2 to j * 2 + 1 are the restorations whose saved rows sit on replica j, in the order of its stripes; they name different destination replicas. The stripe index b names positions b * 256 to b * 256 + 255 of the destination context. No two rows name the same destination replica and slot. At most 3 rows name one destination replica, and exactly 3 rows name one. Some row names slot 7 and some row names stripe 2 - 1. `page_table`: for each replica and each index of shard, the entries of that index over the replica's contexts and pages are a permutation of 0 to 15. `context_lengths`: some context has exactly 64 positions and some has 512. A restored context is at least as long as the end of its restored stripe.
All inputs are finite; a program needn't handle non-finite values.
Results may differ from the reference program's by a relative error of at most 0.028.
Values may be sent and summed in bfloat16 or wider, within the bound.
No kernel may reach another device: no remote copies, remote signals or barrier semaphores. Data moves between devices by JAX's collectives and lax.ppermute only.
A program may use at most 128 MiB of HBM per device.

```python
import math
from functools import partial
import jax
import jax.numpy as jnp
from jax import lax

D = 8192
QH = 64
KVH = 8
HD = 128
PAGE = 64
SENDS = 2
DEST_CAP = 3
SLOTS = 8
PAGES_DEV = 2
STRIPE = 256
CTX = 512
POOL_DEV = 16
N_REP = 4
N_SHARD = 4


def restore_plan(key):
    key = jax.random.fold_in(key, 11)
    key_source, key_target, key_slot, key_stripe, key_length, key_short, key_flip = jax.random.split(key, 7)
    job_count = N_REP * SENDS
    sources = jax.random.permutation(key_source, N_REP)
    targets = jax.random.permutation(key_target, N_REP).astype(jnp.int32)
    ranks = jnp.arange(N_REP, dtype=jnp.int32)
    first = targets[ranks]
    second_rank = jnp.where(ranks == N_REP - 1, 1, (ranks + 1) % N_REP)
    second = targets[second_rank]
    pair = jnp.stack([first, second], axis=1)
    flip = jax.random.randint(key_flip, (N_REP, 1), 0, 2).astype(jnp.int32)
    pair = jnp.where(flip == 1, pair[:, ::-1], pair)
    destination = jnp.zeros((N_REP, SENDS), jnp.int32).at[sources].set(pair).reshape(job_count)
    order = jnp.arange(job_count, dtype=jnp.int32)
    same = (destination[:, None] == destination[None, :]) & (order[:, None] > order[None, :])
    rank_in_target = jnp.sum(same.astype(jnp.int32), axis=1).astype(jnp.int32)
    slot_order = jax.random.permutation(key_slot, SLOTS).astype(jnp.int32)
    top_place = jnp.argmax(slot_order).astype(jnp.int32)
    slot_order = jnp.roll(slot_order, -top_place)
    context = slot_order[rank_in_target]
    stripe_index = jax.random.randint(key_stripe, (job_count,), 0, PAGES_DEV).astype(jnp.int32)
    stripe_index = stripe_index.at[0].set(PAGES_DEV - 1)
    lengths = jax.random.randint(key_length, (N_REP * SLOTS,), PAGE, CTX + 1).astype(jnp.int32)
    short_rep = jax.random.randint(key_short, (), 0, N_REP).astype(jnp.int32)
    lengths = lengths.at[short_rep * SLOTS + slot_order[DEST_CAP]].set(PAGE)
    lengths = lengths.at[(short_rep + 1) % N_REP * SLOTS + slot_order[DEST_CAP]].set(CTX)
    lengths = lengths.at[destination * SLOTS + context].max((stripe_index + 1) * STRIPE)
    jobs = jnp.stack([destination, context, stripe_index], axis=1).astype(jnp.int32)
    return (jobs, lengths.astype(jnp.int32))


def query_base(key):
    return jax.random.normal(jax.random.fold_in(key, 17), (N_REP * SLOTS, QH * HD), jnp.float32)


def draw_restore_jobs(key, part):
    return restore_plan(key)[0]


def draw_context_lengths(key, part):
    return restore_plan(key)[1]


def draw_page_table(key, part):
    key = jax.random.fold_in(key, 3)
    keys = jax.random.split(key, N_REP * N_SHARD)
    perms = jax.vmap(partial(jax.random.permutation, x=POOL_DEV))(keys)
    perms = perms.reshape(N_REP, N_SHARD, SLOTS, PAGES_DEV).transpose(0, 2, 3, 1)
    return perms.reshape(N_REP * SLOTS, PAGES_DEV, N_SHARD).astype(jnp.int32)


def draw_queries(key, part):
    base = query_base(key)
    return jnp.clip(3.0 * base, -12.0, 12.0).astype(jnp.bfloat16)


def draw_kv_pool(key, part):
    key = jax.random.fold_in(key, 7)
    pages = N_REP * N_SHARD * POOL_DEV
    kv_width = 2 * KVH * HD
    pool = jax.random.normal(key, (pages, PAGE, kv_width), jnp.float32)
    return jnp.clip(pool, -4.0, 4.0).astype(jnp.bfloat16)


def draw_hidden(key, part):
    key = jax.random.fold_in(key, 9)
    key_value, key_row, key_column = jax.random.split(key, 3)
    row_count = N_REP * SENDS * STRIPE
    trend = jnp.sqrt(1.0 + 2.0 * jnp.arange(D, dtype=jnp.float32) / (D - 1))
    column_scale = trend * jnp.exp(jax.random.uniform(key_column, (D,), jnp.float32, jnp.log(0.5), jnp.log(5.0)))
    row_scale = jnp.exp(jax.random.uniform(key_row, (row_count, 1), jnp.float32, 0.0, jnp.log(10.0)))
    values = jnp.clip(jax.random.normal(key_value, (row_count, D), jnp.float32), -4.0, 4.0)
    return (values * column_scale[None, :] * row_scale * 0.3).astype(jnp.bfloat16)


def level_of(key, extent, shards, low, largest):
    loudness = 1.0
    for position, shards_of in shards:
        steps = jax.random.uniform(jax.random.fold_in(jax.random.fold_in(key, 6), position), (shards_of,), jnp.float32, low / len(shards), largest / len(shards))
        loudness = loudness * jnp.repeat(jnp.exp(steps), extent[position] // shards_of).reshape((-1,) + (1,) * (len(extent) - 1 - position))
    return loudness


def scatter_about(rng, extent, deviation, limit, cuts=(), kind=jnp.bfloat16):
    values = deviation * jax.random.normal(rng, extent, jnp.float32)
    if cuts:
        values = values * level_of(rng, extent, cuts, -0.22, 0.18)
    return jnp.clip(values, -limit, limit).astype(kind)


def setup_inputs(seed: int = 0, part: int = 0) -> dict:
    arg_keys = jax.random.split(jax.random.key(seed), 9)
    part_splits = jax.random.split(jax.random.fold_in(arg_keys[8], part), 9)
    hidden = draw_hidden(jax.random.fold_in(jax.random.fold_in(arg_keys[8], part), 71), part)
    norm_gain = jnp.clip(1.0 + 0.18 * jax.random.normal(arg_keys[1], (D,), jnp.float32), 0.099609375, 1.8984375).astype(jnp.bfloat16)
    kv_weight = scatter_about(arg_keys[2], (D, 2 * KVH * HD), D ** -0.5, 0.0625, ((0, 4),))
    restore_jobs = draw_restore_jobs(jax.random.fold_in(jax.random.fold_in(arg_keys[8], part), 71), part)
    page_table = draw_page_table(jax.random.fold_in(jax.random.fold_in(arg_keys[8], part), 71), part)
    context_lengths = draw_context_lengths(jax.random.fold_in(jax.random.fold_in(arg_keys[8], part), 71), part)
    queries = draw_queries(jax.random.fold_in(jax.random.fold_in(arg_keys[8], part), 71), part)
    kv_pool = draw_kv_pool(jax.random.fold_in(jax.random.fold_in(arg_keys[8], part), 71), part)
    return dict(hidden=hidden, norm_gain=norm_gain, kv_weight=kv_weight, restore_jobs=restore_jobs, page_table=page_table, context_lengths=context_lengths, queries=queries, kv_pool=kv_pool)


THETA = 500000.0
EPS = 1e-05
FLOOR_SCORE = -1e+30

def rotate(key_rows, positions):
    half_dim = key_rows.shape[-1] // 2
    frequency = THETA ** (-(jnp.arange(half_dim, dtype=jnp.float32) * 2.0 / key_rows.shape[-1]))
    angles = positions.astype(jnp.float32)[:, None] * frequency[None, :]
    cosine = jnp.cos(angles)[:, None, :]
    sine_part = jnp.sin(angles)[:, None, :]
    first_half = key_rows[..., :half_dim]
    second = key_rows[..., half_dim:]
    return jnp.concatenate([first_half * cosine - second * sine_part, second * cosine + first_half * sine_part], axis=-1)

def finish(projected, inverse, positions):
    row_count = projected.shape[0]
    half_width = projected.shape[1] // 2
    scaled = projected * inverse[:, None]
    key_rows = rotate(scaled[:, :half_width].reshape(row_count, KVH, HD), positions).reshape(row_count, half_width)
    return jnp.concatenate([key_rows, scaled[:, half_width:]], axis=1).astype(jnp.bfloat16)

def reference(hidden, norm_gain, kv_weight, restore_jobs, page_table, context_lengths, queries, kv_pool):
    kv_width = 2 * KVH * HD
    job_count = N_REP * SENDS
    row_count = job_count * STRIPE
    wide = hidden.astype(jnp.float32)
    inverse = lax.rsqrt(lax.optimization_barrier(jnp.sum(wide * wide, axis=1)) / D + EPS)
    gained = (wide * norm_gain.astype(jnp.float32)[None, :]).astype(jnp.bfloat16)
    blocks = gained.reshape(row_count, N_SHARD, D // N_SHARD).transpose(1, 0, 2)
    weight_blocks = kv_weight.reshape(N_SHARD, D // N_SHARD, kv_width)

    def add_block(running, pair):
        partial_sum = jnp.dot(pair[0], pair[1], preferred_element_type=jnp.float32).astype(jnp.bfloat16)
        partial_sum = lax.optimization_barrier(partial_sum)
        return (running + partial_sum.astype(jnp.float32), None)
    projected, _ = lax.scan(add_block, jnp.zeros((row_count, kv_width), jnp.float32), (blocks, weight_blocks))
    destination = restore_jobs[:, 0]
    context = restore_jobs[:, 1]
    stripe_index = restore_jobs[:, 2]
    positions = jnp.repeat(stripe_index, STRIPE) * STRIPE + jnp.tile(jnp.arange(STRIPE, dtype=jnp.int32), job_count)
    restored = finish(projected, inverse, positions)
    owners = jnp.arange(N_SHARD, dtype=jnp.int32)
    physical = page_table[destination * SLOTS + context][jnp.arange(job_count, dtype=jnp.int32), stripe_index]
    target = (destination[:, None] * N_SHARD + owners[None, :]) * POOL_DEV + physical
    new_pool = kv_pool.at[target.reshape(-1)].set(restored.reshape(job_count * N_SHARD, PAGE, kv_width))
    scale = 1.0 / math.sqrt(HD)
    group = QH // KVH

    def attend(context_index):
        replica = context_index // SLOTS
        physical_pages = (replica * N_SHARD + owners[None, :]) * POOL_DEV + page_table[context_index]
        cached = new_pool[physical_pages.reshape(-1)].reshape(CTX, kv_width).astype(jnp.float32)
        key_rows = cached[:, :KVH * HD].reshape(CTX, KVH, HD)
        value_rows = cached[:, KVH * HD:].reshape(PAGES_DEV, N_SHARD, PAGE, KVH, HD)
        query_rows = queries[context_index].astype(jnp.float32).reshape(KVH, group, HD)
        scores = jnp.einsum('gmd,pgd->gmp', query_rows, key_rows) * scale
        scores = scores.reshape(KVH, group, PAGES_DEV, N_SHARD, PAGE)
        usable = (jnp.arange(CTX, dtype=jnp.int32) < context_lengths[context_index]).reshape(PAGES_DEV, N_SHARD, PAGE)[None, None]
        block_max = lax.optimization_barrier(jnp.max(jnp.where(usable, scores, FLOOR_SCORE), axis=(2, 4), keepdims=True))
        weights = jnp.where(usable, jnp.exp(scores - block_max), 0.0)
        row_max = lax.optimization_barrier(jnp.max(block_max, axis=3, keepdims=True))
        factor = jnp.exp(block_max - row_max)
        denominator = lax.optimization_barrier(jnp.sum(weights * factor, axis=(2, 3, 4)))
        rounded = lax.optimization_barrier(weights.astype(jnp.bfloat16)).astype(jnp.float32)
        block_sums = jnp.einsum('gmknp,knpgd->gmnd', rounded, value_rows)
        numerator = lax.optimization_barrier(jnp.sum(block_sums * factor[:, :, 0, :, 0][..., None], axis=2))
        return (numerator / denominator[..., None]).reshape(QH * HD).astype(jnp.bfloat16)
    attention_out = lax.map(attend, jnp.arange(N_REP * SLOTS, dtype=jnp.int32))
    return (new_pool, attention_out)
```

```python
import functools
import math

import jax
import jax.numpy as jnp
from jax import lax
from jax.experimental import pallas as pl
from jax.experimental.pallas import tpu as pltpu
from jax.sharding import PartitionSpec as P

D = 8192
QH = 64
KVH = 8
HD = 128
SENDS = 2


THETA = 500000.0
EPS = 1e-05
FLOOR_SCORE = -1e30


def rotate(key_rows, positions):
    half_dim = key_rows.shape[-1] // 2
    frequency = THETA ** (-(jnp.arange(half_dim, dtype=jnp.float32) * 2.0 / key_rows.shape[-1]))
    angles = positions.astype(jnp.float32)[:, None] * frequency[None, :]
    cosine = jnp.cos(angles)[:, None, :]
    sine_part = jnp.sin(angles)[:, None, :]
    first_half = key_rows[..., :half_dim]
    second = key_rows[..., half_dim:]
    return jnp.concatenate(
        [first_half * cosine - second * sine_part, second * cosine + first_half * sine_part],
        axis=-1,
    )


def finish(projected, inverse, positions):
    row_count = projected.shape[0]
    half_width = projected.shape[1] // 2
    scaled = projected * inverse[:, None]
    key_rows = rotate(scaled[:, :half_width].reshape(row_count, KVH, HD), positions).reshape(
        row_count, half_width
    )
    return jnp.concatenate([key_rows, scaled[:, half_width:]], axis=1).astype(jnp.bfloat16)


def spread_out(pieces, targets, replicas):
    outgoing = jnp.zeros((replicas,) + pieces.shape[1:], pieces.dtype)
    for send_index in range(SENDS):
        hit = (jnp.arange(replicas, dtype=jnp.int32) == targets[send_index])[:, None, None]
        outgoing = jnp.where(hit, pieces[send_index][None], outgoing)
    return outgoing


def on_device_general(
    hidden, norm_gain, kv_weight, restore_jobs, page_table, context_lengths, queries, kv_pool
):
    shards = lax.axis_size("shard")
    replicas = lax.axis_size("rep")
    my_replica = lax.axis_index("rep")
    my_shard = lax.axis_index("shard")
    stripe = hidden.shape[0] // SENDS
    page_len = stripe // shards
    features = hidden.shape[1]
    kv_width = kv_weight.shape[1]
    pool_pages = kv_pool.shape[0]
    destination = restore_jobs[:, 0]
    context = restore_jobs[:, 1]
    stripe_index = restore_jobs[:, 2]
    my_targets = lax.dynamic_slice_in_dim(destination, my_replica * SENDS, SENDS, 0)
    is_mine = destination == my_replica
    gain_wide = norm_gain.astype(jnp.float32)[None, :]
    page_rows = jnp.arange(page_len, dtype=jnp.int32)
    wide = hidden.astype(jnp.float32)
    squares = lax.psum(jnp.sum(wide * wide, axis=1), "shard")
    inverse = lax.rsqrt(squares / D + EPS)
    gained = (wide * gain_wide).astype(jnp.bfloat16)
    arranged = gained.reshape(SENDS, shards, page_len, features).transpose(1, 0, 2, 3)
    arranged = arranged.reshape(shards * SENDS * page_len, features)
    owned = lax.psum_scatter(
        jnp.dot(arranged, kv_weight, preferred_element_type=jnp.float32).astype(jnp.bfloat16),
        "shard",
        scatter_dimension=0,
        tiled=True,
    ).astype(jnp.float32)
    owned_inverse = lax.dynamic_slice_in_dim(
        inverse.reshape(SENDS, stripe), my_shard * page_len, page_len, 1
    )
    my_stripes = lax.dynamic_slice_in_dim(stripe_index, my_replica * SENDS, SENDS, 0)
    positions = my_stripes[:, None] * stripe + my_shard * page_len + page_rows[None, :]
    finished = finish(owned, owned_inverse.reshape(-1), positions.reshape(-1)).reshape(
        SENDS, page_len, kv_width
    )
    outgoing = spread_out(finished, my_targets, replicas)
    arrived = lax.all_to_all(outgoing, "rep", split_axis=0, concat_axis=0, tiled=True)
    mine_grid = is_mine.reshape(replicas, SENDS)
    has_page = jnp.any(mine_grid, axis=1)
    which = jnp.argmax(mine_grid.astype(jnp.int32), axis=1)
    job_index = jnp.arange(replicas, dtype=jnp.int32) * SENDS + which
    physical = jnp.where(
        has_page, page_table[context[job_index], stripe_index[job_index], 0], pool_pages
    )
    new_pool = kv_pool.at[physical].set(arrived, mode="drop")
    slots = queries.shape[0]
    pages_dev = page_table.shape[1]
    group = QH // KVH
    scale = 1.0 / math.sqrt(HD)
    cached = new_pool[page_table[:, :, 0]]
    key_rows = cached[..., : KVH * HD].reshape(slots, pages_dev * page_len, KVH, HD)
    value_rows = cached[..., KVH * HD :].reshape(slots, pages_dev * page_len, KVH, HD)
    query_rows = queries.reshape(slots, KVH, group, HD)
    scores = (
        jnp.einsum("cgmd,cpgd->cgmp", query_rows, key_rows, preferred_element_type=jnp.float32)
        * scale
    )
    position = (
        (jnp.arange(pages_dev, dtype=jnp.int32)[:, None] * shards + my_shard) * page_len
        + page_rows[None, :]
    ).reshape(-1)
    usable = (position[None, :] < context_lengths[:, None])[:, None, None, :]
    local_max = jnp.max(jnp.where(usable, scores, FLOOR_SCORE), axis=-1)
    weights = jnp.where(usable, jnp.exp(scores - local_max[..., None]), 0.0)
    denominator = jnp.sum(weights, axis=-1).reshape(slots, QH)
    numerator = jnp.einsum(
        "cgmp,cpgd->cgmd",
        weights.astype(jnp.bfloat16),
        value_rows,
        preferred_element_type=jnp.float32,
    )
    numerator = numerator.reshape(slots, QH, HD)
    local_max = local_max.reshape(slots, QH)
    heads_here = QH // shards
    row_max = lax.pmax(local_max, "shard")
    factor = jnp.exp(local_max - row_max)
    scaled_num = (numerator * factor[..., None]).reshape(slots, QH * HD)
    numerator, denominator = (
        lax.psum(scaled_num.astype(jnp.bfloat16), "shard").astype(jnp.float32),
        lax.psum((denominator * factor).astype(jnp.bfloat16), "shard").astype(jnp.float32),
    )
    numerator = lax.dynamic_slice_in_dim(numerator, my_shard * heads_here * HD, heads_here * HD, 1)
    denominator = lax.dynamic_slice_in_dim(denominator, my_shard * heads_here, heads_here, 1)
    numerator = numerator.reshape(slots, heads_here, HD)
    attention_out = numerator / denominator[..., None]
    return (new_pool, attention_out.reshape(slots, heads_here * HD).astype(jnp.bfloat16))


OUTWARD = [(0, 1), (3, 2)]
NEIGHBOUR = [(0, 1), (1, 0), (2, 3), (3, 2)]
FAR = [(1, 3), (2, 0)]
ACROSS = [(1, 2), (2, 1)]
LANES = 128
TILE = 256
BF16 = jnp.bfloat16
F32 = jnp.float32
SMEM = pltpu.SMEM
VMEM = pltpu.VMEM


def whole(space=VMEM):
    return pl.BlockSpec(memory_space=space)


def split_sum(total, offset):
    high = total.astype(BF16).astype(F32)
    low = total - high
    lane = lax.broadcasted_iota(jnp.int32, (total.shape[0], LANES), 1)
    return jnp.where(lane == offset, high, jnp.where(lane == offset + 1, low, 0.0)).astype(BF16)


def project_kernel(plan, first, second, gain, weight, *rest, keys, values, after):
    outs = rest[after : after + 2 * (keys + values)]
    gained = rest[-1]
    step = pl.program_id(0)
    rows = first.shape[0] * first.shape[2]

    @pl.when(step == 0)
    def _():
        for place, block in enumerate((first, second)):
            wide = block[...].reshape(rows, block.shape[3]).astype(F32)
            gained[place * rows : (place + 1) * rows, :] = (wide * gain[...]).astype(BF16)
            if keys:
                total = jnp.sum(wide * wide, axis=1, keepdims=True)
                width = outs[place].shape[1] - LANES
                outs[place][:, width:] = split_sum(total, plan[2])

    product = jnp.dot(gained[...], weight[...], preferred_element_type=F32).astype(BF16)

    def put(pair, tile):
        columns = pl.ds(pl.multiple_of(tile * TILE, TILE), TILE)
        pair[0][:, columns] = product[:rows]
        pair[1][:, columns] = product[rows:]

    if keys and values:
        half = pl.num_programs(0) // 2

        @pl.when(step < half)
        def _():
            put(outs[:2], step)

        @pl.when(step >= half)
        def _():
            put(outs[2:], step - half)
    else:
        put(outs, step)


def project(plan, hidden, gain, weight, after, keys, values):
    stripes, blocks, page_len, features = hidden.shape
    half = weight.shape[1] // 2
    rows = stripes * page_len
    tiles = half // TILE
    first_tile = 0 if keys else tiles
    shapes = []
    if keys:
        shapes += [jax.ShapeDtypeStruct((rows, half + LANES), BF16)] * 2
    if values:
        shapes += [jax.ShapeDtypeStruct((rows, half), BF16)] * 2
    steps = tiles * (keys + values)
    block = (stripes, 1, page_len, features)
    return pl.pallas_call(
        functools.partial(project_kernel, keys=keys, values=values, after=len(after)),
        grid_spec=pltpu.PrefetchScalarGridSpec(
            num_scalar_prefetch=1,
            grid=(steps,),
            in_specs=[
                pl.BlockSpec(block, lambda j, plan: (0, plan[0], 0, 0)),
                pl.BlockSpec(block, lambda j, plan: (0, plan[1], 0, 0)),
                pl.BlockSpec((1, features), lambda j, plan: (0, 0)),
                pl.BlockSpec((features, TILE), lambda j, plan: (0, j + first_tile)),
            ]
            + [whole(pl.ANY)] * len(after),
            out_specs=[pl.BlockSpec(s.shape, lambda j, plan: (0, 0)) for s in shapes],
            scratch_shapes=[pltpu.VMEM((2 * rows, features), BF16)],
        ),
        out_shape=shapes,
        compiler_params=pltpu.CompilerParams(vmem_limit_bytes=32 * 1024 * 1024),
        cost_estimate=pl.CostEstimate(
            flops=4 * rows * features * steps * TILE,
            bytes_accessed=2 * features * steps * TILE + 4 * rows * features,
            transcendentals=0,
        ),
        name="project_" + "k" * keys + "v" * values,
    )(plan, hidden, hidden, gain, weight, *after)


def attend(query, key_rows, value_rows, usable):
    heads = query.shape[0]
    width = key_rows.shape[1]
    group = heads // (width // LANES)
    head = lax.broadcasted_iota(jnp.int32, (heads, LANES), 0)
    spread = jnp.concatenate(
        [jnp.where(head // group == g, query, jnp.zeros_like(query)) for g in range(width // LANES)], axis=1
    )
    scores = lax.dot_general(spread, key_rows, (((1,), (1,)), ((), ())), preferred_element_type=F32)
    scores = jnp.where(usable, scores * (1.0 / math.sqrt(LANES)), FLOOR_SCORE)
    largest = jnp.max(scores, axis=1, keepdims=True)
    weights = jnp.where(usable, jnp.exp(scores - largest), 0.0)
    total = jnp.sum(weights, axis=1, keepdims=True)
    products = jnp.dot(weights.astype(BF16), value_rows, preferred_element_type=F32)
    picked = jnp.zeros((heads, LANES), F32)
    for g in range(width // LANES):
        picked = jnp.where(head // group == g, products[:, g * LANES : (g + 1) * LANES], picked)
    some = total > 0.0
    safe = jnp.where(some, total, 1.0)
    return picked / safe, jnp.where(some, largest + jnp.log(safe), FLOOR_SCORE)


def kept_kernel(jobs, table, lengths, query, page_a, page_b, pool, after, out, level, new_pool, sem, *, shards):
    context = pl.program_id(0)
    replica = lax.axis_index("rep")
    shard = lax.axis_index("shard")
    copy = pltpu.make_async_copy(pool, new_pool, sem)

    @pl.when(context == 0)
    def _():
        copy.start()

    gone = [jnp.int32(0), jnp.int32(0)]
    for job in range(jobs.shape[1]):
        hit = (jobs[0, job] == replica) & (jobs[1, job] == context)
        for page in range(2):
            gone[page] = gone[page] | (hit & (jobs[2, job] == page)).astype(jnp.int32)
    page_len = page_a.shape[1]
    half = page_a.shape[2] // 2
    lane = lax.broadcasted_iota(jnp.int32, (query.shape[1], 2 * page_len), 1)
    page = lane // page_len
    position = (page * shards + shard) * page_len + lane % page_len
    usable = (position < lengths[context]) & (jnp.where(page == 0, gone[0], gone[1]) == 0)
    key_rows = jnp.concatenate([page_a[0, :, :half], page_b[0, :, :half]], axis=0)
    value_rows = jnp.concatenate([page_a[0, :, half:], page_b[0, :, half:]], axis=0)
    result, logarithm = attend(query[0], key_rows, value_rows, usable)
    out[0] = result
    level[0] = jnp.broadcast_to(logarithm, result.shape)

    @pl.when(context == pl.num_programs(0) - 1)
    def _():
        copy.wait()


def kept(jobs, table, lengths, query, pool, after, shards):
    slots, heads, size = query.shape
    page = (1,) + pool.shape[1:]
    return pl.pallas_call(
        functools.partial(kept_kernel, shards=shards),
        grid_spec=pltpu.PrefetchScalarGridSpec(
            num_scalar_prefetch=3,
            grid=(slots,),
            in_specs=[
                pl.BlockSpec((1, heads, size), lambda c, jobs, table, lengths: (c, 0, 0)),
                pl.BlockSpec(page, lambda c, jobs, table, lengths: (table[0, c], 0, 0)),
                pl.BlockSpec(page, lambda c, jobs, table, lengths: (table[1, c], 0, 0)),
                whole(pl.ANY),
                whole(pl.ANY),
            ],
            out_specs=[
                pl.BlockSpec((1, heads, size), lambda c, jobs, table, lengths: (c, 0, 0)),
                pl.BlockSpec((1, heads, size), lambda c, jobs, table, lengths: (c, 0, 0)),
                whole(pl.ANY),
            ],
            scratch_shapes=[pltpu.SemaphoreType.DMA],
        ),
        out_shape=[
            jax.ShapeDtypeStruct((slots, heads, size), F32),
            jax.ShapeDtypeStruct((slots, heads, size), F32),
            jax.ShapeDtypeStruct(pool.shape, pool.dtype),
        ],
        compiler_params=pltpu.CompilerParams(vmem_limit_bytes=32 * 1024 * 1024),
        cost_estimate=pl.CostEstimate(flops=1 << 28, bytes_accessed=12 << 20, transcendentals=1 << 16),
        name="kept",
    )(jobs, table, lengths, query, pool, pool, pool, after)


def route(jobs, finished, outs):
    replica = lax.axis_index("rep")
    page_len = finished.shape[0] // SENDS
    for step, out in enumerate(outs):
        chosen = jobs[0, replica * SENDS] == jnp.bitwise_xor(replica, step)

        @pl.when(chosen)
        def _():
            out[...] = finished[:page_len]

        @pl.when(jnp.logical_not(chosen))
        def _():
            out[...] = finished[page_len:]


def finish_keys_kernel(jobs, own, near, far, across, frequency, *rest, stripe):
    outs, scale, finished = rest[:4], rest[4], rest[5]
    replica = lax.axis_index("rep")
    shard = lax.axis_index("shard")
    rows = own.shape[0]
    page_len = rows // SENDS
    width = own.shape[1] - LANES

    def added(columns):
        parts = [ref[:, columns].astype(F32) for ref in (own, near, far, across)]
        return (parts[0] + parts[1]) + (parts[2] + parts[3])

    squares = jnp.sum(added(slice(width, width + LANES)), axis=1, keepdims=True)
    inverse = jnp.broadcast_to(lax.rsqrt(squares / D + EPS), (rows, LANES))
    scale[...] = inverse
    row = lax.broadcasted_iota(jnp.int32, (rows, LANES), 0)
    lane = lax.broadcasted_iota(jnp.int32, (rows, LANES), 1)
    index = jnp.where(row < page_len, jobs[2, replica * SENDS], jobs[2, replica * SENDS + 1])
    position = index * stripe + shard * page_len + row % page_len
    angle = position.astype(F32) * frequency[...]
    cosine = jnp.cos(angle) * inverse
    sine_part = jnp.where(lane < LANES // 2, -jnp.sin(angle), jnp.sin(angle)) * inverse
    for head in range(width // LANES):
        columns = slice(head * LANES, (head + 1) * LANES)
        value = added(columns)
        turned = value * cosine + pltpu.roll(value, LANES // 2, 1) * sine_part
        finished[:, columns] = turned.astype(BF16)
    route(jobs, finished, outs)


def finish_values_kernel(jobs, own, near, far, across, scale, *rest):
    outs, finished = rest[:4], rest[4]
    for head in range(own.shape[1] // LANES):
        columns = slice(head * LANES, (head + 1) * LANES)
        parts = [ref[:, columns].astype(F32) for ref in (own, near, far, across)]
        total = (parts[0] + parts[1]) + (parts[2] + parts[3])
        finished[:, columns] = (total * scale[...]).astype(BF16)
    route(jobs, finished, outs)


def finish_part(jobs, parts, extra, stripe, keys):
    rows = parts[0].shape[0]
    width = parts[0].shape[1] - (LANES if keys else 0)
    page = jax.ShapeDtypeStruct((rows // SENDS, width), BF16)
    shapes = [page] * 4
    if keys:
        shapes.append(jax.ShapeDtypeStruct((rows, LANES), F32))
        kernel = functools.partial(finish_keys_kernel, stripe=stripe)
    else:
        kernel = finish_values_kernel
    return pl.pallas_call(
        kernel,
        in_specs=[whole(SMEM)] + [whole()] * 5,
        out_specs=[whole()] * len(shapes),
        out_shape=shapes,
        scratch_shapes=[pltpu.VMEM((rows, width), BF16)],
        cost_estimate=pl.CostEstimate(flops=1 << 21, bytes_accessed=2 << 20, transcendentals=1 << 15),
        name="finish_keys" if keys else "finish_values",
    )(jobs, *parts, extra)


def job_from(jobs, step):
    replica = lax.axis_index("rep")
    first = jnp.bitwise_xor(replica, step) * SENDS
    hit_first = jobs[0, first] == replica
    hit = hit_first | (jobs[0, first + 1] == replica)
    row = jnp.where(hit_first, first, first + 1)
    return hit, jobs[1, row], jobs[2, row]


def merge_kernel(jobs, lengths, query, kept_out, kept_level, *rest, shards):
    key_pages, value_pages = rest[:4], rest[4:8]
    outs, total, level = rest[8:12], rest[12], rest[13]
    shard = lax.axis_index("shard")
    heads = query.shape[1]
    page_len = key_pages[0].shape[0]
    total[...] = kept_out[...]
    level[...] = kept_level[...]
    for step in range(4):
        hit, context, page = job_from(jobs, step)

        @pl.when(hit)
        def _():
            lane = lax.broadcasted_iota(jnp.int32, (heads, page_len), 1)
            usable = (page * shards + shard) * page_len + lane < lengths[context]
            fresh, fresh_level = attend(query[context], key_pages[step][...], value_pages[step][...], usable)
            old_level = level[context]
            top = jnp.maximum(old_level, fresh_level)
            old_share = jnp.exp(old_level - top)
            fresh_share = jnp.exp(fresh_level - top)
            both = old_share + fresh_share
            total[context] = (total[context] * old_share + fresh * fresh_share) / both
            level[context] = top + jnp.log(both)

    slots = query.shape[0]
    here = heads // shards
    rows = slots * here
    place = lax.broadcasted_iota(jnp.int32, (16, LANES), 0)
    for step in range(4):
        start = pl.multiple_of(jnp.bitwise_xor(shard, step) * here, here)
        outs[step][:rows] = total[:, pl.ds(start, here), :].reshape(rows, LANES).astype(BF16)
        lines = level[:, pl.ds(start, here), :].reshape(rows, LANES).T[:16]
        high = lines.astype(BF16).astype(F32)
        middle = (lines - high).astype(BF16).astype(F32)
        low = lines - high - middle
        outs[step][rows:] = jnp.where(place == 0, high, jnp.where(place == 1, middle, jnp.where(place == 2, low, 0.0))).astype(BF16)


def merge(jobs, lengths, query, kept_out, kept_level, key_pages, value_pages, shards):
    slots, heads, size = query.shape
    rows = slots * heads // shards
    return pl.pallas_call(
        functools.partial(merge_kernel, shards=shards),
        in_specs=[whole(SMEM)] * 2 + [whole()] * 11,
        out_specs=[whole()] * 4,
        out_shape=[jax.ShapeDtypeStruct((rows + 16, size), BF16)] * 4,
        scratch_shapes=[pltpu.VMEM((slots, heads, size), F32)] * 2,
        cost_estimate=pl.CostEstimate(flops=1 << 26, bytes_accessed=2 << 20, transcendentals=1 << 15),
        name="merge",
    )(jobs, lengths, query, kept_out, kept_level, *key_pages, *value_pages)


def place_kernel(jobs, table, pool, *rest):
    key_pages, value_pages, out, sem = rest[:4], rest[4:8], rest[8], rest[9]
    half = key_pages[0].shape[1]
    for wait in (False, True):
        for step in range(4):
            hit, context, page = job_from(jobs, step)

            @pl.when(hit)
            def _():
                slot = table[page, context]
                for side, ref in enumerate((key_pages[step], value_pages[step])):
                    copy = pltpu.make_async_copy(
                        ref, out.at[slot, :, pl.ds(side * half, half)], sem.at[step, side]
                    )
                    if wait:
                        copy.wait()
                    else:
                        copy.start()


def place_pages(jobs, table, pool, key_pages, value_pages):
    return pl.pallas_call(
        place_kernel,
        in_specs=[whole(SMEM)] * 2 + [whole(pl.ANY)] * 9,
        out_specs=whole(pl.ANY),
        out_shape=jax.ShapeDtypeStruct(pool.shape, pool.dtype),
        scratch_shapes=[pltpu.SemaphoreType.DMA((4, 2))],
        input_output_aliases={2: 0},
        cost_estimate=pl.CostEstimate(flops=0, bytes_accessed=2 << 20, transcendentals=0),
        name="place_pages",
    )(jobs, table, pool, *key_pages, *value_pages)


def combine_kernel(*refs):
    parts, out, spread = refs[:4], refs[4], refs[5]
    slots, here, size = spread.shape
    rows = slots * here
    levels = []
    for ref in parts:
        tail = ref[rows:].astype(F32)
        line = jnp.sum(tail, axis=0, keepdims=True)
        levels.append(jnp.broadcast_to(line, (rows, rows)).T)
    top = functools.reduce(jnp.maximum, levels)
    total = jnp.zeros((rows, size), F32)
    both = jnp.zeros((rows, size), F32)
    for ref, level in zip(parts, levels):
        share = jnp.exp(level - top)
        total = total + ref[:rows].astype(F32) * share
        both = both + share
    spread[...] = (total / both).reshape(slots, here, size)
    for head in range(here):
        out[:, head * size : (head + 1) * size] = spread[:, head, :].astype(BF16)


def combine(parts, slots, here):
    size = parts[0].shape[1]
    return pl.pallas_call(
        combine_kernel,
        in_specs=[whole()] * 4,
        out_specs=whole(),
        out_shape=jax.ShapeDtypeStruct((slots, here * size), BF16),
        scratch_shapes=[pltpu.VMEM((slots, here, size), F32)],
        cost_estimate=pl.CostEstimate(flops=1 << 18, bytes_accessed=1 << 18, transcendentals=1 << 14),
        name="combine",
    )(*parts)


def added(left, right):
    return (left.astype(F32) + right.astype(F32)).astype(BF16)


def on_device(
    hidden, norm_gain, kv_weight, restore_jobs, page_table, context_lengths, queries, kv_pool
):
    shards = lax.axis_size("shard")
    replicas = lax.axis_size("rep")
    shard = lax.axis_index("shard")
    stripe = hidden.shape[0] // SENDS
    page_len = stripe // shards
    jobs = restore_jobs.T
    table = page_table[:, :, 0].T
    slots = queries.shape[0]
    query = queries.reshape(slots, QH, HD)
    blocks = hidden.reshape(SENDS, shards, page_len, hidden.shape[1])
    gain = norm_gain.astype(F32)[None, :]
    low = shard < 2
    offset = jnp.where((shard == 0) | (shard == 3), 0, 2)
    send_plan = jnp.stack([jnp.where(low, 3, 0), jnp.where(low, 2, 1), offset]).astype(jnp.int32)
    keep_plan = jnp.stack([shard, shard ^ 1, offset]).astype(jnp.int32)

    def along(array, pairs):
        return lax.ppermute(array, "shard", pairs)

    key_1, key_2 = project(send_plan, blocks, gain, kv_weight, [], True, False)
    key_in_1 = along(key_1, OUTWARD)
    key_in_2 = along(key_2, OUTWARD)
    value_1, value_2 = project(send_plan, blocks, gain, kv_weight, [key_1], False, True)
    value_in_1 = along(value_1, OUTWARD)
    value_in_2 = along(value_2, OUTWARD)
    key_0, key_3, value_0, value_3 = project(keep_plan, blocks, gain, kv_weight, [value_1], True, True)
    key_near = along(key_3, NEIGHBOUR)
    value_near = along(value_3, NEIGHBOUR)
    kept_out, kept_level, new_pool = kept(
        jobs, table, context_lengths, query, kv_pool, value_3, shards
    )
    key_far = along(added(key_1, key_in_1), FAR)
    key_across = along(added(key_2, key_in_2), ACROSS)
    value_far = along(added(value_1, value_in_1), FAR)
    value_across = along(added(value_2, value_in_2), ACROSS)
    frequency = THETA ** (-(jnp.arange(HD // 2, dtype=F32) * 2.0 / HD))
    frequency = jnp.concatenate([frequency, frequency])[None, :]
    *key_out, scale = finish_part(jobs, (key_0, key_near, key_far, key_across), frequency, stripe, True)

    def between(pages):
        return [pages[0]] + [
            lax.ppermute(pages[step], "rep", [(i, i ^ step) for i in range(replicas)])
            for step in range(1, replicas)
        ]

    key_pages = between(key_out)
    value_out = finish_part(jobs, (value_0, value_near, value_far, value_across), scale, stripe, False)
    value_pages = between(value_out)
    packed = merge(
        jobs, context_lengths, query, kept_out, kept_level, key_pages, value_pages, shards
    )
    parts = [packed[0]] + [
        along(packed[step], [(i, i ^ step) for i in range(shards)]) for step in range(1, shards)
    ]
    new_pool = place_pages(jobs, table, new_pool, key_pages, value_pages)
    return (new_pool, combine(parts, slots, QH // shards))


def solution(mesh):
    in_specs = (
        P(("outer", "rep"), "shard"),
        P("shard"),
        P("shard", None),
        P("outer", None),
        P(("outer", "rep"), None, "shard"),
        P(("outer", "rep")),
        P(("outer", "rep"), None),
        P(("outer", "rep", "shard"), None, None),
    )
    out_specs = (P(("outer", "rep", "shard"), None, None), P(("outer", "rep"), "shard"))
    fast = mesh.shape["shard"] == 4 and mesh.shape["rep"] == 4
    return jax.shard_map(
        on_device if fast else on_device_general, mesh=mesh, in_specs=in_specs, out_specs=out_specs, check_vma=False
    )
```

```python
import functools
import math

import jax
import jax.numpy as jnp
from jax import lax
from jax.experimental import pallas as pl
from jax.experimental.pallas import tpu as pltpu
from jax.sharding import PartitionSpec as P

D = 8192
QH = 64
KVH = 8
HD = 128
SENDS = 2


THETA = 500000.0
EPS = 1e-05
FLOOR_SCORE = -1e30


def rotate(key_rows, positions):
    half_dim = key_rows.shape[-1] // 2
    frequency = THETA ** (-(jnp.arange(half_dim, dtype=jnp.float32) * 2.0 / key_rows.shape[-1]))
    angles = positions.astype(jnp.float32)[:, None] * frequency[None, :]
    cosine = jnp.cos(angles)[:, None, :]
    sine_part = jnp.sin(angles)[:, None, :]
    first_half = key_rows[..., :half_dim]
    second = key_rows[..., half_dim:]
    return jnp.concatenate(
        [first_half * cosine - second * sine_part, second * cosine + first_half * sine_part],
        axis=-1,
    )


def finish(projected, inverse, positions):
    row_count = projected.shape[0]
    half_width = projected.shape[1] // 2
    scaled = projected * inverse[:, None]
    key_rows = rotate(scaled[:, :half_width].reshape(row_count, KVH, HD), positions).reshape(
        row_count, half_width
    )
    return jnp.concatenate([key_rows, scaled[:, half_width:]], axis=1).astype(jnp.bfloat16)


def spread_out(pieces, targets, replicas):
    outgoing = jnp.zeros((replicas,) + pieces.shape[1:], pieces.dtype)
    for send_index in range(SENDS):
        hit = (jnp.arange(replicas, dtype=jnp.int32) == targets[send_index])[:, None, None]
        outgoing = jnp.where(hit, pieces[send_index][None], outgoing)
    return outgoing


def on_device_general(
    hidden, norm_gain, kv_weight, restore_jobs, page_table, context_lengths, queries, kv_pool
):
    shards = lax.axis_size("shard")
    replicas = lax.axis_size("rep")
    my_replica = lax.axis_index("rep")
    my_shard = lax.axis_index("shard")
    stripe = hidden.shape[0] // SENDS
    page_len = stripe // shards
    features = hidden.shape[1]
    kv_width = kv_weight.shape[1]
    pool_pages = kv_pool.shape[0]
    destination = restore_jobs[:, 0]
    context = restore_jobs[:, 1]
    stripe_index = restore_jobs[:, 2]
    my_targets = lax.dynamic_slice_in_dim(destination, my_replica * SENDS, SENDS, 0)
    is_mine = destination == my_replica
    gain_wide = norm_gain.astype(jnp.float32)[None, :]
    page_rows = jnp.arange(page_len, dtype=jnp.int32)
    wide = hidden.astype(jnp.float32)
    squares = lax.psum(jnp.sum(wide * wide, axis=1), "shard")
    inverse = lax.rsqrt(squares / D + EPS)
    gained = (wide * gain_wide).astype(jnp.bfloat16)
    arranged = gained.reshape(SENDS, shards, page_len, features).transpose(1, 0, 2, 3)
    arranged = arranged.reshape(shards * SENDS * page_len, features)
    owned = lax.psum_scatter(
        jnp.dot(arranged, kv_weight, preferred_element_type=jnp.float32).astype(jnp.bfloat16),
        "shard",
        scatter_dimension=0,
        tiled=True,
    ).astype(jnp.float32)
    owned_inverse = lax.dynamic_slice_in_dim(
        inverse.reshape(SENDS, stripe), my_shard * page_len, page_len, 1
    )
    my_stripes = lax.dynamic_slice_in_dim(stripe_index, my_replica * SENDS, SENDS, 0)
    positions = my_stripes[:, None] * stripe + my_shard * page_len + page_rows[None, :]
    finished = finish(owned, owned_inverse.reshape(-1), positions.reshape(-1)).reshape(
        SENDS, page_len, kv_width
    )
    outgoing = spread_out(finished, my_targets, replicas)
    arrived = lax.all_to_all(outgoing, "rep", split_axis=0, concat_axis=0, tiled=True)
    mine_grid = is_mine.reshape(replicas, SENDS)
    has_page = jnp.any(mine_grid, axis=1)
    which = jnp.argmax(mine_grid.astype(jnp.int32), axis=1)
    job_index = jnp.arange(replicas, dtype=jnp.int32) * SENDS + which
    physical = jnp.where(
        has_page, page_table[context[job_index], stripe_index[job_index], 0], pool_pages
    )
    new_pool = kv_pool.at[physical].set(arrived, mode="drop")
    slots = queries.shape[0]
    pages_dev = page_table.shape[1]
    group = QH // KVH
    scale = 1.0 / math.sqrt(HD)
    cached = new_pool[page_table[:, :, 0]]
    key_rows = cached[..., : KVH * HD].reshape(slots, pages_dev * page_len, KVH, HD)
    value_rows = cached[..., KVH * HD :].reshape(slots, pages_dev * page_len, KVH, HD)
    query_rows = queries.reshape(slots, KVH, group, HD)
    scores = (
        jnp.einsum("cgmd,cpgd->cgmp", query_rows, key_rows, preferred_element_type=jnp.float32)
        * scale
    )
    position = (
        (jnp.arange(pages_dev, dtype=jnp.int32)[:, None] * shards + my_shard) * page_len
        + page_rows[None, :]
    ).reshape(-1)
    usable = (position[None, :] < context_lengths[:, None])[:, None, None, :]
    local_max = jnp.max(jnp.where(usable, scores, FLOOR_SCORE), axis=-1)
    weights = jnp.where(usable, jnp.exp(scores - local_max[..., None]), 0.0)
    denominator = jnp.sum(weights, axis=-1).reshape(slots, QH)
    numerator = jnp.einsum(
        "cgmp,cpgd->cgmd",
        weights.astype(jnp.bfloat16),
        value_rows,
        preferred_element_type=jnp.float32,
    )
    numerator = numerator.reshape(slots, QH, HD)
    local_max = local_max.reshape(slots, QH)
    heads_here = QH // shards
    row_max = lax.pmax(local_max, "shard")
    factor = jnp.exp(local_max - row_max)
    scaled_num = (numerator * factor[..., None]).reshape(slots, QH * HD)
    numerator, denominator = (
        lax.psum(scaled_num.astype(jnp.bfloat16), "shard").astype(jnp.float32),
        lax.psum((denominator * factor).astype(jnp.bfloat16), "shard").astype(jnp.float32),
    )
    numerator = lax.dynamic_slice_in_dim(numerator, my_shard * heads_here * HD, heads_here * HD, 1)
    denominator = lax.dynamic_slice_in_dim(denominator, my_shard * heads_here, heads_here, 1)
    numerator = numerator.reshape(slots, heads_here, HD)
    attention_out = numerator / denominator[..., None]
    return (new_pool, attention_out.reshape(slots, heads_here * HD).astype(jnp.bfloat16))


OUTWARD = [(0, 1), (3, 2)]
NEIGHBOUR = [(0, 1), (1, 0), (2, 3), (3, 2)]
FAR = [(1, 3), (2, 0)]
ACROSS = [(1, 2), (2, 1)]
LANES = 128
CHUNKS = 4
BF16 = jnp.bfloat16
F32 = jnp.float32
SMEM = pltpu.SMEM
VMEM = pltpu.VMEM
SMALL = pl.CostEstimate(flops=1, bytes_accessed=1, transcendentals=0)
LIMIT = 24 * 1024 * 1024


def whole(space=VMEM):
    return pl.BlockSpec(memory_space=space)


def split_sum(total, offset):
    high = total.astype(BF16).astype(F32)
    low = total - high
    lane = lax.broadcasted_iota(jnp.int32, (total.shape[0], LANES), 1)
    return jnp.where(lane == offset, high, jnp.where(lane == offset + 1, low, 0.0)).astype(BF16)


def project_kernel(hidden, gain, weight, *rest, sending, halves, after):
    outs = rest[after : after + 2 * len(halves)]
    rows_in, tiles, total, row_sem, tile_sem = rest[after + 2 * len(halves) :]
    shard = lax.axis_index("shard")
    lower = shard < 2
    if sending:
        places = [jnp.where(lower, 3, 0), jnp.where(lower, 2, 1)]
    else:
        places = [shard, jnp.bitwise_xor(shard, 1)]
    stripes, _, page_len, features = hidden.shape
    rows = stripes * page_len
    half = weight.shape[1] // 2
    depth = features // CHUNKS

    def row_copy(which, stripe):
        return pltpu.make_async_copy(
            hidden.at[stripe, places[which]],
            rows_in.at[pl.ds((which * stripes + stripe) * page_len, page_len)],
            row_sem.at[which, stripe],
        )

    def tile_copy(side, chunk):
        return pltpu.make_async_copy(
            weight.at[pl.ds(chunk * depth, depth), pl.ds(halves[side] * half, half)],
            tiles.at[side, pl.ds(chunk * depth, depth)],
            tile_sem.at[side, chunk],
        )

    copies = [(which, stripe) for which in range(2) for stripe in range(stripes)]
    for which, stripe in copies:
        row_copy(which, stripe).start()
    for side in range(len(halves)):
        for chunk in range(CHUNKS):
            tile_copy(side, chunk).start()
    for which, stripe in copies:
        row_copy(which, stripe).wait()
    squares = jnp.zeros((2 * rows, LANES), F32)
    for side in range(len(halves)):
        for chunk in range(CHUNKS):
            span = slice(chunk * depth, (chunk + 1) * depth)
            if side == 0:
                wide = rows_in[:, span].astype(F32)
                if halves[0] == 0:
                    for lane in range(depth // LANES):
                        part = wide[:, lane * LANES : (lane + 1) * LANES]
                        squares = squares + part * part
                rows_in[:, span] = (wide * gain[:, span]).astype(BF16)
            tile_copy(side, chunk).wait()
            product = jnp.dot(rows_in[:, span], tiles[side, span, :], preferred_element_type=F32)
            if chunk == 0:
                total[...] = product
            elif chunk < CHUNKS - 1:
                total[...] += product
            else:
                product = (total[...] + product).astype(BF16)
                for which in range(2):
                    outs[2 * side + which][:, :half] = product[which * rows : (which + 1) * rows]
    if halves[0] == 0:
        inner = (shard == 1) | (shard == 2)
        offset = jnp.where(inner, 2, 0)
        for which in range(2):
            block = jnp.sum(squares[which * rows : (which + 1) * rows], axis=1, keepdims=True)
            outs[which][:, half:] = split_sum(block, offset)


def project(hidden, gain, weight, after, sending, halves):
    stripes, blocks, page_len, features = hidden.shape
    half = weight.shape[1] // 2
    rows = stripes * page_len
    shapes = []
    for side in halves:
        shapes += [jax.ShapeDtypeStruct((rows, half + LANES * (side == 0)), BF16)] * 2
    return pl.pallas_call(
        functools.partial(project_kernel, sending=sending, halves=halves, after=len(after)),
        in_specs=[whole(pl.ANY), whole(), whole(pl.ANY)] + [whole(pl.ANY)] * len(after),
        out_specs=[whole()] * len(shapes),
        out_shape=shapes,
        scratch_shapes=[
            pltpu.VMEM((2 * rows, features), BF16),
            pltpu.VMEM((len(halves), features, half), BF16),
            pltpu.VMEM((2 * rows, half), F32),
            pltpu.SemaphoreType.DMA((2, stripes)),
            pltpu.SemaphoreType.DMA((len(halves), CHUNKS)),
        ],
        compiler_params=pltpu.CompilerParams(vmem_limit_bytes=LIMIT),
        cost_estimate=SMALL,
        name="project_" + ("send" if sending else "keep") + "_" + "".join("kv"[side] for side in halves),
    )(hidden, gain, weight, *after)


def attend(query, key_rows, value_rows, usable):
    heads = query.shape[0]
    width = key_rows.shape[1]
    group = heads // (width // LANES)
    head = lax.broadcasted_iota(jnp.int32, (heads, LANES), 0)
    spread = jnp.concatenate(
        [jnp.where(head // group == g, query, jnp.zeros_like(query)) for g in range(width // LANES)], axis=1
    )
    scores = lax.dot_general(spread, key_rows, (((1,), (1,)), ((), ())), preferred_element_type=F32)
    scores = jnp.where(usable, scores * (1.0 / math.sqrt(LANES)), FLOOR_SCORE)
    largest = jnp.max(scores, axis=1, keepdims=True)
    weights = jnp.where(usable, jnp.exp(scores - largest), 0.0)
    total = jnp.sum(weights, axis=1, keepdims=True)
    products = jnp.dot(weights.astype(BF16), value_rows, preferred_element_type=F32)
    picked = jnp.zeros((heads, LANES), F32)
    for g in range(width // LANES):
        picked = jnp.where(head // group == g, products[:, g * LANES : (g + 1) * LANES], picked)
    some = total > 0.0
    safe = jnp.where(some, total, 1.0)
    return picked / safe, jnp.where(some, largest + jnp.log(safe), FLOOR_SCORE)


def kept_kernel(jobs, table, lengths, query, page_a, page_b, after, out, level, new_pool, sem, *, shards):
    context = pl.program_id(0)
    replica = lax.axis_index("rep")
    shard = lax.axis_index("shard")
    copies = [
        pltpu.make_async_copy(ref, new_pool.at[pl.ds(table[page, context], 1)], sem.at[page])
        for page, ref in enumerate((page_a, page_b))
    ]
    for copy in copies:
        copy.start()
    gone = [jnp.int32(0), jnp.int32(0)]
    for job in range(jobs.shape[1]):
        hit = (jobs[0, job] == replica) & (jobs[1, job] == context)
        for page in range(2):
            gone[page] = gone[page] | (hit & (jobs[2, job] == page)).astype(jnp.int32)
    page_len = page_a.shape[1]
    half = page_a.shape[2] // 2
    lane = lax.broadcasted_iota(jnp.int32, (query.shape[1], 2 * page_len), 1)
    page = lane // page_len
    position = (page * shards + shard) * page_len + lane % page_len
    usable = (position < lengths[context]) & (jnp.where(page == 0, gone[0], gone[1]) == 0)
    key_rows = jnp.concatenate([page_a[0, :, :half], page_b[0, :, :half]], axis=0)
    value_rows = jnp.concatenate([page_a[0, :, half:], page_b[0, :, half:]], axis=0)
    result, logarithm = attend(query[0], key_rows, value_rows, usable)
    out[0] = result
    level[0] = jnp.broadcast_to(logarithm, result.shape)
    for copy in copies:
        copy.wait()


def kept(jobs, table, lengths, query, pool, after, shards):
    slots, heads, size = query.shape
    page = (1,) + pool.shape[1:]
    return pl.pallas_call(
        functools.partial(kept_kernel, shards=shards),
        grid_spec=pltpu.PrefetchScalarGridSpec(
            num_scalar_prefetch=3,
            grid=(slots,),
            in_specs=[
                pl.BlockSpec((1, heads, size), lambda c, jobs, table, lengths: (c, 0, 0)),
                pl.BlockSpec(page, lambda c, jobs, table, lengths: (table[0, c], 0, 0)),
                pl.BlockSpec(page, lambda c, jobs, table, lengths: (table[1, c], 0, 0)),
                whole(pl.ANY),
            ],
            out_specs=[
                pl.BlockSpec((1, heads, size), lambda c, jobs, table, lengths: (c, 0, 0)),
                pl.BlockSpec((1, heads, size), lambda c, jobs, table, lengths: (c, 0, 0)),
                whole(pl.ANY),
            ],
            scratch_shapes=[pltpu.SemaphoreType.DMA((2,))],
        ),
        out_shape=[
            jax.ShapeDtypeStruct((slots, heads, size), F32),
            jax.ShapeDtypeStruct((slots, heads, size), F32),
            jax.ShapeDtypeStruct(pool.shape, pool.dtype),
        ],
        compiler_params=pltpu.CompilerParams(vmem_limit_bytes=LIMIT),
        cost_estimate=SMALL,
        name="kept",
    )(jobs, table, lengths, query, pool, pool, after)


def route(jobs, finished, outs):
    replica = lax.axis_index("rep")
    page_len = finished.shape[0] // SENDS
    for step, out in enumerate(outs):
        chosen = jobs[0, replica * SENDS] == jnp.bitwise_xor(replica, step)

        @pl.when(chosen)
        def _():
            out[...] = finished[:page_len]

        @pl.when(jnp.logical_not(chosen))
        def _():
            out[...] = finished[page_len:]


def finish_keys_kernel(jobs, own, near, far, across, frequency, *rest, stripe):
    outs, scale, finished = rest[:4], rest[4], rest[5]
    replica = lax.axis_index("rep")
    shard = lax.axis_index("shard")
    rows = own.shape[0]
    page_len = rows // SENDS
    width = own.shape[1] - LANES

    def added(columns):
        parts = [ref[:, columns].astype(F32) for ref in (own, near, far, across)]
        return (parts[0] + parts[1]) + (parts[2] + parts[3])

    squares = jnp.sum(added(slice(width, width + LANES)), axis=1, keepdims=True)
    inverse = jnp.broadcast_to(lax.rsqrt(squares / D + EPS), (rows, LANES))
    scale[...] = inverse
    row = lax.broadcasted_iota(jnp.int32, (rows, LANES), 0)
    lane = lax.broadcasted_iota(jnp.int32, (rows, LANES), 1)
    index = jnp.where(row < page_len, jobs[2, replica * SENDS], jobs[2, replica * SENDS + 1])
    position = index * stripe + shard * page_len + row % page_len
    angle = position.astype(F32) * frequency[...]
    cosine = jnp.cos(angle) * inverse
    sine_part = jnp.where(lane < LANES // 2, -jnp.sin(angle), jnp.sin(angle)) * inverse
    for head in range(width // LANES):
        columns = slice(head * LANES, (head + 1) * LANES)
        value = added(columns)
        turned = value * cosine + pltpu.roll(value, LANES // 2, 1) * sine_part
        finished[:, columns] = turned.astype(BF16)
    route(jobs, finished, outs)


def finish_values_kernel(jobs, own, near, far, across, scale, *rest):
    outs, finished = rest[:4], rest[4]
    for head in range(own.shape[1] // LANES):
        columns = slice(head * LANES, (head + 1) * LANES)
        parts = [ref[:, columns].astype(F32) for ref in (own, near, far, across)]
        total = (parts[0] + parts[1]) + (parts[2] + parts[3])
        finished[:, columns] = (total * scale[...]).astype(BF16)
    route(jobs, finished, outs)


def finish_part(jobs, parts, extra, stripe, keys):
    rows = parts[0].shape[0]
    width = parts[0].shape[1] - (LANES if keys else 0)
    page = jax.ShapeDtypeStruct((rows // SENDS, width), BF16)
    shapes = [page] * 4
    if keys:
        shapes.append(jax.ShapeDtypeStruct((rows, LANES), F32))
        kernel = functools.partial(finish_keys_kernel, stripe=stripe)
    else:
        kernel = finish_values_kernel
    return pl.pallas_call(
        kernel,
        in_specs=[whole(SMEM)] + [whole()] * 5,
        out_specs=[whole()] * len(shapes),
        out_shape=shapes,
        scratch_shapes=[pltpu.VMEM((rows, width), BF16)],
        cost_estimate=SMALL,
        compiler_params=pltpu.CompilerParams(vmem_limit_bytes=LIMIT),
        name="finish_keys" if keys else "finish_values",
    )(jobs, *parts, extra)


def job_from(jobs, step):
    replica = lax.axis_index("rep")
    first = jnp.bitwise_xor(replica, step) * SENDS
    hit_first = jobs[0, first] == replica
    hit = hit_first | (jobs[0, first + 1] == replica)
    row = jnp.where(hit_first, first, first + 1)
    return hit, jobs[1, row], jobs[2, row]


def merge_kernel(jobs, lengths, query, kept_out, kept_level, *rest, shards):
    key_pages, value_pages = rest[:4], rest[4:8]
    outs, total, level = rest[8:12], rest[12], rest[13]
    shard = lax.axis_index("shard")
    heads = query.shape[1]
    page_len = key_pages[0].shape[0]
    total[...] = kept_out[...]
    level[...] = kept_level[...]
    for step in range(4):
        hit, context, page = job_from(jobs, step)

        @pl.when(hit)
        def _():
            lane = lax.broadcasted_iota(jnp.int32, (heads, page_len), 1)
            usable = (page * shards + shard) * page_len + lane < lengths[context]
            fresh, fresh_level = attend(query[context], key_pages[step][...], value_pages[step][...], usable)
            old_level = level[context]
            top = jnp.maximum(old_level, fresh_level)
            old_share = jnp.exp(old_level - top)
            fresh_share = jnp.exp(fresh_level - top)
            both = old_share + fresh_share
            total[context] = (total[context] * old_share + fresh * fresh_share) / both
            level[context] = top + jnp.log(both)

    slots = query.shape[0]
    here = heads // shards
    rows = slots * here
    place = lax.broadcasted_iota(jnp.int32, (16, LANES), 0)
    for step in range(4):
        start = pl.multiple_of(jnp.bitwise_xor(shard, step) * here, here)
        outs[step][:rows] = total[:, pl.ds(start, here), :].reshape(rows, LANES).astype(BF16)
        lines = level[:, pl.ds(start, here), :].reshape(rows, LANES).T[:16]
        high = lines.astype(BF16).astype(F32)
        middle = (lines - high).astype(BF16).astype(F32)
        low = lines - high - middle
        outs[step][rows:] = jnp.where(place == 0, high, jnp.where(place == 1, middle, jnp.where(place == 2, low, 0.0))).astype(BF16)


def merge(jobs, lengths, query, kept_out, kept_level, key_pages, value_pages, shards):
    slots, heads, size = query.shape
    rows = slots * heads // shards
    return pl.pallas_call(
        functools.partial(merge_kernel, shards=shards),
        in_specs=[whole(SMEM)] * 2 + [whole()] * 11,
        out_specs=[whole()] * 4,
        out_shape=[jax.ShapeDtypeStruct((rows + 16, size), BF16)] * 4,
        scratch_shapes=[pltpu.VMEM((slots, heads, size), F32)] * 2,
        cost_estimate=SMALL,
        compiler_params=pltpu.CompilerParams(vmem_limit_bytes=LIMIT),
        name="merge",
    )(jobs, lengths, query, kept_out, kept_level, *key_pages, *value_pages)


def place_kernel(jobs, table, pool, *rest):
    key_pages, value_pages, out, pages, sem = rest[:4], rest[4:8], rest[8], rest[9], rest[10]
    half = key_pages[0].shape[1]
    for wait in (False, True):
        for step in range(4):
            hit, context, page = job_from(jobs, step)

            @pl.when(hit)
            def _():
                slot = table[page, context]
                copy = pltpu.make_async_copy(pages.at[step], out.at[slot], sem.at[step])
                if wait:
                    copy.wait()
                else:
                    pages[step, :, :half] = key_pages[step][...]
                    pages[step, :, half:] = value_pages[step][...]
                    copy.start()


def place_pages(jobs, table, pool, key_pages, value_pages):
    return pl.pallas_call(
        place_kernel,
        in_specs=[whole(SMEM)] * 2 + [whole(pl.ANY)] + [whole()] * 8,
        out_specs=whole(pl.ANY),
        out_shape=jax.ShapeDtypeStruct(pool.shape, pool.dtype),
        scratch_shapes=[pltpu.VMEM((4,) + pool.shape[1:], pool.dtype), pltpu.SemaphoreType.DMA((4,))],
        input_output_aliases={2: 0},
        cost_estimate=SMALL,
        compiler_params=pltpu.CompilerParams(vmem_limit_bytes=LIMIT),
        name="place_pages",
    )(jobs, table, pool, *key_pages, *value_pages)


def combine_kernel(*refs):
    parts, out, spread = refs[:4], refs[4], refs[5]
    slots, here, size = spread.shape
    rows = slots * here
    levels = []
    for ref in parts:
        tail = ref[rows:].astype(F32)
        line = jnp.sum(tail, axis=0, keepdims=True)
        levels.append(jnp.broadcast_to(line, (rows, rows)).T)
    top = functools.reduce(jnp.maximum, levels)
    total = jnp.zeros((rows, size), F32)
    both = jnp.zeros((rows, size), F32)
    for ref, level in zip(parts, levels):
        share = jnp.exp(level - top)
        total = total + ref[:rows].astype(F32) * share
        both = both + share
    spread[...] = (total / both).reshape(slots, here, size)
    for head in range(here):
        out[:, head * size : (head + 1) * size] = spread[:, head, :].astype(BF16)


def combine(parts, slots, here):
    size = parts[0].shape[1]
    return pl.pallas_call(
        combine_kernel,
        in_specs=[whole()] * 4,
        out_specs=whole(),
        out_shape=jax.ShapeDtypeStruct((slots, here * size), BF16),
        scratch_shapes=[pltpu.VMEM((slots, here, size), F32)],
        cost_estimate=SMALL,
        compiler_params=pltpu.CompilerParams(vmem_limit_bytes=LIMIT),
        name="combine",
    )(*parts)


def added(left, right):
    return (left.astype(F32) + right.astype(F32)).astype(BF16)


def on_device(
    hidden, norm_gain, kv_weight, restore_jobs, page_table, context_lengths, queries, kv_pool
):
    shards = lax.axis_size("shard")
    replicas = lax.axis_size("rep")
    stripe = hidden.shape[0] // SENDS
    page_len = stripe // shards
    kv_weight = pltpu.with_memory_space_constraint(kv_weight, pltpu.HBM)
    kv_pool = pltpu.with_memory_space_constraint(kv_pool, pltpu.HBM)
    jobs = restore_jobs.T
    table = page_table[:, :, 0].T
    slots = queries.shape[0]
    query = queries.reshape(slots, QH, HD)
    blocks = pltpu.with_memory_space_constraint(
        hidden.reshape(SENDS, shards, page_len, hidden.shape[1]), pltpu.HBM
    )
    gain = norm_gain.astype(F32)[None, :]

    def along(array, pairs):
        return lax.ppermute(array, "shard", pairs)

    key_1, key_2 = project(blocks, gain, kv_weight, [], True, (0,))
    key_in_1 = along(key_1, OUTWARD)
    key_in_2 = along(key_2, OUTWARD)
    kept_out, kept_level, new_pool = kept(
        jobs, table, context_lengths, query, kv_pool, key_1, shards
    )
    value_1, value_2 = project(blocks, gain, kv_weight, [kept_level, key_in_1], True, (1,))
    value_in_1 = along(value_1, OUTWARD)
    value_in_2 = along(value_2, OUTWARD)
    key_far = along(added(key_1, key_in_1), FAR)
    key_0, key_3, value_0, value_3 = project(blocks, gain, kv_weight, [value_1, key_in_2], False, (0, 1))
    key_near = along(key_3, NEIGHBOUR)
    value_near = along(value_3, NEIGHBOUR)
    key_across = along(added(key_2, key_in_2), ACROSS)
    value_far = along(added(value_1, value_in_1), FAR)
    value_across = along(added(value_2, value_in_2), ACROSS)
    frequency = THETA ** (-(jnp.arange(HD // 2, dtype=F32) * 2.0 / HD))
    frequency = jnp.concatenate([frequency, frequency])[None, :]
    *key_out, scale = finish_part(jobs, (key_0, key_near, key_far, key_across), frequency, stripe, True)

    def between(pages):
        return [pages[0]] + [
            lax.ppermute(pages[step], "rep", [(i, i ^ step) for i in range(replicas)])
            for step in range(1, replicas)
        ]

    key_pages = between(key_out)
    value_out = finish_part(jobs, (value_0, value_near, value_far, value_across), scale, stripe, False)
    value_pages = between(value_out)
    packed = merge(
        jobs, context_lengths, query, kept_out, kept_level, key_pages, value_pages, shards
    )
    parts = [packed[0]] + [
        along(packed[step], [(i, i ^ step) for i in range(shards)]) for step in range(1, shards)
    ]
    new_pool = place_pages(jobs, table, new_pool, key_pages, value_pages)
    return (new_pool, combine(parts, slots, QH // shards))


def solution(mesh):
    in_specs = (
        P(("outer", "rep"), "shard"),
        P("shard"),
        P("shard", None),
        P("outer", None),
        P(("outer", "rep"), None, "shard"),
        P(("outer", "rep")),
        P(("outer", "rep"), None),
        P(("outer", "rep", "shard"), None, None),
    )
    out_specs = (P(("outer", "rep", "shard"), None, None), P(("outer", "rep"), "shard"))
    fast = mesh.shape["shard"] == 4 and mesh.shape["rep"] == 4
    return jax.shard_map(
        on_device if fast else on_device_general, mesh=mesh, in_specs=in_specs, out_specs=out_specs, check_vma=False
    )
```

```python
import functools
import math

import jax
import jax.numpy as jnp
from jax import lax
from jax.experimental import pallas as pl
from jax.experimental.pallas import tpu as pltpu
from jax.sharding import PartitionSpec as P

D = 8192
QH = 64
KVH = 8
HD = 128
SENDS = 2


THETA = 500000.0
EPS = 1e-05
FLOOR_SCORE = -1e30


def rotate(key_rows, positions):
    half_dim = key_rows.shape[-1] // 2
    frequency = THETA ** (-(jnp.arange(half_dim, dtype=jnp.float32) * 2.0 / key_rows.shape[-1]))
    angles = positions.astype(jnp.float32)[:, None] * frequency[None, :]
    cosine = jnp.cos(angles)[:, None, :]
    sine_part = jnp.sin(angles)[:, None, :]
    first_half = key_rows[..., :half_dim]
    second = key_rows[..., half_dim:]
    return jnp.concatenate(
        [first_half * cosine - second * sine_part, second * cosine + first_half * sine_part],
        axis=-1,
    )


def finish(projected, inverse, positions):
    row_count = projected.shape[0]
    half_width = projected.shape[1] // 2
    scaled = projected * inverse[:, None]
    key_rows = rotate(scaled[:, :half_width].reshape(row_count, KVH, HD), positions).reshape(
        row_count, half_width
    )
    return jnp.concatenate([key_rows, scaled[:, half_width:]], axis=1).astype(jnp.bfloat16)


def spread_out(pieces, targets, replicas):
    outgoing = jnp.zeros((replicas,) + pieces.shape[1:], pieces.dtype)
    for send_index in range(SENDS):
        hit = (jnp.arange(replicas, dtype=jnp.int32) == targets[send_index])[:, None, None]
        outgoing = jnp.where(hit, pieces[send_index][None], outgoing)
    return outgoing


def on_device_general(
    hidden, norm_gain, kv_weight, restore_jobs, page_table, context_lengths, queries, kv_pool
):
    shards = lax.axis_size("shard")
    replicas = lax.axis_size("rep")
    my_replica = lax.axis_index("rep")
    my_shard = lax.axis_index("shard")
    stripe = hidden.shape[0] // SENDS
    page_len = stripe // shards
    features = hidden.shape[1]
    kv_width = kv_weight.shape[1]
    pool_pages = kv_pool.shape[0]
    destination = restore_jobs[:, 0]
    context = restore_jobs[:, 1]
    stripe_index = restore_jobs[:, 2]
    my_targets = lax.dynamic_slice_in_dim(destination, my_replica * SENDS, SENDS, 0)
    is_mine = destination == my_replica
    gain_wide = norm_gain.astype(jnp.float32)[None, :]
    page_rows = jnp.arange(page_len, dtype=jnp.int32)
    wide = hidden.astype(jnp.float32)
    squares = lax.psum(jnp.sum(wide * wide, axis=1), "shard")
    inverse = lax.rsqrt(squares / D + EPS)
    gained = (wide * gain_wide).astype(jnp.bfloat16)
    arranged = gained.reshape(SENDS, shards, page_len, features).transpose(1, 0, 2, 3)
    arranged = arranged.reshape(shards * SENDS * page_len, features)
    owned = lax.psum_scatter(
        jnp.dot(arranged, kv_weight, preferred_element_type=jnp.float32).astype(jnp.bfloat16),
        "shard",
        scatter_dimension=0,
        tiled=True,
    ).astype(jnp.float32)
    owned_inverse = lax.dynamic_slice_in_dim(
        inverse.reshape(SENDS, stripe), my_shard * page_len, page_len, 1
    )
    my_stripes = lax.dynamic_slice_in_dim(stripe_index, my_replica * SENDS, SENDS, 0)
    positions = my_stripes[:, None] * stripe + my_shard * page_len + page_rows[None, :]
    finished = finish(owned, owned_inverse.reshape(-1), positions.reshape(-1)).reshape(
        SENDS, page_len, kv_width
    )
    outgoing = spread_out(finished, my_targets, replicas)
    arrived = lax.all_to_all(outgoing, "rep", split_axis=0, concat_axis=0, tiled=True)
    mine_grid = is_mine.reshape(replicas, SENDS)
    has_page = jnp.any(mine_grid, axis=1)
    which = jnp.argmax(mine_grid.astype(jnp.int32), axis=1)
    job_index = jnp.arange(replicas, dtype=jnp.int32) * SENDS + which
    physical = jnp.where(
        has_page, page_table[context[job_index], stripe_index[job_index], 0], pool_pages
    )
    new_pool = kv_pool.at[physical].set(arrived, mode="drop")
    slots = queries.shape[0]
    pages_dev = page_table.shape[1]
    group = QH // KVH
    scale = 1.0 / math.sqrt(HD)
    cached = new_pool[page_table[:, :, 0]]
    key_rows = cached[..., : KVH * HD].reshape(slots, pages_dev * page_len, KVH, HD)
    value_rows = cached[..., KVH * HD :].reshape(slots, pages_dev * page_len, KVH, HD)
    query_rows = queries.reshape(slots, KVH, group, HD)
    scores = (
        jnp.einsum("cgmd,cpgd->cgmp", query_rows, key_rows, preferred_element_type=jnp.float32)
        * scale
    )
    position = (
        (jnp.arange(pages_dev, dtype=jnp.int32)[:, None] * shards + my_shard) * page_len
        + page_rows[None, :]
    ).reshape(-1)
    usable = (position[None, :] < context_lengths[:, None])[:, None, None, :]
    local_max = jnp.max(jnp.where(usable, scores, FLOOR_SCORE), axis=-1)
    weights = jnp.where(usable, jnp.exp(scores - local_max[..., None]), 0.0)
    denominator = jnp.sum(weights, axis=-1).reshape(slots, QH)
    numerator = jnp.einsum(
        "cgmp,cpgd->cgmd",
        weights.astype(jnp.bfloat16),
        value_rows,
        preferred_element_type=jnp.float32,
    )
    numerator = numerator.reshape(slots, QH, HD)
    local_max = local_max.reshape(slots, QH)
    heads_here = QH // shards
    row_max = lax.pmax(local_max, "shard")
    factor = jnp.exp(local_max - row_max)
    scaled_num = (numerator * factor[..., None]).reshape(slots, QH * HD)
    numerator, denominator = (
        lax.psum(scaled_num.astype(jnp.bfloat16), "shard").astype(jnp.float32),
        lax.psum((denominator * factor).astype(jnp.bfloat16), "shard").astype(jnp.float32),
    )
    numerator = lax.dynamic_slice_in_dim(numerator, my_shard * heads_here * HD, heads_here * HD, 1)
    denominator = lax.dynamic_slice_in_dim(denominator, my_shard * heads_here, heads_here, 1)
    numerator = numerator.reshape(slots, heads_here, HD)
    attention_out = numerator / denominator[..., None]
    return (new_pool, attention_out.reshape(slots, heads_here * HD).astype(jnp.bfloat16))


FIRST = [(0, 1), (3, 2), (1, 3), (2, 0)]
NEAR = [(0, 1), (1, 0), (2, 3), (3, 2)]
THIRD = [(0, 3), (3, 0), (1, 2), (2, 1)]
LANES = 128
BF16 = jnp.bfloat16
F32 = jnp.float32
SMEM = pltpu.SMEM
VMEM = pltpu.VMEM
SMALL = pl.CostEstimate(flops=1, bytes_accessed=1, transcendentals=0)
LIMIT = 24 * 1024 * 1024


def whole(space=VMEM):
    return pl.BlockSpec(memory_space=space)


def split_sum(total, offset):
    high = total.astype(BF16).astype(F32)
    low = total - high
    lane = lax.broadcasted_iota(jnp.int32, (total.shape[0], LANES), 1)
    return jnp.where(lane == offset, high, jnp.where(lane == offset + 1, low, 0.0)).astype(BF16)


def row_copies(hidden, blocks, rows_in, sem):
    stripes, _, page_len, _ = hidden.shape
    return [
        pltpu.make_async_copy(
            hidden.at[stripe, block],
            rows_in.at[pl.ds((place * stripes + stripe) * page_len, page_len)],
            sem.at[place * stripes + stripe],
        )
        for place, block in enumerate(blocks)
        for stripe in range(stripes)
    ]


def weight_copies(weight, tiles, sem):
    half = weight.shape[1] // 2
    return [
        pltpu.make_async_copy(weight.at[:, pl.ds(side * half, half)], tiles.at[side], sem.at[side])
        for side in range(2)
    ]


def scale_rows(rows_in, gained, gain_in, span):
    wide_gain = gain_in[...].astype(F32).reshape(1, gain_in.shape[0])
    gained[span] = (rows_in[span].astype(F32) * wide_gain).astype(BF16)


def put_squares(rows_in, span, out, columns, offset):
    squares = jnp.zeros((out.shape[0], LANES), F32)
    for lane in range(rows_in.shape[1] // LANES):
        part = rows_in[span, lane * LANES : (lane + 1) * LANES].astype(F32)
        squares = squares + part * part
    total = jnp.sum(squares, axis=1, keepdims=True)
    out[:, columns] = split_sum(total, offset)


def is_inner(shard):
    return (shard == 1) | (shard == 2)


def far_blocks(shard):
    lower = shard < 2
    return jnp.where(lower, 2, 1), jnp.where(lower, 3, 0)


def first_kernel(hidden, gain, weight, out, rows_in, gained, gain_in, tiles, row_sem, gain_sem, tile_sem):
    shard = lax.axis_index("shard")
    half = weight.shape[1] // 2
    inner_block, outer_block = far_blocks(shard)
    rows_here = row_copies(hidden, [jnp.where(is_inner(shard), outer_block, inner_block)], rows_in, row_sem)
    tiles_here = weight_copies(weight, tiles, tile_sem)
    gain_copy = pltpu.make_async_copy(gain, gain_in, gain_sem)
    gain_copy.start()
    for copy in rows_here + tiles_here:
        copy.start()
    gain_copy.wait()
    for copy in rows_here:
        copy.wait()
    scale_rows(rows_in, gained, gain_in, slice(None))
    put_squares(rows_in, slice(None), out, slice(half, half + LANES), 0)
    for side, columns in enumerate((slice(0, half), slice(half + LANES, 2 * half + LANES))):
        tiles_here[side].wait()
        out[:, columns] = jnp.dot(gained[...], tiles[side], preferred_element_type=F32).astype(BF16)


def project_first(hidden, gain, weight):
    stripes, blocks, page_len, features = hidden.shape
    half = weight.shape[1] // 2
    rows = stripes * page_len
    return pl.pallas_call(
        first_kernel,
        in_specs=[whole(pl.ANY)] * 3,
        out_specs=whole(),
        out_shape=jax.ShapeDtypeStruct((rows, 2 * half + LANES), BF16),
        scratch_shapes=[
            pltpu.VMEM((rows, features), BF16),
            pltpu.VMEM((rows, features), BF16),
            pltpu.VMEM((features,), BF16),
            pltpu.VMEM((2, features, half), BF16),
            pltpu.SemaphoreType.DMA((stripes,)),
            pltpu.SemaphoreType.DMA,
            pltpu.SemaphoreType.DMA((2,)),
        ],
        compiler_params=pltpu.CompilerParams(vmem_limit_bytes=LIMIT),
        cost_estimate=SMALL,
        name="project_first",
    )(hidden, gain, weight)


def head_spread(query, width):
    heads = query.shape[0]
    group = heads // (width // LANES)
    head = lax.broadcasted_iota(jnp.int32, (heads, LANES), 0)
    pieces = [jnp.where(head // group == g, query, jnp.zeros_like(query)) for g in range(width // LANES)]
    return jnp.concatenate(pieces, axis=1)


def head_pick(products):
    heads, width = products.shape
    group = heads // (width // LANES)
    head = lax.broadcasted_iota(jnp.int32, (heads, LANES), 0)
    picked = products[:, :LANES]
    for g in range(1, width // LANES):
        picked = jnp.where(head // group == g, products[:, g * LANES : (g + 1) * LANES], picked)
    return picked


def score(query, key_rows):
    spread = head_spread(query, key_rows.shape[1])
    scores = lax.dot_general(spread, key_rows, (((1,), (1,)), ((), ())), preferred_element_type=F32)
    return scores * (1.0 / math.sqrt(LANES))


def attend(query, key_rows, value_rows, usable):
    scores = jnp.where(usable, score(query, key_rows), FLOOR_SCORE)
    largest = jnp.max(scores, axis=1, keepdims=True)
    weights = jnp.where(usable, jnp.exp(scores - largest), 0.0)
    total = jnp.sum(weights, axis=1, keepdims=True)
    picked = head_pick(jnp.dot(weights.astype(BF16), value_rows, preferred_element_type=F32))
    some = total > 0.0
    safe = jnp.where(some, total, 1.0)
    return picked / safe, jnp.where(some, largest + jnp.log(safe), FLOOR_SCORE)


def split_lines(lines, first):
    high = lines.astype(BF16).astype(F32)
    middle_part = (lines - high).astype(BF16).astype(F32)
    low = lines - high - middle_part
    place = lax.broadcasted_iota(jnp.int32, lines.shape, 0) - first
    return jnp.where(place == 0, high, jnp.where(place == 1, middle_part, jnp.where(place == 2, low, 0.0)))


def join_lines(tail, first, rows):
    line = jnp.sum(tail[first : first + 3].astype(F32), axis=0, keepdims=True)
    return jnp.broadcast_to(line, (LANES, LANES)).T[:rows]


def middle_kernel(hidden, gain, weight, *rest, after):
    keys, values = rest[after : after + 3], rest[after + 3 : after + 6]
    rows_in, gained, gain_in, tiles, row_sem, gain_sem, tile_sem = rest[after + 6 :]
    shard = lax.axis_index("shard")
    half = weight.shape[1] // 2
    rows = values[0].shape[0]
    inner_block, outer_block = far_blocks(shard)
    blocks = [shard, jnp.bitwise_xor(shard, 1), jnp.where(is_inner(shard), inner_block, outer_block)]
    rows_here = row_copies(hidden, blocks, rows_in, row_sem)
    tiles_here = weight_copies(weight, tiles, tile_sem)
    gain_copy = pltpu.make_async_copy(gain, gain_in, gain_sem)
    gain_copy.start()
    for copy in rows_here + tiles_here:
        copy.start()
    gain_copy.wait()
    for copy in rows_here:
        copy.wait()
    scale_rows(rows_in, gained, gain_in, slice(None))
    for place, ref in enumerate(keys):
        span = slice(place * rows, (place + 1) * rows)
        put_squares(rows_in, span, ref, slice(half, half + LANES), 2 if place == 2 else 0)
    for side, refs in enumerate((keys, values)):
        tiles_here[side].wait()
        product = jnp.dot(gained[...], tiles[side], preferred_element_type=F32).astype(BF16)
        for place, ref in enumerate(refs):
            ref[:, :half] = product[place * rows : (place + 1) * rows]


def middle(hidden, gain, weight, after):
    stripes, blocks, page_len, features = hidden.shape
    half = weight.shape[1] // 2
    rows = stripes * page_len
    keys = jax.ShapeDtypeStruct((rows, half + LANES), BF16)
    values = jax.ShapeDtypeStruct((rows, half), BF16)
    return pl.pallas_call(
        functools.partial(middle_kernel, after=len(after)),
        in_specs=[whole(pl.ANY)] * (3 + len(after)),
        out_specs=[whole()] * 6,
        out_shape=[keys] * 3 + [values] * 3,
        scratch_shapes=[
            pltpu.VMEM((3 * rows, features), BF16),
            pltpu.VMEM((3 * rows, features), BF16),
            pltpu.VMEM((features,), BF16),
            pltpu.VMEM((2, features, half), BF16),
            pltpu.SemaphoreType.DMA((3 * stripes,)),
            pltpu.SemaphoreType.DMA,
            pltpu.SemaphoreType.DMA((2,)),
        ],
        compiler_params=pltpu.CompilerParams(vmem_limit_bytes=LIMIT),
        cost_estimate=SMALL,
        name="middle",
    )(hidden, gain, weight, *after)


def ask_kernel(jobs, query, after, *outs):
    for step, out in enumerate(outs):
        out[...] = query[job_from(jobs, step)[1]]


def ask(jobs, query, after):
    return pl.pallas_call(
        ask_kernel,
        in_specs=[whole(SMEM), whole(), whole(pl.ANY)],
        out_specs=[whole()] * 4,
        out_shape=[jax.ShapeDtypeStruct(query.shape[1:], BF16)] * 4,
        compiler_params=pltpu.CompilerParams(vmem_limit_bytes=LIMIT),
        cost_estimate=SMALL,
        name="ask",
    )(jobs, query, after)


def kept_kernel(jobs, table, lengths, query, pool, after, *rest, shards):
    outs, new_pool, pages, total, level, in_sem, out_sem = rest[:4], *rest[4:]
    slots, heads, _ = query.shape
    here = heads // shards
    rows = slots * here
    replica = lax.axis_index("rep")
    shard = lax.axis_index("shard")
    page_len = pool.shape[1]
    half = pool.shape[2] // 2

    def copy_in(context, page):
        place = context * 2 + page
        return pltpu.make_async_copy(pool.at[table[page, context]], pages.at[place], in_sem.at[place])

    def copy_out(context, page):
        place = context * 2 + page
        return pltpu.make_async_copy(pages.at[place], new_pool.at[table[page, context]], out_sem.at[place])

    @pl.loop(0, slots)
    def _(context):
        for page in range(2):
            copy_in(context, page).start()

    @pl.loop(0, slots)
    def _(context):
        for page in range(2):
            copy_in(context, page).wait()
            copy_out(context, page).start()
        gone = [jnp.int32(0), jnp.int32(0)]
        for job in range(jobs.shape[1]):
            hit = (jobs[0, job] == replica) & (jobs[1, job] == context)
            for page in range(2):
                gone[page] = gone[page] | (hit & (jobs[2, job] == page)).astype(jnp.int32)
        lane = lax.broadcasted_iota(jnp.int32, (heads, 2 * page_len), 1)
        page = lane // page_len
        position = (page * shards + shard) * page_len + lane % page_len
        usable = (position < lengths[context]) & (jnp.where(page == 0, gone[0], gone[1]) == 0)
        both = pages[pl.ds(context * 2, 2)].reshape(2 * page_len, 2 * half)
        result, logarithm = attend(query[context], both[:, :half], both[:, half:], usable)
        total[context] = result
        level[context] = jnp.broadcast_to(logarithm, result.shape)

    for step, out in enumerate(outs):
        start = pl.multiple_of(jnp.bitwise_xor(shard, step) * here, here)
        out[:rows] = total[:, pl.ds(start, here), :].reshape(rows, LANES).astype(BF16)
        lines = level[:, pl.ds(start, here), :].reshape(rows, LANES).T[:16]
        out[rows:] = split_lines(lines, 0).astype(BF16)

    @pl.loop(0, slots)
    def _(context):
        for page in range(2):
            copy_out(context, page).wait()


def kept(jobs, table, lengths, query, pool, after, shards):
    slots, heads, size = query.shape
    return pl.pallas_call(
        functools.partial(kept_kernel, shards=shards),
        in_specs=[whole(SMEM)] * 3 + [whole()] + [whole(pl.ANY)] * 2,
        out_specs=[whole()] * 4 + [whole(pl.ANY)],
        out_shape=[jax.ShapeDtypeStruct((slots * heads // shards + 16, size), BF16)] * 4
        + [jax.ShapeDtypeStruct(pool.shape, pool.dtype)],
        scratch_shapes=[
            pltpu.VMEM((slots * 2,) + pool.shape[1:], pool.dtype),
            pltpu.VMEM(query.shape, F32),
            pltpu.VMEM(query.shape, F32),
            pltpu.SemaphoreType.DMA((slots * 2,)),
            pltpu.SemaphoreType.DMA((slots * 2,)),
        ],
        compiler_params=pltpu.CompilerParams(vmem_limit_bytes=LIMIT),
        cost_estimate=SMALL,
        name="kept",
    )(jobs, table, lengths, query, pool, after)


def carry_kernel(mine, first, after, out):
    start = first.shape[1] - mine.shape[1]
    inner = is_inner(lax.axis_index("shard"))

    @pl.when(inner)
    def _():
        out[...] = (mine[...].astype(F32) + first[:, start:].astype(F32)).astype(BF16)

    @pl.when(jnp.logical_not(inner))
    def _():
        out[...] = mine[...]


def carry(mine, first, after):
    return pl.pallas_call(
        carry_kernel,
        in_specs=[whole(), whole(), whole(pl.ANY)],
        out_specs=whole(),
        out_shape=jax.ShapeDtypeStruct(mine.shape, BF16),
        compiler_params=pltpu.CompilerParams(vmem_limit_bytes=LIMIT),
        cost_estimate=SMALL,
        name="carry",
    )(mine, first, after)


def route(jobs, finished, outs):
    replica = lax.axis_index("rep")
    page_len = finished.shape[0] // SENDS
    for step, out in enumerate(outs):
        chosen = jobs[0, replica * SENDS] == jnp.bitwise_xor(replica, step)

        @pl.when(chosen)
        def _():
            out[...] = finished[:page_len]

        @pl.when(jnp.logical_not(chosen))
        def _():
            out[...] = finished[page_len:]


def add_parts(own, near, first, third, columns, first_columns):
    direct = jnp.where(is_inner(lax.axis_index("shard")), 0.0, first[:, first_columns].astype(F32))
    return (own[:, columns].astype(F32) + near[:, columns].astype(F32)) + (third[:, columns].astype(F32) + direct)


def finish_keys_kernel(jobs, own, near, first, third, frequency, *rest, stripe):
    asked, outs = rest[:4], rest[4:8]
    scale, weights_out, share, level, finished = rest[8:]
    replica = lax.axis_index("rep")
    shard = lax.axis_index("shard")
    rows = own.shape[0]
    page_len = rows // SENDS
    width = own.shape[1] - LANES

    def added(columns):
        return add_parts(own, near, first, third, columns, columns)

    squares = jnp.sum(added(slice(width, width + LANES)), axis=1, keepdims=True)
    inverse = jnp.broadcast_to(lax.rsqrt(squares / D + EPS), (rows, LANES))
    scale[...] = inverse
    row = lax.broadcasted_iota(jnp.int32, (rows, LANES), 0)
    lane = lax.broadcasted_iota(jnp.int32, (rows, LANES), 1)
    index = jnp.where(row < page_len, jobs[2, replica * SENDS], jobs[2, replica * SENDS + 1])
    position = index * stripe + shard * page_len + row % page_len
    angle = position.astype(F32) * frequency[...]
    cosine = jnp.cos(angle) * inverse
    sine_part = jnp.where(lane < LANES // 2, -jnp.sin(angle), jnp.sin(angle)) * inverse
    for head in range(width // LANES):
        columns = slice(head * LANES, (head + 1) * LANES)
        value = added(columns)
        turned = value * cosine + pltpu.roll(value, LANES // 2, 1) * sine_part
        finished[:, columns] = turned.astype(BF16)
    route(jobs, finished, outs)
    for send in range(SENDS):
        step = jnp.bitwise_xor(jobs[0, replica * SENDS + send], replica)
        query = asked[0][...]
        for other in range(1, 4):
            query = jnp.where(step == other, asked[other][...], query)
        scores = score(query, finished[send * page_len : (send + 1) * page_len])
        largest = jnp.max(scores, axis=1, keepdims=True)
        weights = jnp.exp(scores - largest)
        total = jnp.sum(weights, axis=1, keepdims=True)
        weights_out[send] = weights.astype(BF16)
        share[send] = jnp.broadcast_to(1.0 / total, share.shape[1:])
        level[send] = jnp.broadcast_to(largest + jnp.log(total), level.shape[1:])


def finish_values_kernel(jobs, own, near, first, third, scale, weights, share, level, *rest, shards):
    kept_parts, outs, packed, finished, result = rest[:4], rest[4:8], rest[8:12], rest[12], rest[13]
    shard = lax.axis_index("shard")
    for head in range(own.shape[1] // LANES):
        columns = slice(head * LANES, (head + 1) * LANES)
        start = own.shape[1] + LANES + head * LANES
        total = add_parts(own, near, first, third, columns, slice(start, start + LANES))
        finished[:, columns] = (total * scale[...]).astype(BF16)
    route(jobs, finished, outs)
    page_len = own.shape[0] // SENDS
    for send in range(SENDS):
        products = jnp.dot(
            weights[send], finished[send * page_len : (send + 1) * page_len], preferred_element_type=F32
        )
        result[send] = head_pick(products) * share[send]
    here = level.shape[1] // shards
    count = SENDS * here
    rows = kept_parts[0].shape[0] - 16
    for step in range(4):
        start = pl.multiple_of(jnp.bitwise_xor(shard, step) * here, here)
        packed[step][:rows] = kept_parts[step][:rows]
        packed[step][rows : rows + count] = result[:, pl.ds(start, here), :].reshape(count, LANES).astype(BF16)
        mine = level[:, pl.ds(start, here), :].reshape(count, LANES)
        lines = jnp.concatenate([mine] + [jnp.zeros((LANES - count, LANES), F32)], axis=0).T[:16]
        tail = kept_parts[step][rows:].astype(F32) + split_lines(lines, 3)
        packed[step][rows + count :] = tail.astype(BF16)


def finish_keys(jobs, parts, frequency, asked, stripe):
    rows = parts[0].shape[0]
    width = parts[0].shape[1] - LANES
    heads = asked[0].shape[0]
    page_len = rows // SENDS
    return pl.pallas_call(
        functools.partial(finish_keys_kernel, stripe=stripe),
        in_specs=[whole(SMEM)] + [whole()] * 9,
        out_specs=[whole()] * 8,
        out_shape=[jax.ShapeDtypeStruct((page_len, width), BF16)] * 4
        + [
            jax.ShapeDtypeStruct((rows, LANES), F32),
            jax.ShapeDtypeStruct((SENDS, heads, page_len), BF16),
            jax.ShapeDtypeStruct((SENDS, heads, LANES), F32),
            jax.ShapeDtypeStruct((SENDS, heads, LANES), F32),
        ],
        scratch_shapes=[pltpu.VMEM((rows, width), BF16)],
        compiler_params=pltpu.CompilerParams(vmem_limit_bytes=LIMIT),
        cost_estimate=SMALL,
        name="finish_keys",
    )(jobs, *parts, frequency, *asked)


def finish_values(jobs, parts, scale, weights, share, level, kept_parts, shards):
    rows, width = parts[0].shape
    heads = level.shape[1]
    page_len = rows // SENDS
    packed = kept_parts[0].shape[0] + SENDS * heads // shards
    return pl.pallas_call(
        functools.partial(finish_values_kernel, shards=shards),
        in_specs=[whole(SMEM)] + [whole()] * 12,
        out_specs=[whole()] * 8,
        out_shape=[jax.ShapeDtypeStruct((page_len, width), BF16)] * 4
        + [jax.ShapeDtypeStruct((packed, LANES), BF16)] * 4,
        scratch_shapes=[pltpu.VMEM((rows, width), BF16), pltpu.VMEM((SENDS, heads, LANES), F32)],
        compiler_params=pltpu.CompilerParams(vmem_limit_bytes=LIMIT),
        cost_estimate=SMALL,
        name="finish_values",
    )(jobs, *parts, scale, weights, share, level, *kept_parts)


def job_from(jobs, step):
    replica = lax.axis_index("rep")
    first = jnp.bitwise_xor(replica, step) * SENDS
    hit_first = jobs[0, first] == replica
    hit = hit_first | (jobs[0, first + 1] == replica)
    row = jnp.where(hit_first, first, first + 1)
    return hit, jobs[1, row], jobs[2, row]


def place_kernel(jobs, table, pool, *rest):
    key_pages, value_pages, out, pages, sem = rest[:4], rest[4:8], rest[8], rest[9], rest[10]
    half = key_pages[0].shape[1]
    for wait in (False, True):
        for step in range(4):
            hit, context, page = job_from(jobs, step)

            @pl.when(hit)
            def _():
                slot = table[page, context]
                copy = pltpu.make_async_copy(pages.at[step], out.at[slot], sem.at[step])
                if wait:
                    copy.wait()
                else:
                    pages[step, :, :half] = key_pages[step][...]
                    pages[step, :, half:] = value_pages[step][...]
                    copy.start()


def place_pages(jobs, table, pool, key_pages, value_pages):
    return pl.pallas_call(
        place_kernel,
        in_specs=[whole(SMEM)] * 2 + [whole(pl.ANY)] + [whole()] * 8,
        out_specs=whole(pl.ANY),
        out_shape=jax.ShapeDtypeStruct(pool.shape, pool.dtype),
        scratch_shapes=[pltpu.VMEM((4,) + pool.shape[1:], pool.dtype), pltpu.SemaphoreType.DMA((4,))],
        input_output_aliases={2: 0},
        compiler_params=pltpu.CompilerParams(vmem_limit_bytes=LIMIT),
        cost_estimate=SMALL,
        name="place_pages",
    )(jobs, table, pool, *key_pages, *value_pages)


def blend(parts, levels):
    top = functools.reduce(jnp.maximum, levels)
    shares = [jnp.exp(level - top) for level in levels]
    both = functools.reduce(jnp.add, shares)
    total = functools.reduce(jnp.add, [part * share for part, share in zip(parts, shares)])
    return total / both, top + jnp.log(both)


def gather_kernel(jobs, *refs, rows, count):
    parts, after, kept_out, kept_level, outs = refs[:4], refs[4], refs[5], refs[6], refs[7:]
    tails = [ref[rows + count :] for ref in parts]
    mixed, level = blend(
        [ref[:rows].astype(F32) for ref in parts], [join_lines(tail, 0, rows) for tail in tails]
    )
    kept_out[...] = mixed
    kept_level[...] = level
    mixed, level = blend(
        [ref[rows : rows + count].astype(F32) for ref in parts], [join_lines(tail, 3, count) for tail in tails]
    )
    here = count // SENDS
    replica = lax.axis_index("rep")
    lines = [
        jnp.concatenate([level[send * here : (send + 1) * here], jnp.zeros((LANES - here, LANES), F32)], axis=0).T[:16]
        for send in range(SENDS)
    ]
    for step, out in enumerate(outs):
        chosen = jobs[0, replica * SENDS] == jnp.bitwise_xor(replica, step)
        out[:here] = jnp.where(chosen, mixed[:here], mixed[here:]).astype(BF16)
        out[here:] = split_lines(jnp.where(chosen, lines[0], lines[1]), 0).astype(BF16)


def gather_parts(jobs, parts, after, rows, count):
    here = count // SENDS
    return pl.pallas_call(
        functools.partial(gather_kernel, rows=rows, count=count),
        in_specs=[whole(SMEM)] + [whole()] * 4 + [whole(pl.ANY)],
        out_specs=[whole()] * 6,
        out_shape=[jax.ShapeDtypeStruct((rows, LANES), F32)] * 2
        + [jax.ShapeDtypeStruct((here + 16, LANES), BF16)] * 4,
        compiler_params=pltpu.CompilerParams(vmem_limit_bytes=LIMIT),
        cost_estimate=SMALL,
        name="gather_parts",
    )(jobs, *parts, after)


def combine_kernel(jobs, kept_out, kept_level, *refs):
    parts, out, mixed = refs[:4], refs[4], refs[5]
    slots, here, size = mixed.shape
    mixed[...] = kept_out[...].reshape(mixed.shape)
    for step, ref in enumerate(parts):
        hit, context, _ = job_from(jobs, step)

        @pl.when(hit)
        def _():
            fresh_level = join_lines(ref[here:], 0, here)
            old_level = kept_level[pl.ds(pl.multiple_of(context * here, here), here)]
            blended, _ = blend([mixed[context], ref[:here].astype(F32)], [old_level, fresh_level])
            mixed[context] = blended

    for head in range(here):
        out[:, head * size : (head + 1) * size] = mixed[:, head, :].astype(BF16)


def combine(jobs, kept_out, kept_level, parts, slots):
    here = kept_out.shape[0] // slots
    return pl.pallas_call(
        combine_kernel,
        in_specs=[whole(SMEM)] + [whole()] * 6,
        out_specs=whole(),
        out_shape=jax.ShapeDtypeStruct((slots, here * LANES), BF16),
        scratch_shapes=[pltpu.VMEM((slots, here, LANES), F32)],
        compiler_params=pltpu.CompilerParams(vmem_limit_bytes=LIMIT),
        cost_estimate=SMALL,
        name="combine",
    )(jobs, kept_out, kept_level, *parts)


def on_device(
    hidden, norm_gain, kv_weight, restore_jobs, page_table, context_lengths, queries, kv_pool
):
    shards = lax.axis_size("shard")
    replicas = lax.axis_size("rep")
    stripe = hidden.shape[0] // SENDS
    page_len = stripe // shards
    kv_weight = pltpu.with_memory_space_constraint(kv_weight, pltpu.HBM)
    kv_pool = pltpu.with_memory_space_constraint(kv_pool, pltpu.HBM)
    gain = pltpu.with_memory_space_constraint(norm_gain, pltpu.HBM)
    blocks = pltpu.with_memory_space_constraint(
        hidden.reshape(SENDS, shards, page_len, hidden.shape[1]), pltpu.HBM
    )
    jobs = restore_jobs.T
    table = page_table[:, :, 0].T
    slots = queries.shape[0]
    query = queries.reshape(slots, QH, HD)

    def along(array, pairs):
        return lax.ppermute(array, "shard", pairs)

    def between(arrays):
        return [arrays[0]] + [
            lax.ppermute(arrays[step], "rep", [(i, i ^ step) for i in range(replicas)])
            for step in range(1, replicas)
        ]

    sent = project_first(blocks, gain, kv_weight)
    first = along(sent, FIRST)
    asked = between(ask(jobs, query, sent))
    key_0, key_1, key_2, value_0, value_1, value_2 = middle(blocks, gain, kv_weight, asked[1:])
    key_near = along(key_1, NEAR)
    value_near = along(value_1, NEAR)
    width = key_2.shape[1]
    carried = jnp.where(is_inner(lax.axis_index("shard")), first[:, :width].astype(F32), 0.0)
    key_sum = (key_2.astype(F32) + carried).astype(BF16)
    key_third = along(key_sum, THIRD)
    *kept_parts, new_pool = kept(jobs, table, context_lengths, query, kv_pool, key_sum, shards)
    value_third = along(carry(value_2, first, kept_parts[0]), THIRD)
    frequency = THETA ** (-(jnp.arange(HD // 2, dtype=F32) * 2.0 / HD))
    frequency = jnp.concatenate([frequency, frequency])[None, :]
    *key_out, scale, weights, share, level = finish_keys(
        jobs, (key_0, key_near, first, key_third), frequency, asked, stripe
    )
    key_pages = between(key_out)
    finished = finish_values(
        jobs, (value_0, value_near, first, value_third), scale, weights, share, level, kept_parts, shards
    )
    value_pages = between(finished[:4])
    packed = finished[4:]
    parts = [packed[0]] + [
        along(packed[step], [(i, i ^ step) for i in range(shards)]) for step in range(1, shards)
    ]
    here = QH // shards
    kept_out, kept_level, *fresh = gather_parts(jobs, parts, key_pages[3], slots * here, SENDS * here)
    fresh = between(fresh)
    new_pool = place_pages(jobs, table, new_pool, key_pages, value_pages)
    return (new_pool, combine(jobs, kept_out, kept_level, fresh, slots))


def solution(mesh):
    in_specs = (
        P(("outer", "rep"), "shard"),
        P("shard"),
        P("shard", None),
        P("outer", None),
        P(("outer", "rep"), None, "shard"),
        P(("outer", "rep")),
        P(("outer", "rep"), None),
        P(("outer", "rep", "shard"), None, None),
    )
    out_specs = (P(("outer", "rep", "shard"), None, None), P(("outer", "rep"), "shard"))
    fast = mesh.shape["shard"] == 4 and mesh.shape["rep"] == 4
    return jax.shard_map(
        on_device if fast else on_device_general, mesh=mesh, in_specs=in_specs, out_specs=out_specs, check_vma=False
    )
```

```python
import functools
import math

import jax
import jax.numpy as jnp
from jax import lax
from jax.experimental import pallas as pl
from jax.experimental.pallas import tpu as pltpu
from jax.sharding import PartitionSpec as P

D = 8192
QH = 64
KVH = 8
HD = 128
SENDS = 2


THETA = 500000.0
EPS = 1e-05
FLOOR_SCORE = -1e30


def rotate(key_rows, positions):
    half_dim = key_rows.shape[-1] // 2
    frequency = THETA ** (-(jnp.arange(half_dim, dtype=jnp.float32) * 2.0 / key_rows.shape[-1]))
    angles = positions.astype(jnp.float32)[:, None] * frequency[None, :]
    cosine = jnp.cos(angles)[:, None, :]
    sine_part = jnp.sin(angles)[:, None, :]
    first_half = key_rows[..., :half_dim]
    second = key_rows[..., half_dim:]
    return jnp.concatenate(
        [first_half * cosine - second * sine_part, second * cosine + first_half * sine_part],
        axis=-1,
    )


def finish(projected, inverse, positions):
    row_count = projected.shape[0]
    half_width = projected.shape[1] // 2
    scaled = projected * inverse[:, None]
    key_rows = rotate(scaled[:, :half_width].reshape(row_count, KVH, HD), positions).reshape(
        row_count, half_width
    )
    return jnp.concatenate([key_rows, scaled[:, half_width:]], axis=1).astype(jnp.bfloat16)


def spread_out(pieces, targets, replicas):
    outgoing = jnp.zeros((replicas,) + pieces.shape[1:], pieces.dtype)
    for send_index in range(SENDS):
        hit = (jnp.arange(replicas, dtype=jnp.int32) == targets[send_index])[:, None, None]
        outgoing = jnp.where(hit, pieces[send_index][None], outgoing)
    return outgoing


def on_device_general(
    hidden, norm_gain, kv_weight, restore_jobs, page_table, context_lengths, queries, kv_pool
):
    shards = lax.axis_size("shard")
    replicas = lax.axis_size("rep")
    my_replica = lax.axis_index("rep")
    my_shard = lax.axis_index("shard")
    stripe = hidden.shape[0] // SENDS
    page_len = stripe // shards
    features = hidden.shape[1]
    kv_width = kv_weight.shape[1]
    pool_pages = kv_pool.shape[0]
    destination = restore_jobs[:, 0]
    context = restore_jobs[:, 1]
    stripe_index = restore_jobs[:, 2]
    my_targets = lax.dynamic_slice_in_dim(destination, my_replica * SENDS, SENDS, 0)
    is_mine = destination == my_replica
    gain_wide = norm_gain.astype(jnp.float32)[None, :]
    page_rows = jnp.arange(page_len, dtype=jnp.int32)
    wide = hidden.astype(jnp.float32)
    squares = lax.psum(jnp.sum(wide * wide, axis=1), "shard")
    inverse = lax.rsqrt(squares / D + EPS)
    gained = (wide * gain_wide).astype(jnp.bfloat16)
    arranged = gained.reshape(SENDS, shards, page_len, features).transpose(1, 0, 2, 3)
    arranged = arranged.reshape(shards * SENDS * page_len, features)
    owned = lax.psum_scatter(
        jnp.dot(arranged, kv_weight, preferred_element_type=jnp.float32).astype(jnp.bfloat16),
        "shard",
        scatter_dimension=0,
        tiled=True,
    ).astype(jnp.float32)
    owned_inverse = lax.dynamic_slice_in_dim(
        inverse.reshape(SENDS, stripe), my_shard * page_len, page_len, 1
    )
    my_stripes = lax.dynamic_slice_in_dim(stripe_index, my_replica * SENDS, SENDS, 0)
    positions = my_stripes[:, None] * stripe + my_shard * page_len + page_rows[None, :]
    finished = finish(owned, owned_inverse.reshape(-1), positions.reshape(-1)).reshape(
        SENDS, page_len, kv_width
    )
    outgoing = spread_out(finished, my_targets, replicas)
    arrived = lax.all_to_all(outgoing, "rep", split_axis=0, concat_axis=0, tiled=True)
    mine_grid = is_mine.reshape(replicas, SENDS)
    has_page = jnp.any(mine_grid, axis=1)
    which = jnp.argmax(mine_grid.astype(jnp.int32), axis=1)
    job_index = jnp.arange(replicas, dtype=jnp.int32) * SENDS + which
    physical = jnp.where(
        has_page, page_table[context[job_index], stripe_index[job_index], 0], pool_pages
    )
    new_pool = kv_pool.at[physical].set(arrived, mode="drop")
    slots = queries.shape[0]
    pages_dev = page_table.shape[1]
    group = QH // KVH
    scale = 1.0 / math.sqrt(HD)
    cached = new_pool[page_table[:, :, 0]]
    key_rows = cached[..., : KVH * HD].reshape(slots, pages_dev * page_len, KVH, HD)
    value_rows = cached[..., KVH * HD :].reshape(slots, pages_dev * page_len, KVH, HD)
    query_rows = queries.reshape(slots, KVH, group, HD)
    scores = (
        jnp.einsum("cgmd,cpgd->cgmp", query_rows, key_rows, preferred_element_type=jnp.float32)
        * scale
    )
    position = (
        (jnp.arange(pages_dev, dtype=jnp.int32)[:, None] * shards + my_shard) * page_len
        + page_rows[None, :]
    ).reshape(-1)
    usable = (position[None, :] < context_lengths[:, None])[:, None, None, :]
    local_max = jnp.max(jnp.where(usable, scores, FLOOR_SCORE), axis=-1)
    weights = jnp.where(usable, jnp.exp(scores - local_max[..., None]), 0.0)
    denominator = jnp.sum(weights, axis=-1).reshape(slots, QH)
    numerator = jnp.einsum(
        "cgmp,cpgd->cgmd",
        weights.astype(jnp.bfloat16),
        value_rows,
        preferred_element_type=jnp.float32,
    )
    numerator = numerator.reshape(slots, QH, HD)
    local_max = local_max.reshape(slots, QH)
    heads_here = QH // shards
    row_max = lax.pmax(local_max, "shard")
    factor = jnp.exp(local_max - row_max)
    scaled_num = (numerator * factor[..., None]).reshape(slots, QH * HD)
    numerator, denominator = (
        lax.psum(scaled_num.astype(jnp.bfloat16), "shard").astype(jnp.float32),
        lax.psum((denominator * factor).astype(jnp.bfloat16), "shard").astype(jnp.float32),
    )
    numerator = lax.dynamic_slice_in_dim(numerator, my_shard * heads_here * HD, heads_here * HD, 1)
    denominator = lax.dynamic_slice_in_dim(denominator, my_shard * heads_here, heads_here, 1)
    numerator = numerator.reshape(slots, heads_here, HD)
    attention_out = numerator / denominator[..., None]
    return (new_pool, attention_out.reshape(slots, heads_here * HD).astype(jnp.bfloat16))


FIRST = [(0, 1), (3, 2), (1, 3), (2, 0)]
NEAR = [(0, 1), (1, 0), (2, 3), (3, 2)]
THIRD = [(0, 3), (3, 0), (1, 2), (2, 1)]
LANES = 128
GROUP = 2
BF16 = jnp.bfloat16
F32 = jnp.float32
SMEM = pltpu.SMEM
VMEM = pltpu.VMEM
SMALL = pl.CostEstimate(flops=1, bytes_accessed=1, transcendentals=0)
LIMIT = 24 * 1024 * 1024


def whole(space=VMEM):
    return pl.BlockSpec(memory_space=space)


def split_sum(total, offset):
    high = total.astype(BF16).astype(F32)
    low = total - high
    lane = lax.broadcasted_iota(jnp.int32, (total.shape[0], LANES), 1)
    return jnp.where(lane == offset, high, jnp.where(lane == offset + 1, low, 0.0)).astype(BF16)


def row_copies(hidden, blocks, rows_in, sem):
    stripes, _, page_len, _ = hidden.shape
    return [
        pltpu.make_async_copy(
            hidden.at[stripe, block],
            rows_in.at[pl.ds((place * stripes + stripe) * page_len, page_len)],
            sem.at[place * stripes + stripe],
        )
        for place, block in enumerate(blocks)
        for stripe in range(stripes)
    ]


def weight_copies(weight, tiles, sem):
    half = weight.shape[1] // 2
    return [
        pltpu.make_async_copy(weight.at[:, pl.ds(side * half, half)], tiles.at[side], sem.at[side])
        for side in range(2)
    ]


def scale_rows(rows_in, gained, gain_in, span):
    wide_gain = gain_in[...].astype(F32).reshape(1, gain_in.shape[0])
    gained[span] = (rows_in[span].astype(F32) * wide_gain).astype(BF16)


def put_squares(rows_in, span, out, columns, offset):
    squares = jnp.zeros((out.shape[0], LANES), F32)
    for lane in range(rows_in.shape[1] // LANES):
        part = rows_in[span, lane * LANES : (lane + 1) * LANES].astype(F32)
        squares = squares + part * part
    total = jnp.sum(squares, axis=1, keepdims=True)
    out[:, columns] = split_sum(total, offset)


def is_inner(shard):
    return (shard == 1) | (shard == 2)


def far_blocks(shard):
    lower = shard < 2
    return jnp.where(lower, 2, 1), jnp.where(lower, 3, 0)


def first_kernel(hidden, gain, weight, out, rows_in, gained, gain_in, tiles, row_sem, gain_sem, tile_sem):
    shard = lax.axis_index("shard")
    half = weight.shape[1] // 2
    inner_block, outer_block = far_blocks(shard)
    rows_here = row_copies(hidden, [jnp.where(is_inner(shard), outer_block, inner_block)], rows_in, row_sem)
    tiles_here = weight_copies(weight, tiles, tile_sem)
    gain_copy = pltpu.make_async_copy(gain, gain_in, gain_sem)
    gain_copy.start()
    for copy in rows_here + tiles_here:
        copy.start()
    gain_copy.wait()
    for copy in rows_here:
        copy.wait()
    scale_rows(rows_in, gained, gain_in, slice(None))
    put_squares(rows_in, slice(None), out, slice(half, half + LANES), 0)
    for side, columns in enumerate((slice(0, half), slice(half + LANES, 2 * half + LANES))):
        tiles_here[side].wait()
        out[:, columns] = jnp.dot(gained[...], tiles[side], preferred_element_type=F32).astype(BF16)


def project_first(hidden, gain, weight):
    stripes, blocks, page_len, features = hidden.shape
    half = weight.shape[1] // 2
    rows = stripes * page_len
    return pl.pallas_call(
        first_kernel,
        in_specs=[whole(pl.ANY)] * 3,
        out_specs=whole(),
        out_shape=jax.ShapeDtypeStruct((rows, 2 * half + LANES), BF16),
        scratch_shapes=[
            pltpu.VMEM((rows, features), BF16),
            pltpu.VMEM((rows, features), BF16),
            pltpu.VMEM((features,), BF16),
            pltpu.VMEM((2, features, half), BF16),
            pltpu.SemaphoreType.DMA((stripes,)),
            pltpu.SemaphoreType.DMA,
            pltpu.SemaphoreType.DMA((2,)),
        ],
        compiler_params=pltpu.CompilerParams(vmem_limit_bytes=LIMIT),
        cost_estimate=SMALL,
        name="project_first",
    )(hidden, gain, weight)


def head_spread(query, width):
    heads = query.shape[0]
    group = heads // (width // LANES)
    head = lax.broadcasted_iota(jnp.int32, (heads, LANES), 0)
    pieces = [jnp.where(head // group == g, query, jnp.zeros_like(query)) for g in range(width // LANES)]
    return jnp.concatenate(pieces, axis=1)


def head_pick(products):
    heads, width = products.shape
    group = heads // (width // LANES)
    head = lax.broadcasted_iota(jnp.int32, (heads, LANES), 0)
    picked = products[:, :LANES]
    for g in range(1, width // LANES):
        picked = jnp.where(head // group == g, products[:, g * LANES : (g + 1) * LANES], picked)
    return picked


def score(query, key_rows):
    spread = head_spread(query, key_rows.shape[1])
    scores = lax.dot_general(spread, key_rows, (((1,), (1,)), ((), ())), preferred_element_type=F32)
    return scores * (1.0 / math.sqrt(LANES))


def attend(query, key_rows, value_rows, usable):
    scores = jnp.where(usable, score(query, key_rows), FLOOR_SCORE)
    largest = jnp.max(scores, axis=1, keepdims=True)
    weights = jnp.where(usable, jnp.exp(scores - largest), 0.0)
    total = jnp.sum(weights, axis=1, keepdims=True)
    picked = head_pick(jnp.dot(weights.astype(BF16), value_rows, preferred_element_type=F32))
    some = total > 0.0
    safe = jnp.where(some, total, 1.0)
    return picked / safe, jnp.where(some, largest + jnp.log(safe), FLOOR_SCORE)


def split_lines(lines, first):
    high = lines.astype(BF16).astype(F32)
    middle_part = (lines - high).astype(BF16).astype(F32)
    low = lines - high - middle_part
    place = lax.broadcasted_iota(jnp.int32, lines.shape, 0) - first
    return jnp.where(place == 0, high, jnp.where(place == 1, middle_part, jnp.where(place == 2, low, 0.0)))


def join_lines(tail, first, rows):
    line = jnp.sum(tail[first : first + 3].astype(F32), axis=0, keepdims=True)
    return jnp.broadcast_to(line, (LANES, LANES)).T[:rows]


def project_keys_kernel(hidden, gain, weight, after, own, near, third, gained, rows_in, gain_in, tile, *sems):
    row_sem, gain_sem, tile_sem = sems
    shard = lax.axis_index("shard")
    rows = own.shape[0]
    half = weight.shape[1] // 2
    inner_block, outer_block = far_blocks(shard)
    blocks = [shard, jnp.bitwise_xor(shard, 1), jnp.where(is_inner(shard), inner_block, outer_block)]
    rows_here = row_copies(hidden, blocks, rows_in, row_sem)
    tile_copy = pltpu.make_async_copy(weight.at[:, pl.ds(0, half)], tile, tile_sem)
    gain_copy = pltpu.make_async_copy(gain, gain_in, gain_sem)
    gain_copy.start()
    for copy in rows_here:
        copy.start()
    tile_copy.start()
    gain_copy.wait()
    for copy in rows_here:
        copy.wait()
    scale_rows(rows_in, gained, gain_in, slice(None))
    for place, ref in enumerate((own, near, third)):
        span = slice(place * rows, (place + 1) * rows)
        put_squares(rows_in, span, ref, slice(half, half + LANES), 2 if place == 2 else 0)
    tile_copy.wait()
    product = jnp.dot(gained[...], tile[...], preferred_element_type=F32).astype(BF16)
    for place, ref in enumerate((own, near, third)):
        ref[:, :half] = product[place * rows : (place + 1) * rows]


def project_keys(hidden, gain, weight, after):
    stripes, blocks, page_len, features = hidden.shape
    half = weight.shape[1] // 2
    rows = stripes * page_len
    return pl.pallas_call(
        project_keys_kernel,
        in_specs=[whole(pl.ANY)] * 4,
        out_specs=[whole()] * 4,
        out_shape=[jax.ShapeDtypeStruct((rows, half + LANES), BF16)] * 3
        + [jax.ShapeDtypeStruct((3 * rows, features), BF16)],
        scratch_shapes=[
            pltpu.VMEM((3 * rows, features), BF16),
            pltpu.VMEM((features,), BF16),
            pltpu.VMEM((features, half), BF16),
            pltpu.SemaphoreType.DMA((3 * stripes,)),
            pltpu.SemaphoreType.DMA,
            pltpu.SemaphoreType.DMA,
        ],
        compiler_params=pltpu.CompilerParams(vmem_limit_bytes=LIMIT),
        cost_estimate=SMALL,
        name="project_keys",
    )(hidden, gain, weight, after)


def project_values_kernel(gained, weight, *rest):
    own, near, third, tile, sem = rest[-5:]
    rows, half = own.shape
    tile_copy = pltpu.make_async_copy(weight.at[:, pl.ds(half, half)], tile, sem)
    tile_copy.start()
    tile_copy.wait()
    product = jnp.dot(gained[...], tile[...], preferred_element_type=F32).astype(BF16)
    for place, ref in enumerate((own, near, third)):
        ref[...] = product[place * rows : (place + 1) * rows]


def project_values(gained, weight, after):
    half = weight.shape[1] // 2
    return pl.pallas_call(
        project_values_kernel,
        in_specs=[whole()] + [whole(pl.ANY)] * (1 + len(after)),
        out_specs=[whole()] * 3,
        out_shape=[jax.ShapeDtypeStruct((gained.shape[0] // 3, half), BF16)] * 3,
        scratch_shapes=[pltpu.VMEM((weight.shape[0], half), BF16), pltpu.SemaphoreType.DMA],
        compiler_params=pltpu.CompilerParams(vmem_limit_bytes=LIMIT),
        cost_estimate=SMALL,
        name="project_values",
    )(gained, weight, *after)


def carry_kernel(mine, first, *rest, start):
    out = rest[-1]
    inner = is_inner(lax.axis_index("shard"))
    arrived = first[:, start : start + mine.shape[1]].astype(F32)
    out[...] = (mine[...].astype(F32) + jnp.where(inner, arrived, 0.0)).astype(BF16)


def carry(mine, first, after, start):
    return pl.pallas_call(
        functools.partial(carry_kernel, start=start),
        in_specs=[whole(), whole()] + [whole(pl.ANY)] * len(after),
        out_specs=whole(),
        out_shape=jax.ShapeDtypeStruct(mine.shape, BF16),
        compiler_params=pltpu.CompilerParams(vmem_limit_bytes=LIMIT),
        cost_estimate=SMALL,
        name="carry",
    )(mine, first, *after)


def rep_shapes(rows, width):
    return [jax.ShapeDtypeStruct((rows, width), BF16)] * 4


def ask_kernel(jobs, query, after, *outs):
    for step, out in enumerate(outs):
        out[...] = query[job_from(jobs, step)[1]]


def ask(jobs, query, after):
    return pl.pallas_call(
        ask_kernel,
        in_specs=[whole(SMEM), whole(), whole(pl.ANY)],
        out_specs=[whole()] * 4,
        out_shape=rep_shapes(*query.shape[1:]),
        compiler_params=pltpu.CompilerParams(vmem_limit_bytes=LIMIT),
        cost_estimate=SMALL,
        name="ask",
    )(jobs, query, after)


def kept_kernel(jobs, table, lengths, query, pool, *rest, shards, after):
    outs = rest[after : after + 4]
    new_pool, pages, total, level, in_sem, out_sem = rest[after + 4 :]
    slots, heads, _ = query.shape
    here = heads // shards
    rows = slots * here
    replica = lax.axis_index("rep")
    shard = lax.axis_index("shard")
    page_len = pool.shape[1]
    half = pool.shape[2] // 2

    def copy_in(context, page):
        place = context * 2 + page
        return pltpu.make_async_copy(pool.at[table[page, context]], pages.at[place], in_sem.at[place])

    def copy_out(context, page):
        place = context * 2 + page
        return pltpu.make_async_copy(pages.at[place], new_pool.at[table[page, context]], out_sem.at[place])

    @pl.loop(0, slots)
    def _(context):
        for page in range(2):
            copy_in(context, page).start()

    lane = lax.broadcasted_iota(jnp.int32, (heads, 2 * page_len), 1)
    page_of = lane // page_len
    position = (page_of * shards + shard) * page_len + lane % page_len

    def context_part(context):
        gone = [jnp.int32(0), jnp.int32(0)]
        for job in range(jobs.shape[1]):
            hit = (jobs[0, job] == replica) & (jobs[1, job] == context)
            for page in range(2):
                gone[page] = gone[page] | (hit & (jobs[2, job] == page)).astype(jnp.int32)
        usable = (position < lengths[context]) & (jnp.where(page_of == 0, gone[0], gone[1]) == 0)
        both = pages[pl.ds(context * 2, 2)].reshape(2 * page_len, 2 * half)
        return attend(query[context], both[:, :half], both[:, half:], usable)

    @pl.loop(0, slots // GROUP)
    def _(index):
        contexts = [index * GROUP + member for member in range(GROUP)]
        for context in contexts:
            for page in range(2):
                copy_in(context, page).wait()
                copy_out(context, page).start()
        results = [context_part(context) for context in contexts]
        for context, (result, logarithm) in zip(contexts, results):
            total[context] = result
            level[context] = jnp.broadcast_to(logarithm, result.shape)

    for step, out in enumerate(outs):
        start = pl.multiple_of(jnp.bitwise_xor(shard, step) * here, here)
        out[:rows] = total[:, pl.ds(start, here), :].reshape(rows, LANES).astype(BF16)
        lines = level[:, pl.ds(start, here), :].reshape(rows, LANES).T[:16]
        out[rows:] = split_lines(lines, 0).astype(BF16)

    @pl.loop(0, slots)
    def _(context):
        for page in range(2):
            copy_out(context, page).wait()


def kept(jobs, table, lengths, query, pool, after, shards):
    slots, heads, size = query.shape
    return pl.pallas_call(
        functools.partial(kept_kernel, shards=shards, after=len(after)),
        in_specs=[whole(SMEM)] * 3 + [whole()] + [whole(pl.ANY)] * (1 + len(after)),
        out_specs=[whole()] * 4 + [whole(pl.ANY)],
        out_shape=[jax.ShapeDtypeStruct((slots * heads // shards + 16, size), BF16)] * 4
        + [jax.ShapeDtypeStruct(pool.shape, pool.dtype)],
        scratch_shapes=[
            pltpu.VMEM((slots * 2,) + pool.shape[1:], pool.dtype),
            pltpu.VMEM(query.shape, F32),
            pltpu.VMEM(query.shape, F32),
            pltpu.SemaphoreType.DMA((slots * 2,)),
            pltpu.SemaphoreType.DMA((slots * 2,)),
        ],
        compiler_params=pltpu.CompilerParams(vmem_limit_bytes=LIMIT),
        cost_estimate=SMALL,
        name="kept",
    )(jobs, table, lengths, query, pool, *after)


def route(jobs, finished, outs):
    replica = lax.axis_index("rep")
    page_len = finished.shape[0] // SENDS
    for step, out in enumerate(outs):
        chosen = jobs[0, replica * SENDS] == jnp.bitwise_xor(replica, step)

        @pl.when(chosen)
        def _():
            out[...] = finished[:page_len]

        @pl.when(jnp.logical_not(chosen))
        def _():
            out[...] = finished[page_len:]


def add_parts(own, near, first, third, columns, first_columns):
    direct = jnp.where(is_inner(lax.axis_index("shard")), 0.0, first[:, first_columns].astype(F32))
    return (own[:, columns].astype(F32) + near[:, columns].astype(F32)) + (third[:, columns].astype(F32) + direct)


def finish_keys_kernel(jobs, own, near, first, third, frequency, *rest, stripe):
    asked, outs = rest[:4], rest[4:8]
    scale, weights_out, share, level, finished = rest[8:]
    replica = lax.axis_index("rep")
    shard = lax.axis_index("shard")
    rows = own.shape[0]
    page_len = rows // SENDS
    width = own.shape[1] - LANES

    def added(columns):
        return add_parts(own, near, first, third, columns, columns)

    squares = jnp.sum(added(slice(width, width + LANES)), axis=1, keepdims=True)
    inverse = jnp.broadcast_to(lax.rsqrt(squares / D + EPS), (rows, LANES))
    scale[...] = inverse
    row = lax.broadcasted_iota(jnp.int32, (rows, LANES), 0)
    lane = lax.broadcasted_iota(jnp.int32, (rows, LANES), 1)
    index = jnp.where(row < page_len, jobs[2, replica * SENDS], jobs[2, replica * SENDS + 1])
    position = index * stripe + shard * page_len + row % page_len
    angle = position.astype(F32) * frequency[...]
    cosine = jnp.cos(angle) * inverse
    sine_part = jnp.where(lane < LANES // 2, -jnp.sin(angle), jnp.sin(angle)) * inverse
    for head in range(width // LANES):
        columns = slice(head * LANES, (head + 1) * LANES)
        value = added(columns)
        turned = value * cosine + pltpu.roll(value, LANES // 2, 1) * sine_part
        finished[:, columns] = turned.astype(BF16)
    route(jobs, finished, outs)
    for send in range(SENDS):
        step = jnp.bitwise_xor(jobs[0, replica * SENDS + send], replica)
        query = asked[0][...]
        for other in range(1, 4):
            query = jnp.where(step == other, asked[other][...], query)
        scores = score(query, finished[send * page_len : (send + 1) * page_len])
        largest = jnp.max(scores, axis=1, keepdims=True)
        weights = jnp.exp(scores - largest)
        total = jnp.sum(weights, axis=1, keepdims=True)
        weights_out[send] = weights.astype(BF16)
        share[send] = jnp.broadcast_to(1.0 / total, share.shape[1:])
        level[send] = jnp.broadcast_to(largest + jnp.log(total), level.shape[1:])


def finish_values_kernel(jobs, own, near, first, third, scale, weights, share, level, *rest, shards, after):
    kept_parts, outs = rest[:4], rest[4 + after : 8 + after]
    packed, finished, result = rest[8 + after : 12 + after], rest[12 + after], rest[13 + after]
    shard = lax.axis_index("shard")
    for head in range(own.shape[1] // LANES):
        columns = slice(head * LANES, (head + 1) * LANES)
        start = first.shape[1] - own.shape[1] + head * LANES
        total = add_parts(own, near, first, third, columns, slice(start, start + LANES))
        finished[:, columns] = (total * scale[...]).astype(BF16)
    route(jobs, finished, outs)
    page_len = own.shape[0] // SENDS
    for send in range(SENDS):
        products = jnp.dot(
            weights[send], finished[send * page_len : (send + 1) * page_len], preferred_element_type=F32
        )
        result[send] = head_pick(products) * share[send]
    here = level.shape[1] // shards
    count = SENDS * here
    rows = kept_parts[0].shape[0] - 16
    for step in range(4):
        start = pl.multiple_of(jnp.bitwise_xor(shard, step) * here, here)
        packed[step][:rows] = kept_parts[step][:rows]
        packed[step][rows : rows + count] = result[:, pl.ds(start, here), :].reshape(count, LANES).astype(BF16)
        mine = level[:, pl.ds(start, here), :].reshape(count, LANES)
        lines = jnp.concatenate([mine] + [jnp.zeros((LANES - count, LANES), F32)], axis=0).T[:16]
        tail = kept_parts[step][rows:].astype(F32) + split_lines(lines, 3)
        packed[step][rows + count :] = tail.astype(BF16)


def finish_keys(jobs, parts, frequency, asked, stripe):
    rows = parts[0].shape[0]
    width = parts[0].shape[1] - LANES
    heads = asked[0].shape[0]
    page_len = rows // SENDS
    return pl.pallas_call(
        functools.partial(finish_keys_kernel, stripe=stripe),
        in_specs=[whole(SMEM)] + [whole()] * 9,
        out_specs=[whole()] * 8,
        out_shape=rep_shapes(page_len, width)
        + [
            jax.ShapeDtypeStruct((rows, LANES), F32),
            jax.ShapeDtypeStruct((SENDS, heads, page_len), BF16),
            jax.ShapeDtypeStruct((SENDS, heads, LANES), F32),
            jax.ShapeDtypeStruct((SENDS, heads, LANES), F32),
        ],
        scratch_shapes=[pltpu.VMEM((rows, width), BF16)],
        compiler_params=pltpu.CompilerParams(vmem_limit_bytes=LIMIT),
        cost_estimate=SMALL,
        name="finish_keys",
    )(jobs, *parts, frequency, *asked)


def finish_values(jobs, parts, scale, weights, share, level, kept_parts, after, shards):
    rows, width = parts[0].shape
    heads = level.shape[1]
    page_len = rows // SENDS
    packed = kept_parts[0].shape[0] + SENDS * heads // shards
    return pl.pallas_call(
        functools.partial(finish_values_kernel, shards=shards, after=len(after)),
        in_specs=[whole(SMEM)] + [whole()] * 12 + [whole(pl.ANY)] * len(after),
        out_specs=[whole()] * 8,
        out_shape=rep_shapes(page_len, width) + [jax.ShapeDtypeStruct((packed, LANES), BF16)] * 4,
        scratch_shapes=[pltpu.VMEM((rows, width), BF16), pltpu.VMEM((SENDS, heads, LANES), F32)],
        compiler_params=pltpu.CompilerParams(vmem_limit_bytes=LIMIT),
        cost_estimate=SMALL,
        name="finish_values",
    )(jobs, *parts, scale, weights, share, level, *kept_parts, *after)


def job_from(jobs, step):
    replica = lax.axis_index("rep")
    first = jnp.bitwise_xor(replica, step) * SENDS
    hit_first = jobs[0, first] == replica
    hit = hit_first | (jobs[0, first + 1] == replica)
    row = jnp.where(hit_first, first, first + 1)
    return hit, jobs[1, row], jobs[2, row]


def place_kernel(jobs, table, pool, *rest):
    key_pages, value_pages = rest[:4], rest[4:8]
    out, done, pages, sem = rest[8:]
    half = rest[0].shape[1]
    done[...] = jnp.zeros_like(done)
    for wait in (False, True):
        for step in range(4):
            hit, context, page = job_from(jobs, step)

            @pl.when(hit)
            def _():
                slot = table[page, context]
                copy = pltpu.make_async_copy(pages.at[step], out.at[slot], sem.at[step])
                if wait:
                    copy.wait()
                else:
                    pages[step, :, :half] = key_pages[step][...]
                    pages[step, :, half:] = value_pages[step][...]
                    copy.start()


def place_pages(jobs, table, pool, key_pages, value_pages):
    return pl.pallas_call(
        place_kernel,
        in_specs=[whole(SMEM)] * 2 + [whole(pl.ANY)] + [whole()] * 8,
        out_specs=[whole(pl.ANY), whole()],
        out_shape=[jax.ShapeDtypeStruct(pool.shape, pool.dtype), jax.ShapeDtypeStruct((16, LANES), BF16)],
        scratch_shapes=[pltpu.VMEM((4,) + pool.shape[1:], pool.dtype), pltpu.SemaphoreType.DMA((4,))],
        input_output_aliases={2: 0},
        compiler_params=pltpu.CompilerParams(vmem_limit_bytes=LIMIT),
        cost_estimate=SMALL,
        name="place_pages",
    )(jobs, table, pool, *key_pages, *value_pages)


def blend(parts, levels):
    top = functools.reduce(jnp.maximum, levels)
    shares = [jnp.exp(level - top) for level in levels]
    both = functools.reduce(jnp.add, shares)
    total = functools.reduce(jnp.add, [part * share for part, share in zip(parts, shares)])
    return total / both, top + jnp.log(both)


def gather_kernel(jobs, *refs, rows, count):
    parts, page, outs, page_out = refs[:4], refs[4], refs[5:9], refs[9]
    page_out[...] = page[...]
    mixed, level = blend(
        [ref[rows : rows + count].astype(F32) for ref in parts],
        [join_lines(ref[rows + count :], 3, count) for ref in parts],
    )
    here = count // SENDS
    replica = lax.axis_index("rep")
    lane = lax.broadcasted_iota(jnp.int32, (here, LANES), 1)
    for step, out in enumerate(outs):
        chosen = jobs[0, replica * SENDS] == jnp.bitwise_xor(replica, step)
        total = jnp.where(chosen, level[:here], level[here:])
        high = total.astype(BF16).astype(F32)
        middle_part = (total - high).astype(BF16).astype(F32)
        low = total - high - middle_part
        out[:, :LANES] = jnp.where(chosen, mixed[:here], mixed[here:]).astype(BF16)
        out[:, LANES:] = jnp.where(
            lane == 0, high, jnp.where(lane == 1, middle_part, jnp.where(lane == 2, low, 0.0))
        ).astype(BF16)


def gather_parts(jobs, parts, page, rows, count):
    return pl.pallas_call(
        functools.partial(gather_kernel, rows=rows, count=count),
        in_specs=[whole(SMEM)] + [whole()] * 5,
        out_specs=[whole()] * 5,
        out_shape=rep_shapes(count // SENDS, 2 * LANES) + [jax.ShapeDtypeStruct(page.shape, BF16)],
        compiler_params=pltpu.CompilerParams(vmem_limit_bytes=LIMIT),
        cost_estimate=SMALL,
        name="gather_parts",
    )(jobs, *parts, page)


def blend_kernel(*refs, rows, count):
    parts, after, kept_out, kept_level = refs[:4], refs[4], refs[5], refs[6]
    mixed, level = blend(
        [ref[:rows].astype(F32) for ref in parts], [join_lines(ref[rows + count :], 0, rows) for ref in parts]
    )
    kept_out[...] = mixed
    kept_level[...] = level


def blend_kept(parts, after, rows, count):
    return pl.pallas_call(
        functools.partial(blend_kernel, rows=rows, count=count),
        in_specs=[whole()] * 4 + [whole(pl.ANY)],
        out_specs=[whole()] * 2,
        out_shape=[jax.ShapeDtypeStruct((rows, LANES), F32)] * 2,
        compiler_params=pltpu.CompilerParams(vmem_limit_bytes=LIMIT),
        cost_estimate=SMALL,
        name="blend_kept",
    )(*parts, after)


def combine_kernel(jobs, kept_out, kept_level, *refs):
    parts, out, mixed = refs[:4], refs[5], refs[6]
    slots, here, size = mixed.shape
    mixed[...] = kept_out[...].reshape(mixed.shape)
    for step, ref in enumerate(parts):
        hit, context, _ = job_from(jobs, step)

        @pl.when(hit)
        def _():
            fresh_level = jnp.sum(ref[:, LANES:].astype(F32), axis=1, keepdims=True)
            fresh_level = jnp.broadcast_to(fresh_level, (here, LANES))
            old_level = kept_level[pl.ds(pl.multiple_of(context * here, here), here)]
            blended, _ = blend([mixed[context], ref[:, :LANES].astype(F32)], [old_level, fresh_level])
            mixed[context] = blended

    for head in range(here):
        out[:, head * size : (head + 1) * size] = mixed[:, head, :].astype(BF16)


def combine(jobs, kept_out, kept_level, parts, after, slots):
    here = kept_out.shape[0] // slots
    return pl.pallas_call(
        combine_kernel,
        in_specs=[whole(SMEM)] + [whole()] * 6 + [whole(pl.ANY)],
        out_specs=whole(),
        out_shape=jax.ShapeDtypeStruct((slots, here * LANES), BF16),
        scratch_shapes=[pltpu.VMEM((slots, here, LANES), F32)],
        compiler_params=pltpu.CompilerParams(vmem_limit_bytes=LIMIT),
        cost_estimate=SMALL,
        name="combine",
    )(jobs, kept_out, kept_level, *parts, after)


def on_device(
    hidden, norm_gain, kv_weight, restore_jobs, page_table, context_lengths, queries, kv_pool
):
    shards = lax.axis_size("shard")
    replicas = lax.axis_size("rep")
    stripe = hidden.shape[0] // SENDS
    page_len = stripe // shards
    kv_weight = pltpu.with_memory_space_constraint(kv_weight, pltpu.HBM)
    kv_pool = pltpu.with_memory_space_constraint(kv_pool, pltpu.HBM)
    gain = pltpu.with_memory_space_constraint(norm_gain, pltpu.HBM)
    blocks = pltpu.with_memory_space_constraint(
        hidden.reshape(SENDS, shards, page_len, hidden.shape[1]), pltpu.HBM
    )
    jobs = restore_jobs.T
    table = page_table[:, :, 0].T
    slots = queries.shape[0]
    query = queries.reshape(slots, QH, HD)

    def along(array, pairs):
        return lax.ppermute(array, "shard", pairs)

    def across(array, step):
        return lax.ppermute(array, "rep", [(i, i ^ step) for i in range(replicas)])

    def between(arrays):
        return [arrays[0]] + [across(arrays[step], step) for step in range(1, replicas)]

    sent = project_first(blocks, gain, kv_weight)
    first = along(sent, FIRST)
    key_0, key_1, key_2, gained = project_keys(blocks, gain, kv_weight, sent)
    key_near = along(key_1, NEAR)
    asked = between(ask(jobs, query, key_1))
    key_third = along(carry(key_2, first, asked[1:], 0), THIRD)
    value_0, value_1, value_2 = project_values(gained, kv_weight, asked[1:])
    value_near = along(value_1, NEAR)
    value_third = along(carry(value_2, first, [key_near, key_third], key_2.shape[1]), THIRD)
    frequency = THETA ** (-(jnp.arange(HD // 2, dtype=F32) * 2.0 / HD))
    frequency = jnp.concatenate([frequency, frequency])[None, :]
    *key_out, scale, weights, share, level = finish_keys(
        jobs, (key_0, key_near, first, key_third), frequency, asked, stripe
    )
    key_pages = between(key_out)
    *kept_parts, new_pool = kept(jobs, table, context_lengths, query, kv_pool, [scale], shards)
    finished = finish_values(
        jobs,
        (value_0, value_near, first, value_third),
        scale,
        weights,
        share,
        level,
        kept_parts,
        key_pages[1:],
        shards,
    )
    value_pages = [finished[0], None, across(finished[2], 2), across(finished[3], 3)]
    packed = finished[4:]
    parts = [packed[0]] + [
        along(packed[step], [(i, i ^ step) for i in range(shards)]) for step in range(1, shards)
    ]
    here = QH // shards
    *gathered, near_page = gather_parts(jobs, parts, finished[1], slots * here, SENDS * here)
    fresh = between(gathered)
    value_pages[1] = across(near_page, 1)
    kept_out, kept_level = blend_kept(parts, gathered[0], slots * here, SENDS * here)
    new_pool, placed = place_pages(jobs, table, new_pool, key_pages, value_pages)
    return (new_pool, combine(jobs, kept_out, kept_level, fresh, placed, slots))


def solution(mesh):
    in_specs = (
        P(("outer", "rep"), "shard"),
        P("shard"),
        P("shard", None),
        P("outer", None),
        P(("outer", "rep"), None, "shard"),
        P(("outer", "rep")),
        P(("outer", "rep"), None),
        P(("outer", "rep", "shard"), None, None),
    )
    out_specs = (P(("outer", "rep", "shard"), None, None), P(("outer", "rep"), "shard"))
    fast = mesh.shape["shard"] == 4 and mesh.shape["rep"] == 4
    return jax.shard_map(
        on_device if fast else on_device_general, mesh=mesh, in_specs=in_specs, out_specs=out_specs, check_vma=False
    )
```

```python
import functools
import math

import jax
import jax.numpy as jnp
from jax import lax
from jax.experimental import pallas as pl
from jax.experimental.pallas import tpu as pltpu
from jax.sharding import PartitionSpec as P

D = 8192
QH = 64
KVH = 8
HD = 128
SENDS = 2


THETA = 500000.0
EPS = 1e-05
FLOOR_SCORE = -1e30


def rotate(key_rows, positions):
    half_dim = key_rows.shape[-1] // 2
    frequency = THETA ** (-(jnp.arange(half_dim, dtype=jnp.float32) * 2.0 / key_rows.shape[-1]))
    angles = positions.astype(jnp.float32)[:, None] * frequency[None, :]
    cosine = jnp.cos(angles)[:, None, :]
    sine_part = jnp.sin(angles)[:, None, :]
    first_half = key_rows[..., :half_dim]
    second = key_rows[..., half_dim:]
    return jnp.concatenate(
        [first_half * cosine - second * sine_part, second * cosine + first_half * sine_part],
        axis=-1,
    )


def finish(projected, inverse, positions):
    row_count = projected.shape[0]
    half_width = projected.shape[1] // 2
    scaled = projected * inverse[:, None]
    key_rows = rotate(scaled[:, :half_width].reshape(row_count, KVH, HD), positions).reshape(
        row_count, half_width
    )
    return jnp.concatenate([key_rows, scaled[:, half_width:]], axis=1).astype(jnp.bfloat16)


def spread_out(pieces, targets, replicas):
    outgoing = jnp.zeros((replicas,) + pieces.shape[1:], pieces.dtype)
    for send_index in range(SENDS):
        hit = (jnp.arange(replicas, dtype=jnp.int32) == targets[send_index])[:, None, None]
        outgoing = jnp.where(hit, pieces[send_index][None], outgoing)
    return outgoing


def on_device_general(
    hidden, norm_gain, kv_weight, restore_jobs, page_table, context_lengths, queries, kv_pool
):
    shards = lax.axis_size("shard")
    replicas = lax.axis_size("rep")
    my_replica = lax.axis_index("rep")
    my_shard = lax.axis_index("shard")
    stripe = hidden.shape[0] // SENDS
    page_len = stripe // shards
    features = hidden.shape[1]
    kv_width = kv_weight.shape[1]
    pool_pages = kv_pool.shape[0]
    destination = restore_jobs[:, 0]
    context = restore_jobs[:, 1]
    stripe_index = restore_jobs[:, 2]
    my_targets = lax.dynamic_slice_in_dim(destination, my_replica * SENDS, SENDS, 0)
    is_mine = destination == my_replica
    gain_wide = norm_gain.astype(jnp.float32)[None, :]
    page_rows = jnp.arange(page_len, dtype=jnp.int32)
    wide = hidden.astype(jnp.float32)
    squares = lax.psum(jnp.sum(wide * wide, axis=1), "shard")
    inverse = lax.rsqrt(squares / D + EPS)
    gained = (wide * gain_wide).astype(jnp.bfloat16)
    arranged = gained.reshape(SENDS, shards, page_len, features).transpose(1, 0, 2, 3)
    arranged = arranged.reshape(shards * SENDS * page_len, features)
    owned = lax.psum_scatter(
        jnp.dot(arranged, kv_weight, preferred_element_type=jnp.float32).astype(jnp.bfloat16),
        "shard",
        scatter_dimension=0,
        tiled=True,
    ).astype(jnp.float32)
    owned_inverse = lax.dynamic_slice_in_dim(
        inverse.reshape(SENDS, stripe), my_shard * page_len, page_len, 1
    )
    my_stripes = lax.dynamic_slice_in_dim(stripe_index, my_replica * SENDS, SENDS, 0)
    positions = my_stripes[:, None] * stripe + my_shard * page_len + page_rows[None, :]
    finished = finish(owned, owned_inverse.reshape(-1), positions.reshape(-1)).reshape(
        SENDS, page_len, kv_width
    )
    outgoing = spread_out(finished, my_targets, replicas)
    arrived = lax.all_to_all(outgoing, "rep", split_axis=0, concat_axis=0, tiled=True)
    mine_grid = is_mine.reshape(replicas, SENDS)
    has_page = jnp.any(mine_grid, axis=1)
    which = jnp.argmax(mine_grid.astype(jnp.int32), axis=1)
    job_index = jnp.arange(replicas, dtype=jnp.int32) * SENDS + which
    physical = jnp.where(
        has_page, page_table[context[job_index], stripe_index[job_index], 0], pool_pages
    )
    new_pool = kv_pool.at[physical].set(arrived, mode="drop")
    slots = queries.shape[0]
    pages_dev = page_table.shape[1]
    group = QH // KVH
    scale = 1.0 / math.sqrt(HD)
    cached = new_pool[page_table[:, :, 0]]
    key_rows = cached[..., : KVH * HD].reshape(slots, pages_dev * page_len, KVH, HD)
    value_rows = cached[..., KVH * HD :].reshape(slots, pages_dev * page_len, KVH, HD)
    query_rows = queries.reshape(slots, KVH, group, HD)
    scores = (
        jnp.einsum("cgmd,cpgd->cgmp", query_rows, key_rows, preferred_element_type=jnp.float32)
        * scale
    )
    position = (
        (jnp.arange(pages_dev, dtype=jnp.int32)[:, None] * shards + my_shard) * page_len
        + page_rows[None, :]
    ).reshape(-1)
    usable = (position[None, :] < context_lengths[:, None])[:, None, None, :]
    local_max = jnp.max(jnp.where(usable, scores, FLOOR_SCORE), axis=-1)
    weights = jnp.where(usable, jnp.exp(scores - local_max[..., None]), 0.0)
    denominator = jnp.sum(weights, axis=-1).reshape(slots, QH)
    numerator = jnp.einsum(
        "cgmp,cpgd->cgmd",
        weights.astype(jnp.bfloat16),
        value_rows,
        preferred_element_type=jnp.float32,
    )
    numerator = numerator.reshape(slots, QH, HD)
    local_max = local_max.reshape(slots, QH)
    heads_here = QH // shards
    row_max = lax.pmax(local_max, "shard")
    factor = jnp.exp(local_max - row_max)
    scaled_num = (numerator * factor[..., None]).reshape(slots, QH * HD)
    numerator, denominator = (
        lax.psum(scaled_num.astype(jnp.bfloat16), "shard").astype(jnp.float32),
        lax.psum((denominator * factor).astype(jnp.bfloat16), "shard").astype(jnp.float32),
    )
    numerator = lax.dynamic_slice_in_dim(numerator, my_shard * heads_here * HD, heads_here * HD, 1)
    denominator = lax.dynamic_slice_in_dim(denominator, my_shard * heads_here, heads_here, 1)
    numerator = numerator.reshape(slots, heads_here, HD)
    attention_out = numerator / denominator[..., None]
    return (new_pool, attention_out.reshape(slots, heads_here * HD).astype(jnp.bfloat16))


FIRST = [(0, 1), (3, 2), (1, 3), (2, 0)]
NEAR = [(0, 1), (1, 0), (2, 3), (3, 2)]
THIRD = [(0, 3), (3, 0), (1, 2), (2, 1)]
LANES = 128
GROUP = 2
BF16 = jnp.bfloat16
F32 = jnp.float32
SMEM = pltpu.SMEM
VMEM = pltpu.VMEM
SMALL = pl.CostEstimate(flops=1, bytes_accessed=1, transcendentals=0)
LIMIT = 24 * 1024 * 1024


def whole(space=VMEM):
    return pl.BlockSpec(memory_space=space)


def split_sum(total, offset):
    high = total.astype(BF16).astype(F32)
    low = total - high
    lane = lax.broadcasted_iota(jnp.int32, (total.shape[0], LANES), 1)
    return jnp.where(lane == offset, high, jnp.where(lane == offset + 1, low, 0.0)).astype(BF16)


def row_copies(hidden, blocks, rows_in, sem):
    stripes, _, page_len, _ = hidden.shape
    return [
        pltpu.make_async_copy(
            hidden.at[stripe, block],
            rows_in.at[pl.ds((place * stripes + stripe) * page_len, page_len)],
            sem.at[place * stripes + stripe],
        )
        for place, block in enumerate(blocks)
        for stripe in range(stripes)
    ]


def scale_rows(rows_in, gained, gain_in, span):
    wide_gain = gain_in[...].astype(F32).reshape(1, gain_in.shape[0])
    gained[span] = (rows_in[span].astype(F32) * wide_gain).astype(BF16)


def put_squares(rows_in, span, out, columns, offset):
    squares = jnp.zeros((out.shape[0], LANES), F32)
    for lane in range(rows_in.shape[1] // LANES):
        part = rows_in[span, lane * LANES : (lane + 1) * LANES].astype(F32)
        squares = squares + part * part
    total = jnp.sum(squares, axis=1, keepdims=True)
    out[:, columns] = split_sum(total, offset)


def is_inner(shard):
    return (shard == 1) | (shard == 2)


def far_blocks(shard):
    lower = shard < 2
    return jnp.where(lower, 2, 1), jnp.where(lower, 3, 0)


def first_kernel(hidden, gain, weight, out, gained, tile, rows_in, gain_in, row_sem, gain_sem, tile_sem):
    shard = lax.axis_index("shard")
    half = weight.shape[1] // 2
    inner_block, outer_block = far_blocks(shard)
    rows_here = row_copies(hidden, [jnp.where(is_inner(shard), outer_block, inner_block)], rows_in, row_sem)
    tile_copy = pltpu.make_async_copy(weight.at[:, pl.ds(0, half)], tile, tile_sem)
    gain_copy = pltpu.make_async_copy(gain, gain_in, gain_sem)
    gain_copy.start()
    for copy in rows_here:
        copy.start()
    tile_copy.start()
    gain_copy.wait()
    for copy in rows_here:
        copy.wait()
    scale_rows(rows_in, gained, gain_in, slice(None))
    put_squares(rows_in, slice(None), out, slice(half, half + LANES), 0)
    tile_copy.wait()
    out[:, :half] = jnp.dot(gained[...], tile[...], preferred_element_type=F32).astype(BF16)


def project_first(hidden, gain, weight):
    stripes, blocks, page_len, features = hidden.shape
    half = weight.shape[1] // 2
    rows = stripes * page_len
    return pl.pallas_call(
        first_kernel,
        in_specs=[whole(pl.ANY)] * 3,
        out_specs=[whole()] * 3,
        out_shape=[
            jax.ShapeDtypeStruct((rows, half + LANES), BF16),
            jax.ShapeDtypeStruct((rows, features), BF16),
            jax.ShapeDtypeStruct((features, half), BF16),
        ],
        scratch_shapes=[
            pltpu.VMEM((rows, features), BF16),
            pltpu.VMEM((features,), BF16),
            pltpu.SemaphoreType.DMA((stripes,)),
            pltpu.SemaphoreType.DMA,
            pltpu.SemaphoreType.DMA,
        ],
        compiler_params=pltpu.CompilerParams(vmem_limit_bytes=LIMIT),
        cost_estimate=SMALL,
        name="project_first",
    )(hidden, gain, weight)


def head_spread(query, width):
    heads = query.shape[0]
    group = heads // (width // LANES)
    head = lax.broadcasted_iota(jnp.int32, (heads, LANES), 0)
    pieces = [jnp.where(head // group == g, query, jnp.zeros_like(query)) for g in range(width // LANES)]
    return jnp.concatenate(pieces, axis=1)


def head_pick(products):
    heads, width = products.shape
    group = heads // (width // LANES)
    head = lax.broadcasted_iota(jnp.int32, (heads, LANES), 0)
    picked = products[:, :LANES]
    for g in range(1, width // LANES):
        picked = jnp.where(head // group == g, products[:, g * LANES : (g + 1) * LANES], picked)
    return picked


def score(query, key_rows):
    spread = head_spread(query, key_rows.shape[1])
    scores = lax.dot_general(spread, key_rows, (((1,), (1,)), ((), ())), preferred_element_type=F32)
    return scores * (1.0 / math.sqrt(LANES))


def attend(query, key_rows, value_rows, usable):
    scores = jnp.where(usable, score(query, key_rows), FLOOR_SCORE)
    largest = jnp.max(scores, axis=1, keepdims=True)
    weights = jnp.where(usable, jnp.exp(scores - largest), 0.0)
    total = jnp.sum(weights, axis=1, keepdims=True)
    picked = head_pick(jnp.dot(weights.astype(BF16), value_rows, preferred_element_type=F32))
    some = total > 0.0
    safe = jnp.where(some, total, 1.0)
    return picked / safe, jnp.where(some, largest + jnp.log(safe), FLOOR_SCORE)


def split_lines(lines, first):
    high = lines.astype(BF16).astype(F32)
    middle_part = (lines - high).astype(BF16).astype(F32)
    low = lines - high - middle_part
    place = lax.broadcasted_iota(jnp.int32, lines.shape, 0) - first
    return jnp.where(place == 0, high, jnp.where(place == 1, middle_part, jnp.where(place == 2, low, 0.0)))


def join_lines(tail, first, rows):
    line = jnp.sum(tail[first : first + 3].astype(F32), axis=0, keepdims=True)
    return jnp.broadcast_to(line, (LANES, LANES)).T[:rows]


def project_keys_kernel(hidden, gain, weight, sent, key_tile, *rest):
    own, near, third, values, gained, value_tile = rest[:6]
    rows_in, gain_in, row_sem, gain_sem, tile_sem = rest[6:]
    shard = lax.axis_index("shard")
    rows = own.shape[0]
    half = weight.shape[1] // 2
    inner_block, outer_block = far_blocks(shard)
    blocks = [shard, jnp.bitwise_xor(shard, 1), jnp.where(is_inner(shard), inner_block, outer_block)]
    rows_here = row_copies(hidden, blocks, rows_in, row_sem)
    tile_copy = pltpu.make_async_copy(weight.at[:, pl.ds(half, half)], value_tile, tile_sem)
    gain_copy = pltpu.make_async_copy(gain, gain_in, gain_sem)
    gain_copy.start()
    for copy in rows_here + [tile_copy]:
        copy.start()
    gain_copy.wait()
    for copy in rows_here:
        copy.wait()
    scale_rows(rows_in, gained, gain_in, slice(None))
    for place, ref in enumerate((own, near, third)):
        span = slice(place * rows, (place + 1) * rows)
        put_squares(rows_in, span, ref, slice(half, half + LANES), 2 if place == 2 else 0)
    product = jnp.dot(gained[...], key_tile[...], preferred_element_type=F32).astype(BF16)
    for place, ref in enumerate((own, near, third)):
        ref[:, :half] = product[place * rows : (place + 1) * rows]
    tile_copy.wait()
    values[...] = jnp.dot(sent[...], value_tile[...], preferred_element_type=F32).astype(BF16)


def project_keys(hidden, gain, weight, sent, tile):
    stripes, blocks, page_len, features = hidden.shape
    half = weight.shape[1] // 2
    rows = stripes * page_len
    return pl.pallas_call(
        project_keys_kernel,
        in_specs=[whole(pl.ANY)] * 3 + [whole()] * 2,
        out_specs=[whole()] * 6,
        out_shape=[jax.ShapeDtypeStruct((rows, half + LANES), BF16)] * 3
        + [
            jax.ShapeDtypeStruct((rows, half), BF16),
            jax.ShapeDtypeStruct((3 * rows, features), BF16),
            jax.ShapeDtypeStruct((features, half), BF16),
        ],
        scratch_shapes=[
            pltpu.VMEM((3 * rows, features), BF16),
            pltpu.VMEM((features,), BF16),
            pltpu.SemaphoreType.DMA((3 * stripes,)),
            pltpu.SemaphoreType.DMA,
            pltpu.SemaphoreType.DMA,
        ],
        compiler_params=pltpu.CompilerParams(vmem_limit_bytes=LIMIT),
        cost_estimate=SMALL,
        name="project_keys",
    )(hidden, gain, weight, sent, tile)


def project_values_kernel(gained, tile, *rest):
    product = jnp.dot(gained[...], tile[...], preferred_element_type=F32).astype(BF16)
    rows = rest[-1].shape[0]
    for place, ref in enumerate(rest[-3:]):
        ref[...] = product[place * rows : (place + 1) * rows]


def project_values(gained, tile, after):
    return pl.pallas_call(
        project_values_kernel,
        in_specs=[whole()] * 2 + [whole(pl.ANY)] * len(after),
        out_specs=[whole()] * 3,
        out_shape=[jax.ShapeDtypeStruct((gained.shape[0] // 3, tile.shape[1]), BF16)] * 3,
        compiler_params=pltpu.CompilerParams(vmem_limit_bytes=LIMIT),
        cost_estimate=SMALL,
        name="project_values",
    )(gained, tile, *after)


def carry_kernel(mine, first, *rest):
    inner = is_inner(lax.axis_index("shard"))
    arrived = jnp.where(inner, first[...].astype(F32), 0.0)
    rest[-1][...] = (mine[...].astype(F32) + arrived).astype(BF16)


def carry(mine, first, after):
    return pl.pallas_call(
        carry_kernel,
        in_specs=[whole(), whole()] + [whole(pl.ANY)] * len(after),
        out_specs=whole(),
        out_shape=jax.ShapeDtypeStruct(mine.shape, BF16),
        compiler_params=pltpu.CompilerParams(vmem_limit_bytes=LIMIT),
        cost_estimate=SMALL,
        name="carry",
    )(mine, first, *after)


def rep_shapes(rows, width):
    return [jax.ShapeDtypeStruct((rows, width), BF16)] * 4


def ask_kernel(jobs, query, *rest):
    for step, out in enumerate(rest[-4:]):
        out[...] = query[job_from(jobs, step)[1]]


def ask(jobs, query, after):
    return pl.pallas_call(
        ask_kernel,
        in_specs=[whole(SMEM), whole()] + [whole(pl.ANY)] * len(after),
        out_specs=[whole()] * 4,
        out_shape=rep_shapes(*query.shape[1:]),
        compiler_params=pltpu.CompilerParams(vmem_limit_bytes=LIMIT),
        cost_estimate=SMALL,
        name="ask",
    )(jobs, query, *after)


def kept_kernel(jobs, table, lengths, query, pool, *rest, shards, after):
    outs = rest[after : after + 4]
    new_pool, pages, total, level, in_sem, out_sem = rest[after + 4 :]
    slots, heads, _ = query.shape
    here = heads // shards
    rows = slots * here
    replica = lax.axis_index("rep")
    shard = lax.axis_index("shard")
    page_len = pool.shape[1]
    half = pool.shape[2] // 2

    def copy_in(context, page):
        place = context * 2 + page
        return pltpu.make_async_copy(pool.at[table[page, context]], pages.at[place], in_sem.at[place])

    def copy_out(context, page):
        place = context * 2 + page
        return pltpu.make_async_copy(pages.at[place], new_pool.at[table[page, context]], out_sem.at[place])

    @pl.loop(0, slots)
    def _(context):
        for page in range(2):
            copy_in(context, page).start()

    lane = lax.broadcasted_iota(jnp.int32, (heads, 2 * page_len), 1)
    page_of = lane // page_len
    position = (page_of * shards + shard) * page_len + lane % page_len

    def context_part(context):
        gone = [jnp.int32(0), jnp.int32(0)]
        for job in range(jobs.shape[1]):
            hit = (jobs[0, job] == replica) & (jobs[1, job] == context)
            for page in range(2):
                gone[page] = gone[page] | (hit & (jobs[2, job] == page)).astype(jnp.int32)
        usable = (position < lengths[context]) & (jnp.where(page_of == 0, gone[0], gone[1]) == 0)
        both = pages[pl.ds(context * 2, 2)].reshape(2 * page_len, 2 * half)
        return attend(query[context], both[:, :half], both[:, half:], usable)

    @pl.loop(0, slots // GROUP)
    def _(index):
        contexts = [index * GROUP + member for member in range(GROUP)]
        for context in contexts:
            for page in range(2):
                copy_in(context, page).wait()
                copy_out(context, page).start()
        results = [context_part(context) for context in contexts]
        for context, (result, logarithm) in zip(contexts, results):
            total[context] = result
            level[context] = jnp.broadcast_to(logarithm, result.shape)

    for step, out in enumerate(outs):
        start = pl.multiple_of(jnp.bitwise_xor(shard, step) * here, here)
        out[:rows] = total[:, pl.ds(start, here), :].reshape(rows, LANES).astype(BF16)
        lines = level[:, pl.ds(start, here), :].reshape(rows, LANES).T[:16]
        out[rows:] = split_lines(lines, 0).astype(BF16)

    @pl.loop(0, slots)
    def _(context):
        for page in range(2):
            copy_out(context, page).wait()


def kept(jobs, table, lengths, query, pool, after, shards):
    slots, heads, size = query.shape
    return pl.pallas_call(
        functools.partial(kept_kernel, shards=shards, after=len(after)),
        in_specs=[whole(SMEM)] * 3 + [whole()] + [whole(pl.ANY)] * (1 + len(after)),
        out_specs=[whole()] * 4 + [whole(pl.ANY)],
        out_shape=[jax.ShapeDtypeStruct((slots * heads // shards + 16, size), BF16)] * 4
        + [jax.ShapeDtypeStruct(pool.shape, pool.dtype)],
        scratch_shapes=[
            pltpu.VMEM((slots * 2,) + pool.shape[1:], pool.dtype),
            pltpu.VMEM(query.shape, F32),
            pltpu.VMEM(query.shape, F32),
            pltpu.SemaphoreType.DMA((slots * 2,)),
            pltpu.SemaphoreType.DMA((slots * 2,)),
        ],
        compiler_params=pltpu.CompilerParams(vmem_limit_bytes=LIMIT),
        cost_estimate=SMALL,
        name="kept",
    )(jobs, table, lengths, query, pool, *after)


def route(jobs, finished, outs):
    replica = lax.axis_index("rep")
    page_len = finished.shape[0] // SENDS
    for step, out in enumerate(outs):
        chosen = jobs[0, replica * SENDS] == jnp.bitwise_xor(replica, step)

        @pl.when(chosen)
        def _():
            out[...] = finished[:page_len]

        @pl.when(jnp.logical_not(chosen))
        def _():
            out[...] = finished[page_len:]


def add_parts(own, near, first, third, columns):
    direct = jnp.where(is_inner(lax.axis_index("shard")), 0.0, first[:, columns].astype(F32))
    return (own[:, columns].astype(F32) + near[:, columns].astype(F32)) + (third[:, columns].astype(F32) + direct)


def finish_keys_kernel(jobs, own, near, first, third, frequency, *rest, stripe):
    asked, outs = rest[:4], rest[4:8]
    scale, weights_out, share, level, finished = rest[8:]
    replica = lax.axis_index("rep")
    shard = lax.axis_index("shard")
    rows = own.shape[0]
    page_len = rows // SENDS
    width = own.shape[1] - LANES

    def added(columns):
        return add_parts(own, near, first, third, columns)

    squares = jnp.sum(added(slice(width, width + LANES)), axis=1, keepdims=True)
    inverse = jnp.broadcast_to(lax.rsqrt(squares / D + EPS), (rows, LANES))
    scale[...] = inverse
    row = lax.broadcasted_iota(jnp.int32, (rows, LANES), 0)
    lane = lax.broadcasted_iota(jnp.int32, (rows, LANES), 1)
    index = jnp.where(row < page_len, jobs[2, replica * SENDS], jobs[2, replica * SENDS + 1])
    position = index * stripe + shard * page_len + row % page_len
    angle = position.astype(F32) * frequency[...]
    cosine = jnp.cos(angle) * inverse
    sine_part = jnp.where(lane < LANES // 2, -jnp.sin(angle), jnp.sin(angle)) * inverse
    for head in range(width // LANES):
        columns = slice(head * LANES, (head + 1) * LANES)
        value = added(columns)
        turned = value * cosine + pltpu.roll(value, LANES // 2, 1) * sine_part
        finished[:, columns] = turned.astype(BF16)
    route(jobs, finished, outs)
    for send in range(SENDS):
        step = jnp.bitwise_xor(jobs[0, replica * SENDS + send], replica)
        query = asked[0][...]
        for other in range(1, 4):
            query = jnp.where(step == other, asked[other][...], query)
        scores = score(query, finished[send * page_len : (send + 1) * page_len])
        largest = jnp.max(scores, axis=1, keepdims=True)
        weights = jnp.exp(scores - largest)
        total = jnp.sum(weights, axis=1, keepdims=True)
        weights_out[send] = weights.astype(BF16)
        share[send] = jnp.broadcast_to(1.0 / total, share.shape[1:])
        level[send] = jnp.broadcast_to(largest + jnp.log(total), level.shape[1:])


def finish_values_kernel(jobs, own, near, first, third, scale, weights, share, level, *rest, shards, after):
    kept_parts, outs = rest[:4], rest[4 + after : 8 + after]
    packed, finished, result = rest[8 + after : 12 + after], rest[12 + after], rest[13 + after]
    shard = lax.axis_index("shard")
    for head in range(own.shape[1] // LANES):
        columns = slice(head * LANES, (head + 1) * LANES)
        total = add_parts(own, near, first, third, columns)
        finished[:, columns] = (total * scale[...]).astype(BF16)
    route(jobs, finished, outs)
    page_len = own.shape[0] // SENDS
    for send in range(SENDS):
        products = jnp.dot(
            weights[send], finished[send * page_len : (send + 1) * page_len], preferred_element_type=F32
        )
        result[send] = head_pick(products) * share[send]
    here = level.shape[1] // shards
    count = SENDS * here
    rows = kept_parts[0].shape[0] - 16
    for step in range(4):
        start = pl.multiple_of(jnp.bitwise_xor(shard, step) * here, here)
        packed[step][:rows] = kept_parts[step][:rows]
        packed[step][rows : rows + count] = result[:, pl.ds(start, here), :].reshape(count, LANES).astype(BF16)
        mine = level[:, pl.ds(start, here), :].reshape(count, LANES)
        lines = jnp.concatenate([mine] + [jnp.zeros((LANES - count, LANES), F32)], axis=0).T[:16]
        tail = kept_parts[step][rows:].astype(F32) + split_lines(lines, 3)
        packed[step][rows + count :] = tail.astype(BF16)


def finish_keys(jobs, parts, frequency, asked, stripe):
    rows = parts[0].shape[0]
    width = parts[0].shape[1] - LANES
    heads = asked[0].shape[0]
    page_len = rows // SENDS
    return pl.pallas_call(
        functools.partial(finish_keys_kernel, stripe=stripe),
        in_specs=[whole(SMEM)] + [whole()] * 9,
        out_specs=[whole()] * 8,
        out_shape=rep_shapes(page_len, width)
        + [
            jax.ShapeDtypeStruct((rows, LANES), F32),
            jax.ShapeDtypeStruct((SENDS, heads, page_len), BF16),
            jax.ShapeDtypeStruct((SENDS, heads, LANES), F32),
            jax.ShapeDtypeStruct((SENDS, heads, LANES), F32),
        ],
        scratch_shapes=[pltpu.VMEM((rows, width), BF16)],
        compiler_params=pltpu.CompilerParams(vmem_limit_bytes=LIMIT),
        cost_estimate=SMALL,
        name="finish_keys",
    )(jobs, *parts, frequency, *asked)


def finish_values(jobs, parts, scale, weights, share, level, kept_parts, after, shards):
    rows, width = parts[0].shape
    heads = level.shape[1]
    page_len = rows // SENDS
    packed = kept_parts[0].shape[0] + SENDS * heads // shards
    return pl.pallas_call(
        functools.partial(finish_values_kernel, shards=shards, after=len(after)),
        in_specs=[whole(SMEM)] + [whole()] * 12 + [whole(pl.ANY)] * len(after),
        out_specs=[whole()] * 8,
        out_shape=rep_shapes(page_len, width) + [jax.ShapeDtypeStruct((packed, LANES), BF16)] * 4,
        scratch_shapes=[pltpu.VMEM((rows, width), BF16), pltpu.VMEM((SENDS, heads, LANES), F32)],
        compiler_params=pltpu.CompilerParams(vmem_limit_bytes=LIMIT),
        cost_estimate=SMALL,
        name="finish_values",
    )(jobs, *parts, scale, weights, share, level, *kept_parts, *after)


def job_from(jobs, step):
    replica = lax.axis_index("rep")
    first = jnp.bitwise_xor(replica, step) * SENDS
    hit_first = jobs[0, first] == replica
    hit = hit_first | (jobs[0, first + 1] == replica)
    row = jnp.where(hit_first, first, first + 1)
    return hit, jobs[1, row], jobs[2, row]


def place_kernel(jobs, table, pool, *rest):
    key_pages, value_pages = rest[:4], rest[4:8]
    out, done, pages, sem = rest[8:]
    half = rest[0].shape[1]
    done[...] = jnp.zeros_like(done)
    for wait in (False, True):
        for step in range(4):
            hit, context, page = job_from(jobs, step)

            @pl.when(hit)
            def _():
                slot = table[page, context]
                copy = pltpu.make_async_copy(pages.at[step], out.at[slot], sem.at[step])
                if wait:
                    copy.wait()
                else:
                    pages[step, :, :half] = key_pages[step][...]
                    pages[step, :, half:] = value_pages[step][...]
                    copy.start()


def place_pages(jobs, table, pool, key_pages, value_pages):
    return pl.pallas_call(
        place_kernel,
        in_specs=[whole(SMEM)] * 2 + [whole(pl.ANY)] + [whole()] * 8,
        out_specs=[whole(pl.ANY), whole()],
        out_shape=[jax.ShapeDtypeStruct(pool.shape, pool.dtype), jax.ShapeDtypeStruct((16, LANES), BF16)],
        scratch_shapes=[pltpu.VMEM((4,) + pool.shape[1:], pool.dtype), pltpu.SemaphoreType.DMA((4,))],
        input_output_aliases={2: 0},
        compiler_params=pltpu.CompilerParams(vmem_limit_bytes=LIMIT),
        cost_estimate=SMALL,
        name="place_pages",
    )(jobs, table, pool, *key_pages, *value_pages)


def blend(parts, levels):
    top = functools.reduce(jnp.maximum, levels)
    shares = [jnp.exp(level - top) for level in levels]
    both = functools.reduce(jnp.add, shares)
    total = functools.reduce(jnp.add, [part * share for part, share in zip(parts, shares)])
    return total / both, top + jnp.log(both)


def gather_kernel(jobs, *refs, rows, count):
    parts, page, outs, page_out = refs[:4], refs[4], refs[5:9], refs[9]
    page_out[...] = page[...]
    mixed, level = blend(
        [ref[rows : rows + count].astype(F32) for ref in parts],
        [join_lines(ref[rows + count :], 3, count) for ref in parts],
    )
    here = count // SENDS
    replica = lax.axis_index("rep")
    lane = lax.broadcasted_iota(jnp.int32, (here, LANES), 1)
    for step, out in enumerate(outs):
        chosen = jobs[0, replica * SENDS] == jnp.bitwise_xor(replica, step)
        total = jnp.where(chosen, level[:here], level[here:])
        high = total.astype(BF16).astype(F32)
        middle_part = (total - high).astype(BF16).astype(F32)
        low = total - high - middle_part
        out[:, :LANES] = jnp.where(chosen, mixed[:here], mixed[here:]).astype(BF16)
        out[:, LANES:] = jnp.where(
            lane == 0, high, jnp.where(lane == 1, middle_part, jnp.where(lane == 2, low, 0.0))
        ).astype(BF16)


def gather_parts(jobs, parts, page, rows, count):
    return pl.pallas_call(
        functools.partial(gather_kernel, rows=rows, count=count),
        in_specs=[whole(SMEM)] + [whole()] * 5,
        out_specs=[whole()] * 5,
        out_shape=rep_shapes(count // SENDS, 2 * LANES) + [jax.ShapeDtypeStruct(page.shape, BF16)],
        compiler_params=pltpu.CompilerParams(vmem_limit_bytes=LIMIT),
        cost_estimate=SMALL,
        name="gather_parts",
    )(jobs, *parts, page)


def blend_kernel(*refs, rows, count):
    parts, after, kept_out, kept_level = refs[:4], refs[4], refs[5], refs[6]
    mixed, level = blend(
        [ref[:rows].astype(F32) for ref in parts], [join_lines(ref[rows + count :], 0, rows) for ref in parts]
    )
    kept_out[...] = mixed
    kept_level[...] = level


def blend_kept(parts, after, rows, count):
    return pl.pallas_call(
        functools.partial(blend_kernel, rows=rows, count=count),
        in_specs=[whole()] * 4 + [whole(pl.ANY)],
        out_specs=[whole()] * 2,
        out_shape=[jax.ShapeDtypeStruct((rows, LANES), F32)] * 2,
        compiler_params=pltpu.CompilerParams(vmem_limit_bytes=LIMIT),
        cost_estimate=SMALL,
        name="blend_kept",
    )(*parts, after)


def combine_kernel(jobs, kept_out, kept_level, *refs):
    parts, out, mixed = refs[:4], refs[5], refs[6]
    slots, here, size = mixed.shape
    mixed[...] = kept_out[...].reshape(mixed.shape)
    for step, ref in enumerate(parts):
        hit, context, _ = job_from(jobs, step)

        @pl.when(hit)
        def _():
            fresh_level = jnp.sum(ref[:, LANES:].astype(F32), axis=1, keepdims=True)
            fresh_level = jnp.broadcast_to(fresh_level, (here, LANES))
            old_level = kept_level[pl.ds(pl.multiple_of(context * here, here), here)]
            blended, _ = blend([mixed[context], ref[:, :LANES].astype(F32)], [old_level, fresh_level])
            mixed[context] = blended

    for head in range(here):
        out[:, head * size : (head + 1) * size] = mixed[:, head, :].astype(BF16)


def combine(jobs, kept_out, kept_level, parts, after, slots):
    here = kept_out.shape[0] // slots
    return pl.pallas_call(
        combine_kernel,
        in_specs=[whole(SMEM)] + [whole()] * 6 + [whole(pl.ANY)],
        out_specs=whole(),
        out_shape=jax.ShapeDtypeStruct((slots, here * LANES), BF16),
        scratch_shapes=[pltpu.VMEM((slots, here, LANES), F32)],
        compiler_params=pltpu.CompilerParams(vmem_limit_bytes=LIMIT),
        cost_estimate=SMALL,
        name="combine",
    )(jobs, kept_out, kept_level, *parts, after)


def on_device(
    hidden, norm_gain, kv_weight, restore_jobs, page_table, context_lengths, queries, kv_pool
):
    shards = lax.axis_size("shard")
    replicas = lax.axis_size("rep")
    stripe = hidden.shape[0] // SENDS
    page_len = stripe // shards
    kv_weight = pltpu.with_memory_space_constraint(kv_weight, pltpu.HBM)
    kv_pool = pltpu.with_memory_space_constraint(kv_pool, pltpu.HBM)
    gain = pltpu.with_memory_space_constraint(norm_gain, pltpu.HBM)
    blocks = pltpu.with_memory_space_constraint(
        hidden.reshape(SENDS, shards, page_len, hidden.shape[1]), pltpu.HBM
    )
    jobs = restore_jobs.T
    table = page_table[:, :, 0].T
    slots = queries.shape[0]
    query = queries.reshape(slots, QH, HD)

    def along(array, pairs):
        return lax.ppermute(array, "shard", pairs)

    def across(array, step):
        return lax.ppermute(array, "rep", [(i, i ^ step) for i in range(replicas)])

    def between(arrays):
        return [arrays[0]] + [across(arrays[step], step) for step in range(1, replicas)]

    key_sent, gained_sent, key_tile = project_first(blocks, gain, kv_weight)
    key_first = along(key_sent, FIRST)
    key_0, key_1, key_2, value_sent, gained, tile = project_keys(
        blocks, gain, kv_weight, gained_sent, key_tile
    )
    value_first = along(value_sent, FIRST)
    key_near = along(key_1, NEAR)
    key_2 = carry(key_2, key_first, [])
    key_third = along(key_2, THIRD)
    *kept_parts, new_pool = kept(jobs, table, context_lengths, query, kv_pool, [key_2], shards)
    asked = between(ask(jobs, query, [value_first, kept_parts[0]]))
    value_0, value_1, value_2 = project_values(gained, tile, asked[1:])
    value_near = along(value_1, NEAR)
    value_third = along(carry(value_2, value_first, []), THIRD)
    frequency = THETA ** (-(jnp.arange(HD // 2, dtype=F32) * 2.0 / HD))
    frequency = jnp.concatenate([frequency, frequency])[None, :]
    *key_out, scale, weights, share, level = finish_keys(
        jobs, (key_0, key_near, key_first, key_third), frequency, asked, stripe
    )
    key_pages = between(key_out)
    finished = finish_values(
        jobs,
        (value_0, value_near, value_first, value_third),
        scale,
        weights,
        share,
        level,
        kept_parts,
        key_pages[1:],
        shards,
    )
    value_pages = [finished[0], None, across(finished[2], 2), across(finished[3], 3)]
    packed = finished[4:]
    parts = [packed[0]] + [
        along(packed[step], [(i, i ^ step) for i in range(shards)]) for step in range(1, shards)
    ]
    here = QH // shards
    *gathered, near_page = gather_parts(jobs, parts, finished[1], slots * here, SENDS * here)
    fresh = between(gathered)
    value_pages[1] = across(near_page, 1)
    kept_out, kept_level = blend_kept(parts, gathered[0], slots * here, SENDS * here)
    new_pool, placed = place_pages(jobs, table, new_pool, key_pages, value_pages)
    return (new_pool, combine(jobs, kept_out, kept_level, fresh, placed, slots))


def solution(mesh):
    in_specs = (
        P(("outer", "rep"), "shard"),
        P("shard"),
        P("shard", None),
        P("outer", None),
        P(("outer", "rep"), None, "shard"),
        P(("outer", "rep")),
        P(("outer", "rep"), None),
        P(("outer", "rep", "shard"), None, None),
    )
    out_specs = (P(("outer", "rep", "shard"), None, None), P(("outer", "rep"), "shard"))
    fast = mesh.shape["shard"] == 4 and mesh.shape["rep"] == 4
    return jax.shard_map(
        on_device if fast else on_device_general, mesh=mesh, in_specs=in_specs, out_specs=out_specs, check_vma=False
    )
```

```python
import functools
import math

import jax
import jax.numpy as jnp
from jax import lax
from jax.experimental import pallas as pl
from jax.experimental.pallas import tpu as pltpu
from jax.sharding import PartitionSpec as P

D = 8192
QH = 64
KVH = 8
HD = 128
SENDS = 2


THETA = 500000.0
EPS = 1e-05
FLOOR_SCORE = -1e30


def rotate(key_rows, positions):
    half_dim = key_rows.shape[-1] // 2
    frequency = THETA ** (-(jnp.arange(half_dim, dtype=jnp.float32) * 2.0 / key_rows.shape[-1]))
    angles = positions.astype(jnp.float32)[:, None] * frequency[None, :]
    cosine = jnp.cos(angles)[:, None, :]
    sine_part = jnp.sin(angles)[:, None, :]
    first_half = key_rows[..., :half_dim]
    second = key_rows[..., half_dim:]
    return jnp.concatenate(
        [first_half * cosine - second * sine_part, second * cosine + first_half * sine_part],
        axis=-1,
    )


def finish(projected, inverse, positions):
    row_count = projected.shape[0]
    half_width = projected.shape[1] // 2
    scaled = projected * inverse[:, None]
    key_rows = rotate(scaled[:, :half_width].reshape(row_count, KVH, HD), positions).reshape(
        row_count, half_width
    )
    return jnp.concatenate([key_rows, scaled[:, half_width:]], axis=1).astype(jnp.bfloat16)


def spread_out(pieces, targets, replicas):
    outgoing = jnp.zeros((replicas,) + pieces.shape[1:], pieces.dtype)
    for send_index in range(SENDS):
        hit = (jnp.arange(replicas, dtype=jnp.int32) == targets[send_index])[:, None, None]
        outgoing = jnp.where(hit, pieces[send_index][None], outgoing)
    return outgoing


def on_device_general(
    hidden, norm_gain, kv_weight, restore_jobs, page_table, context_lengths, queries, kv_pool
):
    shards = lax.axis_size("shard")
    replicas = lax.axis_size("rep")
    my_replica = lax.axis_index("rep")
    my_shard = lax.axis_index("shard")
    stripe = hidden.shape[0] // SENDS
    page_len = stripe // shards
    features = hidden.shape[1]
    kv_width = kv_weight.shape[1]
    pool_pages = kv_pool.shape[0]
    destination = restore_jobs[:, 0]
    context = restore_jobs[:, 1]
    stripe_index = restore_jobs[:, 2]
    my_targets = lax.dynamic_slice_in_dim(destination, my_replica * SENDS, SENDS, 0)
    is_mine = destination == my_replica
    gain_wide = norm_gain.astype(jnp.float32)[None, :]
    page_rows = jnp.arange(page_len, dtype=jnp.int32)
    wide = hidden.astype(jnp.float32)
    squares = lax.psum(jnp.sum(wide * wide, axis=1), "shard")
    inverse = lax.rsqrt(squares / D + EPS)
    gained = (wide * gain_wide).astype(jnp.bfloat16)
    arranged = gained.reshape(SENDS, shards, page_len, features).transpose(1, 0, 2, 3)
    arranged = arranged.reshape(shards * SENDS * page_len, features)
    owned = lax.psum_scatter(
        jnp.dot(arranged, kv_weight, preferred_element_type=jnp.float32).astype(jnp.bfloat16),
        "shard",
        scatter_dimension=0,
        tiled=True,
    ).astype(jnp.float32)
    owned_inverse = lax.dynamic_slice_in_dim(
        inverse.reshape(SENDS, stripe), my_shard * page_len, page_len, 1
    )
    my_stripes = lax.dynamic_slice_in_dim(stripe_index, my_replica * SENDS, SENDS, 0)
    positions = my_stripes[:, None] * stripe + my_shard * page_len + page_rows[None, :]
    finished = finish(owned, owned_inverse.reshape(-1), positions.reshape(-1)).reshape(
        SENDS, page_len, kv_width
    )
    outgoing = spread_out(finished, my_targets, replicas)
    arrived = lax.all_to_all(outgoing, "rep", split_axis=0, concat_axis=0, tiled=True)
    mine_grid = is_mine.reshape(replicas, SENDS)
    has_page = jnp.any(mine_grid, axis=1)
    which = jnp.argmax(mine_grid.astype(jnp.int32), axis=1)
    job_index = jnp.arange(replicas, dtype=jnp.int32) * SENDS + which
    physical = jnp.where(
        has_page, page_table[context[job_index], stripe_index[job_index], 0], pool_pages
    )
    new_pool = kv_pool.at[physical].set(arrived, mode="drop")
    slots = queries.shape[0]
    pages_dev = page_table.shape[1]
    group = QH // KVH
    scale = 1.0 / math.sqrt(HD)
    cached = new_pool[page_table[:, :, 0]]
    key_rows = cached[..., : KVH * HD].reshape(slots, pages_dev * page_len, KVH, HD)
    value_rows = cached[..., KVH * HD :].reshape(slots, pages_dev * page_len, KVH, HD)
    query_rows = queries.reshape(slots, KVH, group, HD)
    scores = (
        jnp.einsum("cgmd,cpgd->cgmp", query_rows, key_rows, preferred_element_type=jnp.float32)
        * scale
    )
    position = (
        (jnp.arange(pages_dev, dtype=jnp.int32)[:, None] * shards + my_shard) * page_len
        + page_rows[None, :]
    ).reshape(-1)
    usable = (position[None, :] < context_lengths[:, None])[:, None, None, :]
    local_max = jnp.max(jnp.where(usable, scores, FLOOR_SCORE), axis=-1)
    weights = jnp.where(usable, jnp.exp(scores - local_max[..., None]), 0.0)
    denominator = jnp.sum(weights, axis=-1).reshape(slots, QH)
    numerator = jnp.einsum(
        "cgmp,cpgd->cgmd",
        weights.astype(jnp.bfloat16),
        value_rows,
        preferred_element_type=jnp.float32,
    )
    numerator = numerator.reshape(slots, QH, HD)
    local_max = local_max.reshape(slots, QH)
    heads_here = QH // shards
    row_max = lax.pmax(local_max, "shard")
    factor = jnp.exp(local_max - row_max)
    scaled_num = (numerator * factor[..., None]).reshape(slots, QH * HD)
    numerator, denominator = (
        lax.psum(scaled_num.astype(jnp.bfloat16), "shard").astype(jnp.float32),
        lax.psum((denominator * factor).astype(jnp.bfloat16), "shard").astype(jnp.float32),
    )
    numerator = lax.dynamic_slice_in_dim(numerator, my_shard * heads_here * HD, heads_here * HD, 1)
    denominator = lax.dynamic_slice_in_dim(denominator, my_shard * heads_here, heads_here, 1)
    numerator = numerator.reshape(slots, heads_here, HD)
    attention_out = numerator / denominator[..., None]
    return (new_pool, attention_out.reshape(slots, heads_here * HD).astype(jnp.bfloat16))


FIRST = [(0, 1), (3, 2), (1, 3), (2, 0)]
NEAR = [(0, 1), (1, 0), (2, 3), (3, 2)]
THIRD = [(0, 3), (3, 0), (1, 2), (2, 1)]
LANES = 128
LINES = 8
GROUP = 2
BF16 = jnp.bfloat16
F32 = jnp.float32
SMEM = pltpu.SMEM
VMEM = pltpu.VMEM
SMALL = pl.CostEstimate(flops=1, bytes_accessed=1, transcendentals=0)
LIMIT = 24 * 1024 * 1024


def whole(space=VMEM):
    return pl.BlockSpec(memory_space=space)


def row_copies(hidden, blocks, rows_in, sem):
    stripes, _, page_len, _ = hidden.shape
    return [
        pltpu.make_async_copy(
            hidden.at[stripe, block],
            rows_in.at[pl.ds((place * stripes + stripe) * page_len, page_len)],
            sem.at[place * stripes + stripe],
        )
        for place, block in enumerate(blocks)
        for stripe in range(stripes)
    ]


def scale_rows(rows_in, gained, gain_in, span):
    wide_gain = gain_in[...].astype(F32).reshape(1, gain_in.shape[0])
    gained[span] = (rows_in[span].astype(F32) * wide_gain).astype(BF16)


def put_squares(rows_in, span, out, first):
    rows = out.shape[0] - LINES
    squares = jnp.zeros((rows, LANES), F32)
    for lane in range(rows_in.shape[1] // LANES):
        part = rows_in[span, lane * LANES : (lane + 1) * LANES].astype(F32)
        squares = squares + part * part
    total = jnp.sum(squares.T, axis=0, keepdims=True)
    high = total.astype(BF16).astype(F32)
    place = lax.broadcasted_iota(jnp.int32, (LINES, LANES), 0) - first
    lines = jnp.where(place == 0, high, jnp.where(place == 1, total - high, 0.0))
    rest = jnp.zeros((LINES, out.shape[1] - LANES), F32)
    out[rows:] = jnp.concatenate([lines, rest], axis=1).astype(BF16)


def is_inner(shard):
    return (shard == 1) | (shard == 2)


def far_blocks(shard):
    lower = shard < 2
    return jnp.where(lower, 2, 1), jnp.where(lower, 3, 0)


def first_kernel(hidden, gain, weight, out, gained, tile, rows_in, gain_in, row_sem, gain_sem, tile_sem):
    shard = lax.axis_index("shard")
    half = weight.shape[1] // 2
    inner_block, outer_block = far_blocks(shard)
    rows_here = row_copies(hidden, [jnp.where(is_inner(shard), outer_block, inner_block)], rows_in, row_sem)
    piece = half // 2
    pieces = [slice(index * piece, (index + 1) * piece) for index in range(2)]
    tile_copies = [
        pltpu.make_async_copy(weight.at[:, columns], tile.at[:, columns], tile_sem.at[index])
        for index, columns in enumerate(pieces)
    ]
    gain_copy = pltpu.make_async_copy(gain, gain_in, gain_sem)
    gain_copy.start()
    for copy in rows_here + tile_copies:
        copy.start()
    gain_copy.wait()
    for copy in rows_here:
        copy.wait()
    scale_rows(rows_in, gained, gain_in, slice(None))
    put_squares(rows_in, slice(None), out, 0)
    for copy, columns in zip(tile_copies, pieces):
        copy.wait()
        product = jnp.dot(gained[...], tile[:, columns], preferred_element_type=F32)
        out[: gained.shape[0], columns] = product.astype(BF16)


def project_first(hidden, gain, weight):
    stripes, blocks, page_len, features = hidden.shape
    half = weight.shape[1] // 2
    rows = stripes * page_len
    return pl.pallas_call(
        first_kernel,
        in_specs=[whole(pl.ANY)] * 3,
        out_specs=[whole()] * 3,
        out_shape=[
            jax.ShapeDtypeStruct((rows + LINES, half), BF16),
            jax.ShapeDtypeStruct((rows, features), BF16),
            jax.ShapeDtypeStruct((features, half), BF16),
        ],
        scratch_shapes=[
            pltpu.VMEM((rows, features), BF16),
            pltpu.VMEM((features,), BF16),
            pltpu.SemaphoreType.DMA((stripes,)),
            pltpu.SemaphoreType.DMA,
            pltpu.SemaphoreType.DMA((2,)),
        ],
        compiler_params=pltpu.CompilerParams(vmem_limit_bytes=LIMIT),
        cost_estimate=SMALL,
        name="project_first",
    )(hidden, gain, weight)


def head_spread(query, width):
    heads = query.shape[0]
    group = heads // (width // LANES)
    head = lax.broadcasted_iota(jnp.int32, (heads, LANES), 0)
    pieces = [jnp.where(head // group == g, query, jnp.zeros_like(query)) for g in range(width // LANES)]
    return jnp.concatenate(pieces, axis=1)


def head_pick(products):
    heads, width = products.shape
    group = heads // (width // LANES)
    head = lax.broadcasted_iota(jnp.int32, (heads, LANES), 0)
    picked = products[:, :LANES]
    for g in range(1, width // LANES):
        picked = jnp.where(head // group == g, products[:, g * LANES : (g + 1) * LANES], picked)
    return picked


def score(query, key_rows):
    spread = head_spread(query, key_rows.shape[1])
    scores = lax.dot_general(spread, key_rows, (((1,), (1,)), ((), ())), preferred_element_type=F32)
    return scores * (1.0 / math.sqrt(LANES))


def attend(query, key_rows, value_rows, usable):
    scores = jnp.where(usable, score(query, key_rows), FLOOR_SCORE)
    largest = jnp.max(scores, axis=1, keepdims=True)
    weights = jnp.where(usable, jnp.exp(scores - largest), 0.0)
    total = jnp.sum(weights, axis=1, keepdims=True)
    picked = head_pick(jnp.dot(weights.astype(BF16), value_rows, preferred_element_type=F32))
    some = total > 0.0
    safe = jnp.where(some, total, 1.0)
    return picked / safe, jnp.where(some, largest + jnp.log(safe), FLOOR_SCORE)


def split_lines(lines, first):
    high = lines.astype(BF16).astype(F32)
    middle_part = (lines - high).astype(BF16).astype(F32)
    low = lines - high - middle_part
    place = lax.broadcasted_iota(jnp.int32, lines.shape, 0) - first
    return jnp.where(place == 0, high, jnp.where(place == 1, middle_part, jnp.where(place == 2, low, 0.0)))


def join_lines(tail, first, rows):
    line = jnp.sum(tail[first : first + 3].astype(F32), axis=0, keepdims=True)
    return jnp.broadcast_to(line, (LANES, LANES)).T[:rows]


def project_keys_kernel(hidden, gain, weight, sent, key_tile, *rest):
    own, near, third, values, gained, value_tile = rest[:6]
    rows_in, gain_in, row_sem, gain_sem, tile_sem = rest[6:]
    shard = lax.axis_index("shard")
    rows = values.shape[0]
    half = weight.shape[1] // 2
    inner_block, outer_block = far_blocks(shard)
    blocks = [shard, jnp.bitwise_xor(shard, 1), jnp.where(is_inner(shard), inner_block, outer_block)]
    rows_here = row_copies(hidden, blocks, rows_in, row_sem)
    tile_copy = pltpu.make_async_copy(weight.at[:, pl.ds(half, half)], value_tile, tile_sem)
    gain_copy = pltpu.make_async_copy(gain, gain_in, gain_sem)
    gain_copy.start()
    for copy in rows_here + [tile_copy]:
        copy.start()
    gain_copy.wait()
    for copy in rows_here:
        copy.wait()
    scale_rows(rows_in, gained, gain_in, slice(None))
    for place, ref in enumerate((own, near, third)):
        span = slice(place * rows, (place + 1) * rows)
        put_squares(rows_in, span, ref, 2 if place == 2 else 0)
    product = jnp.dot(gained[...], key_tile[...], preferred_element_type=F32).astype(BF16)
    for place, ref in enumerate((own, near, third)):
        ref[:rows] = product[place * rows : (place + 1) * rows]
    tile_copy.wait()
    values[...] = jnp.dot(sent[...], value_tile[...], preferred_element_type=F32).astype(BF16)


def project_keys(hidden, gain, weight, sent, tile):
    stripes, blocks, page_len, features = hidden.shape
    half = weight.shape[1] // 2
    rows = stripes * page_len
    return pl.pallas_call(
        project_keys_kernel,
        in_specs=[whole(pl.ANY)] * 3 + [whole()] * 2,
        out_specs=[whole()] * 6,
        out_shape=[jax.ShapeDtypeStruct((rows + LINES, half), BF16)] * 3
        + [
            jax.ShapeDtypeStruct((rows, half), BF16),
            jax.ShapeDtypeStruct((3 * rows, features), BF16),
            jax.ShapeDtypeStruct((features, half), BF16),
        ],
        scratch_shapes=[
            pltpu.VMEM((3 * rows, features), BF16),
            pltpu.VMEM((features,), BF16),
            pltpu.SemaphoreType.DMA((3 * stripes,)),
            pltpu.SemaphoreType.DMA,
            pltpu.SemaphoreType.DMA,
        ],
        compiler_params=pltpu.CompilerParams(vmem_limit_bytes=LIMIT),
        cost_estimate=SMALL,
        name="project_keys",
    )(hidden, gain, weight, sent, tile)


def project_values_kernel(gained, tile, *rest):
    product = jnp.dot(gained[...], tile[...], preferred_element_type=F32).astype(BF16)
    rows = rest[-1].shape[0]
    for place, ref in enumerate(rest[-3:]):
        ref[...] = product[place * rows : (place + 1) * rows]


def project_values(gained, tile, after):
    return pl.pallas_call(
        project_values_kernel,
        in_specs=[whole()] * 2 + [whole(pl.ANY)] * len(after),
        out_specs=[whole()] * 3,
        out_shape=[jax.ShapeDtypeStruct((gained.shape[0] // 3, tile.shape[1]), BF16)] * 3,
        compiler_params=pltpu.CompilerParams(vmem_limit_bytes=LIMIT),
        cost_estimate=SMALL,
        name="project_values",
    )(gained, tile, *after)


def carry_kernel(mine, first, *rest):
    inner = is_inner(lax.axis_index("shard"))
    arrived = jnp.where(inner, first[...].astype(F32), 0.0)
    rest[-1][...] = (mine[...].astype(F32) + arrived).astype(BF16)


def carry(mine, first, after):
    return pl.pallas_call(
        carry_kernel,
        in_specs=[whole(), whole()] + [whole(pl.ANY)] * len(after),
        out_specs=whole(),
        out_shape=jax.ShapeDtypeStruct(mine.shape, BF16),
        compiler_params=pltpu.CompilerParams(vmem_limit_bytes=LIMIT),
        cost_estimate=SMALL,
        name="carry",
    )(mine, first, *after)


def rep_shapes(rows, width):
    return [jax.ShapeDtypeStruct((rows, width), BF16)] * 4


def ask_kernel(jobs, query, *rest):
    for step, out in enumerate(rest[-4:]):
        out[...] = query[job_from(jobs, step)[1]]


def ask(jobs, query, after):
    return pl.pallas_call(
        ask_kernel,
        in_specs=[whole(SMEM), whole()] + [whole(pl.ANY)] * len(after),
        out_specs=[whole()] * 4,
        out_shape=rep_shapes(*query.shape[1:]),
        compiler_params=pltpu.CompilerParams(vmem_limit_bytes=LIMIT),
        cost_estimate=SMALL,
        name="ask",
    )(jobs, query, *after)


def kept_kernel(jobs, table, lengths, query, pool, *rest, shards, after):
    outs = rest[after : after + 4]
    new_pool, pages, total, level, in_sem, out_sem = rest[after + 4 :]
    slots, heads, _ = query.shape
    here = heads // shards
    rows = slots * here
    replica = lax.axis_index("rep")
    shard = lax.axis_index("shard")
    page_len = pool.shape[1]
    half = pool.shape[2] // 2

    def copy_in(context, page):
        place = context * 2 + page
        return pltpu.make_async_copy(pool.at[table[page, context]], pages.at[place], in_sem.at[place])

    def copy_out(context, page):
        place = context * 2 + page
        return pltpu.make_async_copy(pages.at[place], new_pool.at[table[page, context]], out_sem.at[place])

    @pl.loop(0, slots)
    def _(context):
        for page in range(2):
            copy_in(context, page).start()

    lane = lax.broadcasted_iota(jnp.int32, (heads, 2 * page_len), 1)
    page_of = lane // page_len
    position = (page_of * shards + shard) * page_len + lane % page_len

    def context_part(context):
        gone = [jnp.int32(0), jnp.int32(0)]
        for job in range(jobs.shape[1]):
            hit = (jobs[0, job] == replica) & (jobs[1, job] == context)
            for page in range(2):
                gone[page] = gone[page] | (hit & (jobs[2, job] == page)).astype(jnp.int32)
        usable = (position < lengths[context]) & (jnp.where(page_of == 0, gone[0], gone[1]) == 0)
        both = pages[pl.ds(context * 2, 2)].reshape(2 * page_len, 2 * half)
        return attend(query[context], both[:, :half], both[:, half:], usable)

    @pl.loop(0, slots // GROUP)
    def _(index):
        contexts = [index * GROUP + member for member in range(GROUP)]
        for context in contexts:
            for page in range(2):
                copy_in(context, page).wait()
                copy_out(context, page).start()
        results = [context_part(context) for context in contexts]
        for context, (result, logarithm) in zip(contexts, results):
            total[context] = result
            level[context] = jnp.broadcast_to(logarithm, result.shape)

    for step, out in enumerate(outs):
        start = pl.multiple_of(jnp.bitwise_xor(shard, step) * here, here)
        out[:rows] = total[:, pl.ds(start, here), :].reshape(rows, LANES).astype(BF16)
        lines = level[:, pl.ds(start, here), :].reshape(rows, LANES).T[:16]
        out[rows:] = split_lines(lines, 0).astype(BF16)

    @pl.loop(0, slots)
    def _(context):
        for page in range(2):
            copy_out(context, page).wait()


def kept(jobs, table, lengths, query, pool, after, shards):
    slots, heads, size = query.shape
    return pl.pallas_call(
        functools.partial(kept_kernel, shards=shards, after=len(after)),
        in_specs=[whole(SMEM)] * 3 + [whole()] + [whole(pl.ANY)] * (1 + len(after)),
        out_specs=[whole()] * 4 + [whole(pl.ANY)],
        out_shape=[jax.ShapeDtypeStruct((slots * heads // shards + 16, size), BF16)] * 4
        + [jax.ShapeDtypeStruct(pool.shape, pool.dtype)],
        scratch_shapes=[
            pltpu.VMEM((slots * 2,) + pool.shape[1:], pool.dtype),
            pltpu.VMEM(query.shape, F32),
            pltpu.VMEM(query.shape, F32),
            pltpu.SemaphoreType.DMA((slots * 2,)),
            pltpu.SemaphoreType.DMA((slots * 2,)),
        ],
        compiler_params=pltpu.CompilerParams(vmem_limit_bytes=LIMIT),
        cost_estimate=SMALL,
        name="kept",
    )(jobs, table, lengths, query, pool, *after)


def route(jobs, finished, outs):
    replica = lax.axis_index("rep")
    page_len = finished.shape[0] // SENDS
    for step, out in enumerate(outs):
        chosen = jobs[0, replica * SENDS] == jnp.bitwise_xor(replica, step)

        @pl.when(chosen)
        def _():
            out[...] = finished[:page_len]

        @pl.when(jnp.logical_not(chosen))
        def _():
            out[...] = finished[page_len:]


def add_parts(own, near, first, third, rows, columns):
    direct = jnp.where(is_inner(lax.axis_index("shard")), 0.0, first[rows, columns].astype(F32))
    parts = [ref[rows, columns].astype(F32) for ref in (own, near, third)]
    return (parts[0] + parts[1]) + (parts[2] + direct)


def finish_keys_kernel(jobs, own, near, first, third, frequency, *rest, stripe):
    asked, outs = rest[:4], rest[4:8]
    scale, weights_out, share, level, finished = rest[8:]
    replica = lax.axis_index("rep")
    shard = lax.axis_index("shard")
    rows, width = finished.shape
    page_len = rows // SENDS

    def added(span, columns):
        return add_parts(own, near, first, third, span, columns)

    squares = jnp.sum(added(slice(rows, rows + LINES), slice(0, LANES)), axis=0, keepdims=True)
    squares = jnp.broadcast_to(squares, (LANES, LANES)).T[:rows]
    inverse = lax.rsqrt(squares / D + EPS)
    scale[...] = inverse
    row = lax.broadcasted_iota(jnp.int32, (rows, LANES), 0)
    lane = lax.broadcasted_iota(jnp.int32, (rows, LANES), 1)
    index = jnp.where(row < page_len, jobs[2, replica * SENDS], jobs[2, replica * SENDS + 1])
    position = index * stripe + shard * page_len + row % page_len
    angle = position.astype(F32) * frequency[...]
    cosine = jnp.cos(angle) * inverse
    sine_part = jnp.where(lane < LANES // 2, -jnp.sin(angle), jnp.sin(angle)) * inverse
    for head in range(width // LANES):
        columns = slice(head * LANES, (head + 1) * LANES)
        value = added(slice(0, rows), columns)
        turned = value * cosine + pltpu.roll(value, LANES // 2, 1) * sine_part
        finished[:, columns] = turned.astype(BF16)
    route(jobs, finished, outs)
    for send in range(SENDS):
        step = jnp.bitwise_xor(jobs[0, replica * SENDS + send], replica)
        query = asked[0][...]
        for other in range(1, 4):
            query = jnp.where(step == other, asked[other][...], query)
        scores = score(query, finished[send * page_len : (send + 1) * page_len])
        largest = jnp.max(scores, axis=1, keepdims=True)
        weights = jnp.exp(scores - largest)
        total = jnp.sum(weights, axis=1, keepdims=True)
        weights_out[send] = weights.astype(BF16)
        share[send] = jnp.broadcast_to(1.0 / total, share.shape[1:])
        level[send] = jnp.broadcast_to(largest + jnp.log(total), level.shape[1:])


def finish_values_kernel(jobs, own, near, first, third, scale, weights, share, level, *rest, shards, after):
    kept_parts, outs = rest[:4], rest[4 + after : 8 + after]
    packed, finished, result = rest[8 + after : 12 + after], rest[12 + after], rest[13 + after]
    shard = lax.axis_index("shard")
    for head in range(own.shape[1] // LANES):
        columns = slice(head * LANES, (head + 1) * LANES)
        total = add_parts(own, near, first, third, slice(None), columns)
        finished[:, columns] = (total * scale[...]).astype(BF16)
    route(jobs, finished, outs)
    page_len = own.shape[0] // SENDS
    for send in range(SENDS):
        products = jnp.dot(
            weights[send], finished[send * page_len : (send + 1) * page_len], preferred_element_type=F32
        )
        result[send] = head_pick(products) * share[send]
    here = level.shape[1] // shards
    count = SENDS * here
    rows = kept_parts[0].shape[0] - 16
    for step in range(4):
        start = pl.multiple_of(jnp.bitwise_xor(shard, step) * here, here)
        packed[step][:rows] = kept_parts[step][:rows]
        packed[step][rows : rows + count] = result[:, pl.ds(start, here), :].reshape(count, LANES).astype(BF16)
        mine = level[:, pl.ds(start, here), :].reshape(count, LANES)
        lines = jnp.concatenate([mine] + [jnp.zeros((LANES - count, LANES), F32)], axis=0).T[:16]
        tail = kept_parts[step][rows:].astype(F32) + split_lines(lines, 3)
        packed[step][rows + count :] = tail.astype(BF16)


def finish_keys(jobs, parts, frequency, asked, stripe):
    rows, width = parts[0].shape[0] - LINES, parts[0].shape[1]
    heads = asked[0].shape[0]
    page_len = rows // SENDS
    return pl.pallas_call(
        functools.partial(finish_keys_kernel, stripe=stripe),
        in_specs=[whole(SMEM)] + [whole()] * 9,
        out_specs=[whole()] * 8,
        out_shape=rep_shapes(page_len, width)
        + [
            jax.ShapeDtypeStruct((rows, LANES), F32),
            jax.ShapeDtypeStruct((SENDS, heads, page_len), BF16),
            jax.ShapeDtypeStruct((SENDS, heads, LANES), F32),
            jax.ShapeDtypeStruct((SENDS, heads, LANES), F32),
        ],
        scratch_shapes=[pltpu.VMEM((rows, width), BF16)],
        compiler_params=pltpu.CompilerParams(vmem_limit_bytes=LIMIT),
        cost_estimate=SMALL,
        name="finish_keys",
    )(jobs, *parts, frequency, *asked)


def finish_values(jobs, parts, scale, weights, share, level, kept_parts, after, shards):
    rows, width = parts[0].shape
    heads = level.shape[1]
    page_len = rows // SENDS
    packed = kept_parts[0].shape[0] + SENDS * heads // shards
    return pl.pallas_call(
        functools.partial(finish_values_kernel, shards=shards, after=len(after)),
        in_specs=[whole(SMEM)] + [whole()] * 12 + [whole(pl.ANY)] * len(after),
        out_specs=[whole()] * 8,
        out_shape=rep_shapes(page_len, width) + [jax.ShapeDtypeStruct((packed, LANES), BF16)] * 4,
        scratch_shapes=[pltpu.VMEM((rows, width), BF16), pltpu.VMEM((SENDS, heads, LANES), F32)],
        compiler_params=pltpu.CompilerParams(vmem_limit_bytes=LIMIT),
        cost_estimate=SMALL,
        name="finish_values",
    )(jobs, *parts, scale, weights, share, level, *kept_parts, *after)


def job_from(jobs, step):
    replica = lax.axis_index("rep")
    first = jnp.bitwise_xor(replica, step) * SENDS
    hit_first = jobs[0, first] == replica
    hit = hit_first | (jobs[0, first + 1] == replica)
    row = jnp.where(hit_first, first, first + 1)
    return hit, jobs[1, row], jobs[2, row]


def place_kernel(jobs, table, pool, *rest):
    key_pages, value_pages = rest[:4], rest[4:8]
    out, done, pages, sem = rest[8:]
    half = rest[0].shape[1]
    done[...] = jnp.zeros_like(done)
    for wait in (False, True):
        for step in range(4):
            hit, context, page = job_from(jobs, step)

            @pl.when(hit)
            def _():
                slot = table[page, context]
                copy = pltpu.make_async_copy(pages.at[step], out.at[slot], sem.at[step])
                if wait:
                    copy.wait()
                else:
                    pages[step, :, :half] = key_pages[step][...]
                    pages[step, :, half:] = value_pages[step][...]
                    copy.start()


def place_pages(jobs, table, pool, key_pages, value_pages):
    return pl.pallas_call(
        place_kernel,
        in_specs=[whole(SMEM)] * 2 + [whole(pl.ANY)] + [whole()] * 8,
        out_specs=[whole(pl.ANY), whole()],
        out_shape=[jax.ShapeDtypeStruct(pool.shape, pool.dtype), jax.ShapeDtypeStruct((16, LANES), BF16)],
        scratch_shapes=[pltpu.VMEM((4,) + pool.shape[1:], pool.dtype), pltpu.SemaphoreType.DMA((4,))],
        input_output_aliases={2: 0},
        compiler_params=pltpu.CompilerParams(vmem_limit_bytes=LIMIT),
        cost_estimate=SMALL,
        name="place_pages",
    )(jobs, table, pool, *key_pages, *value_pages)


def blend(parts, levels):
    top = functools.reduce(jnp.maximum, levels)
    shares = [jnp.exp(level - top) for level in levels]
    both = functools.reduce(jnp.add, shares)
    total = functools.reduce(jnp.add, [part * share for part, share in zip(parts, shares)])
    return total / both, top + jnp.log(both)


def gather_kernel(jobs, *refs, rows, count):
    parts, page, outs, page_out = refs[:4], refs[4], refs[5:9], refs[9]
    page_out[...] = page[...]
    mixed, level = blend(
        [ref[rows : rows + count].astype(F32) for ref in parts],
        [join_lines(ref[rows + count :], 3, count) for ref in parts],
    )
    here = count // SENDS
    replica = lax.axis_index("rep")
    lane = lax.broadcasted_iota(jnp.int32, (here, LANES), 1)
    for step, out in enumerate(outs):
        chosen = jobs[0, replica * SENDS] == jnp.bitwise_xor(replica, step)
        total = jnp.where(chosen, level[:here], level[here:])
        high = total.astype(BF16).astype(F32)
        middle_part = (total - high).astype(BF16).astype(F32)
        low = total - high - middle_part
        out[:, :LANES] = jnp.where(chosen, mixed[:here], mixed[here:]).astype(BF16)
        out[:, LANES:] = jnp.where(
            lane == 0, high, jnp.where(lane == 1, middle_part, jnp.where(lane == 2, low, 0.0))
        ).astype(BF16)


def gather_parts(jobs, parts, page, rows, count):
    return pl.pallas_call(
        functools.partial(gather_kernel, rows=rows, count=count),
        in_specs=[whole(SMEM)] + [whole()] * 5,
        out_specs=[whole()] * 5,
        out_shape=rep_shapes(count // SENDS, 2 * LANES) + [jax.ShapeDtypeStruct(page.shape, BF16)],
        compiler_params=pltpu.CompilerParams(vmem_limit_bytes=LIMIT),
        cost_estimate=SMALL,
        name="gather_parts",
    )(jobs, *parts, page)


def blend_kernel(*refs, rows, count):
    parts, after, kept_out, kept_level = refs[:4], refs[4], refs[5], refs[6]
    mixed, level = blend(
        [ref[:rows].astype(F32) for ref in parts], [join_lines(ref[rows + count :], 0, rows) for ref in parts]
    )
    kept_out[...] = mixed
    kept_level[...] = level


def blend_kept(parts, after, rows, count):
    return pl.pallas_call(
        functools.partial(blend_kernel, rows=rows, count=count),
        in_specs=[whole()] * 4 + [whole(pl.ANY)],
        out_specs=[whole()] * 2,
        out_shape=[jax.ShapeDtypeStruct((rows, LANES), F32)] * 2,
        compiler_params=pltpu.CompilerParams(vmem_limit_bytes=LIMIT),
        cost_estimate=SMALL,
        name="blend_kept",
    )(*parts, after)


def combine_kernel(jobs, kept_out, kept_level, *refs):
    parts, out, mixed = refs[:4], refs[5], refs[6]
    slots, here, size = mixed.shape
    mixed[...] = kept_out[...].reshape(mixed.shape)
    for step, ref in enumerate(parts):
        hit, context, _ = job_from(jobs, step)

        @pl.when(hit)
        def _():
            fresh_level = jnp.sum(ref[:, LANES:].astype(F32), axis=1, keepdims=True)
            fresh_level = jnp.broadcast_to(fresh_level, (here, LANES))
            old_level = kept_level[pl.ds(pl.multiple_of(context * here, here), here)]
            blended, _ = blend([mixed[context], ref[:, :LANES].astype(F32)], [old_level, fresh_level])
            mixed[context] = blended

    for head in range(here):
        out[:, head * size : (head + 1) * size] = mixed[:, head, :].astype(BF16)


def combine(jobs, kept_out, kept_level, parts, after, slots):
    here = kept_out.shape[0] // slots
    return pl.pallas_call(
        combine_kernel,
        in_specs=[whole(SMEM)] + [whole()] * 6 + [whole(pl.ANY)],
        out_specs=whole(),
        out_shape=jax.ShapeDtypeStruct((slots, here * LANES), BF16),
        scratch_shapes=[pltpu.VMEM((slots, here, LANES), F32)],
        compiler_params=pltpu.CompilerParams(vmem_limit_bytes=LIMIT),
        cost_estimate=SMALL,
        name="combine",
    )(jobs, kept_out, kept_level, *parts, after)


def on_device(
    hidden, norm_gain, kv_weight, restore_jobs, page_table, context_lengths, queries, kv_pool
):
    shards = lax.axis_size("shard")
    replicas = lax.axis_size("rep")
    stripe = hidden.shape[0] // SENDS
    page_len = stripe // shards
    kv_weight = pltpu.with_memory_space_constraint(kv_weight, pltpu.HBM)
    kv_pool = pltpu.with_memory_space_constraint(kv_pool, pltpu.HBM)
    gain = pltpu.with_memory_space_constraint(norm_gain, pltpu.HBM)
    blocks = pltpu.with_memory_space_constraint(
        hidden.reshape(SENDS, shards, page_len, hidden.shape[1]), pltpu.HBM
    )
    jobs = restore_jobs.T
    table = page_table[:, :, 0].T
    slots = queries.shape[0]
    query = queries.reshape(slots, QH, HD)

    def along(array, pairs):
        return lax.ppermute(array, "shard", pairs)

    def across(array, step):
        return lax.ppermute(array, "rep", [(i, i ^ step) for i in range(replicas)])

    def between(arrays):
        return [arrays[0]] + [across(arrays[step], step) for step in range(1, replicas)]

    key_sent, gained_sent, key_tile = project_first(blocks, gain, kv_weight)
    key_first = along(key_sent, FIRST)
    key_0, key_1, key_2, value_sent, gained, tile = project_keys(
        blocks, gain, kv_weight, gained_sent, key_tile
    )
    value_first = along(value_sent, FIRST)
    key_near = along(key_1, NEAR)
    key_2 = carry(key_2, key_first, [])
    key_third = along(key_2, THIRD)
    asked = between(ask(jobs, query, [key_2]))
    value_0, value_1, value_2 = project_values(gained, tile, [asked[0], value_first])
    value_near = along(value_1, NEAR)
    *kept_parts, new_pool = kept(jobs, table, context_lengths, query, kv_pool, [value_1] + asked[1:], shards)
    value_third = along(carry(value_2, value_first, [kept_parts[0]]), THIRD)
    frequency = THETA ** (-(jnp.arange(HD // 2, dtype=F32) * 2.0 / HD))
    frequency = jnp.concatenate([frequency, frequency])[None, :]
    *key_out, scale, weights, share, level = finish_keys(
        jobs, (key_0, key_near, key_first, key_third), frequency, asked, stripe
    )
    key_pages = between(key_out)
    finished = finish_values(
        jobs,
        (value_0, value_near, value_first, value_third),
        scale,
        weights,
        share,
        level,
        kept_parts,
        key_pages[1:],
        shards,
    )
    value_pages = [finished[0], None, across(finished[2], 2), across(finished[3], 3)]
    packed = finished[4:]
    parts = [packed[0]] + [
        along(packed[step], [(i, i ^ step) for i in range(shards)]) for step in range(shards - 1, 0, -1)
    ]
    here = QH // shards
    *gathered, near_page = gather_parts(jobs, parts, finished[1], slots * here, SENDS * here)
    fresh = between(gathered)
    value_pages[1] = across(near_page, 1)
    kept_out, kept_level = blend_kept(parts, gathered[0], slots * here, SENDS * here)
    new_pool, placed = place_pages(jobs, table, new_pool, key_pages, value_pages)
    return (new_pool, combine(jobs, kept_out, kept_level, fresh, placed, slots))


def solution(mesh):
    in_specs = (
        P(("outer", "rep"), "shard"),
        P("shard"),
        P("shard", None),
        P("outer", None),
        P(("outer", "rep"), None, "shard"),
        P(("outer", "rep")),
        P(("outer", "rep"), None),
        P(("outer", "rep", "shard"), None, None),
    )
    out_specs = (P(("outer", "rep", "shard"), None, None), P(("outer", "rep"), "shard"))
    fast = mesh.shape["shard"] == 4 and mesh.shape["rep"] == 4
    return jax.shard_map(
        on_device if fast else on_device_general, mesh=mesh, in_specs=in_specs, out_specs=out_specs, check_vma=False
    )
```

```python
import functools
import math

import jax
import jax.numpy as jnp
from jax import lax
from jax.experimental import pallas as pl
from jax.experimental.pallas import tpu as pltpu
from jax.sharding import PartitionSpec as P

D = 8192
QH = 64
KVH = 8
HD = 128
SENDS = 2


THETA = 500000.0
EPS = 1e-05
FLOOR_SCORE = -1e30


def rotate(key_rows, positions):
    half_dim = key_rows.shape[-1] // 2
    frequency = THETA ** (-(jnp.arange(half_dim, dtype=jnp.float32) * 2.0 / key_rows.shape[-1]))
    angles = positions.astype(jnp.float32)[:, None] * frequency[None, :]
    cosine = jnp.cos(angles)[:, None, :]
    sine_part = jnp.sin(angles)[:, None, :]
    first_half = key_rows[..., :half_dim]
    second = key_rows[..., half_dim:]
    return jnp.concatenate(
        [first_half * cosine - second * sine_part, second * cosine + first_half * sine_part],
        axis=-1,
    )


def finish(projected, inverse, positions):
    row_count = projected.shape[0]
    half_width = projected.shape[1] // 2
    scaled = projected * inverse[:, None]
    key_rows = rotate(scaled[:, :half_width].reshape(row_count, KVH, HD), positions).reshape(
        row_count, half_width
    )
    return jnp.concatenate([key_rows, scaled[:, half_width:]], axis=1).astype(jnp.bfloat16)


def spread_out(pieces, targets, replicas):
    outgoing = jnp.zeros((replicas,) + pieces.shape[1:], pieces.dtype)
    for send_index in range(SENDS):
        hit = (jnp.arange(replicas, dtype=jnp.int32) == targets[send_index])[:, None, None]
        outgoing = jnp.where(hit, pieces[send_index][None], outgoing)
    return outgoing


def on_device_general(
    hidden, norm_gain, kv_weight, restore_jobs, page_table, context_lengths, queries, kv_pool
):
    shards = lax.axis_size("shard")
    replicas = lax.axis_size("rep")
    my_replica = lax.axis_index("rep")
    my_shard = lax.axis_index("shard")
    stripe = hidden.shape[0] // SENDS
    page_len = stripe // shards
    features = hidden.shape[1]
    kv_width = kv_weight.shape[1]
    pool_pages = kv_pool.shape[0]
    destination = restore_jobs[:, 0]
    context = restore_jobs[:, 1]
    stripe_index = restore_jobs[:, 2]
    my_targets = lax.dynamic_slice_in_dim(destination, my_replica * SENDS, SENDS, 0)
    is_mine = destination == my_replica
    gain_wide = norm_gain.astype(jnp.float32)[None, :]
    page_rows = jnp.arange(page_len, dtype=jnp.int32)
    wide = hidden.astype(jnp.float32)
    squares = lax.psum(jnp.sum(wide * wide, axis=1), "shard")
    inverse = lax.rsqrt(squares / D + EPS)
    gained = (wide * gain_wide).astype(jnp.bfloat16)
    arranged = gained.reshape(SENDS, shards, page_len, features).transpose(1, 0, 2, 3)
    arranged = arranged.reshape(shards * SENDS * page_len, features)
    owned = lax.psum_scatter(
        jnp.dot(arranged, kv_weight, preferred_element_type=jnp.float32).astype(jnp.bfloat16),
        "shard",
        scatter_dimension=0,
        tiled=True,
    ).astype(jnp.float32)
    owned_inverse = lax.dynamic_slice_in_dim(
        inverse.reshape(SENDS, stripe), my_shard * page_len, page_len, 1
    )
    my_stripes = lax.dynamic_slice_in_dim(stripe_index, my_replica * SENDS, SENDS, 0)
    positions = my_stripes[:, None] * stripe + my_shard * page_len + page_rows[None, :]
    finished = finish(owned, owned_inverse.reshape(-1), positions.reshape(-1)).reshape(
        SENDS, page_len, kv_width
    )
    outgoing = spread_out(finished, my_targets, replicas)
    arrived = lax.all_to_all(outgoing, "rep", split_axis=0, concat_axis=0, tiled=True)
    mine_grid = is_mine.reshape(replicas, SENDS)
    has_page = jnp.any(mine_grid, axis=1)
    which = jnp.argmax(mine_grid.astype(jnp.int32), axis=1)
    job_index = jnp.arange(replicas, dtype=jnp.int32) * SENDS + which
    physical = jnp.where(
        has_page, page_table[context[job_index], stripe_index[job_index], 0], pool_pages
    )
    new_pool = kv_pool.at[physical].set(arrived, mode="drop")
    slots = queries.shape[0]
    pages_dev = page_table.shape[1]
    group = QH // KVH
    scale = 1.0 / math.sqrt(HD)
    cached = new_pool[page_table[:, :, 0]]
    key_rows = cached[..., : KVH * HD].reshape(slots, pages_dev * page_len, KVH, HD)
    value_rows = cached[..., KVH * HD :].reshape(slots, pages_dev * page_len, KVH, HD)
    query_rows = queries.reshape(slots, KVH, group, HD)
    scores = (
        jnp.einsum("cgmd,cpgd->cgmp", query_rows, key_rows, preferred_element_type=jnp.float32)
        * scale
    )
    position = (
        (jnp.arange(pages_dev, dtype=jnp.int32)[:, None] * shards + my_shard) * page_len
        + page_rows[None, :]
    ).reshape(-1)
    usable = (position[None, :] < context_lengths[:, None])[:, None, None, :]
    local_max = jnp.max(jnp.where(usable, scores, FLOOR_SCORE), axis=-1)
    weights = jnp.where(usable, jnp.exp(scores - local_max[..., None]), 0.0)
    denominator = jnp.sum(weights, axis=-1).reshape(slots, QH)
    numerator = jnp.einsum(
        "cgmp,cpgd->cgmd",
        weights.astype(jnp.bfloat16),
        value_rows,
        preferred_element_type=jnp.float32,
    )
    numerator = numerator.reshape(slots, QH, HD)
    local_max = local_max.reshape(slots, QH)
    heads_here = QH // shards
    row_max = lax.pmax(local_max, "shard")
    factor = jnp.exp(local_max - row_max)
    scaled_num = (numerator * factor[..., None]).reshape(slots, QH * HD)
    numerator, denominator = (
        lax.psum(scaled_num.astype(jnp.bfloat16), "shard").astype(jnp.float32),
        lax.psum((denominator * factor).astype(jnp.bfloat16), "shard").astype(jnp.float32),
    )
    numerator = lax.dynamic_slice_in_dim(numerator, my_shard * heads_here * HD, heads_here * HD, 1)
    denominator = lax.dynamic_slice_in_dim(denominator, my_shard * heads_here, heads_here, 1)
    numerator = numerator.reshape(slots, heads_here, HD)
    attention_out = numerator / denominator[..., None]
    return (new_pool, attention_out.reshape(slots, heads_here * HD).astype(jnp.bfloat16))


FIRST = [(0, 1), (3, 2), (1, 3), (2, 0)]
NEAR = [(0, 1), (1, 0), (2, 3), (3, 2)]
THIRD = [(0, 3), (3, 0), (1, 2), (2, 1)]
LANES = 128
LINES = 8
GROUP = 2
BF16 = jnp.bfloat16
F32 = jnp.float32
SMEM = pltpu.SMEM
VMEM = pltpu.VMEM
SMALL = pl.CostEstimate(flops=1, bytes_accessed=1, transcendentals=0)
LIMIT = 24 * 1024 * 1024


def whole(space=VMEM):
    return pl.BlockSpec(memory_space=space)


def row_copies(hidden, blocks, rows_in, sem):
    stripes, _, page_len, _ = hidden.shape
    return [
        pltpu.make_async_copy(
            hidden.at[stripe, block],
            rows_in.at[pl.ds((place * stripes + stripe) * page_len, page_len)],
            sem.at[place * stripes + stripe],
        )
        for place, block in enumerate(blocks)
        for stripe in range(stripes)
    ]


def scale_rows(rows_in, gained, gain_in, span):
    wide_gain = gain_in[...].astype(F32).reshape(1, gain_in.shape[0])
    gained[span] = (rows_in[span].astype(F32) * wide_gain).astype(BF16)


def put_squares(rows_in, span, out, first):
    rows = out.shape[0] - LINES
    squares = jnp.zeros((rows, LANES), F32)
    for lane in range(rows_in.shape[1] // LANES):
        part = rows_in[span, lane * LANES : (lane + 1) * LANES].astype(F32)
        squares = squares + part * part
    total = jnp.sum(squares.T, axis=0, keepdims=True)
    high = total.astype(BF16).astype(F32)
    place = lax.broadcasted_iota(jnp.int32, (LINES, LANES), 0) - first
    lines = jnp.where(place == 0, high, jnp.where(place == 1, total - high, 0.0))
    rest = jnp.zeros((LINES, out.shape[1] - LANES), F32)
    out[rows:] = jnp.concatenate([lines, rest], axis=1).astype(BF16)


def is_inner(shard):
    return (shard == 1) | (shard == 2)


def far_blocks(shard):
    lower = shard < 2
    return jnp.where(lower, 2, 1), jnp.where(lower, 3, 0)


def first_kernel(hidden, gain, weight, out, gained, tile, rows_in, gain_in, row_sem, gain_sem, tile_sem):
    shard = lax.axis_index("shard")
    half = weight.shape[1] // 2
    inner_block, outer_block = far_blocks(shard)
    rows_here = row_copies(hidden, [jnp.where(is_inner(shard), outer_block, inner_block)], rows_in, row_sem)
    piece = half // 2
    pieces = [slice(index * piece, (index + 1) * piece) for index in range(2)]
    tile_copies = [
        pltpu.make_async_copy(weight.at[:, columns], tile.at[:, columns], tile_sem.at[index])
        for index, columns in enumerate(pieces)
    ]
    gain_copy = pltpu.make_async_copy(gain, gain_in, gain_sem)
    gain_copy.start()
    for copy in rows_here + tile_copies:
        copy.start()
    gain_copy.wait()
    for copy in rows_here:
        copy.wait()
    scale_rows(rows_in, gained, gain_in, slice(None))
    put_squares(rows_in, slice(None), out, 0)
    for copy, columns in zip(tile_copies, pieces):
        copy.wait()
        product = jnp.dot(gained[...], tile[:, columns], preferred_element_type=F32)
        out[: gained.shape[0], columns] = product.astype(BF16)


def project_first(hidden, gain, weight):
    stripes, blocks, page_len, features = hidden.shape
    half = weight.shape[1] // 2
    rows = stripes * page_len
    return pl.pallas_call(
        first_kernel,
        in_specs=[whole(pl.ANY)] * 3,
        out_specs=[whole()] * 3,
        out_shape=[
            jax.ShapeDtypeStruct((rows + LINES, half), BF16),
            jax.ShapeDtypeStruct((rows, features), BF16),
            jax.ShapeDtypeStruct((features, half), BF16),
        ],
        scratch_shapes=[
            pltpu.VMEM((rows, features), BF16),
            pltpu.VMEM((features,), BF16),
            pltpu.SemaphoreType.DMA((stripes,)),
            pltpu.SemaphoreType.DMA,
            pltpu.SemaphoreType.DMA((2,)),
        ],
        compiler_params=pltpu.CompilerParams(vmem_limit_bytes=LIMIT),
        cost_estimate=SMALL,
        name="project_first",
    )(hidden, gain, weight)


def head_spread(query, width):
    heads = query.shape[0]
    group = heads // (width // LANES)
    head = lax.broadcasted_iota(jnp.int32, (heads, LANES), 0)
    pieces = [jnp.where(head // group == g, query, jnp.zeros_like(query)) for g in range(width // LANES)]
    return jnp.concatenate(pieces, axis=1)


def head_pick(products):
    heads, width = products.shape
    group = heads // (width // LANES)
    head = lax.broadcasted_iota(jnp.int32, (heads, LANES), 0)
    picked = products[:, :LANES]
    for g in range(1, width // LANES):
        picked = jnp.where(head // group == g, products[:, g * LANES : (g + 1) * LANES], picked)
    return picked


def score(query, key_rows):
    spread = head_spread(query, key_rows.shape[1])
    scores = lax.dot_general(spread, key_rows, (((1,), (1,)), ((), ())), preferred_element_type=F32)
    return scores * (1.0 / math.sqrt(LANES))


def attend(query, key_rows, value_rows, usable):
    scores = jnp.where(usable, score(query, key_rows), FLOOR_SCORE)
    largest = jnp.max(scores, axis=1, keepdims=True)
    weights = jnp.where(usable, jnp.exp(scores - largest), 0.0)
    total = jnp.sum(weights, axis=1, keepdims=True)
    picked = head_pick(jnp.dot(weights.astype(BF16), value_rows, preferred_element_type=F32))
    some = total > 0.0
    safe = jnp.where(some, total, 1.0)
    return picked / safe, jnp.where(some, largest + jnp.log(safe), FLOOR_SCORE)


def split_lines(lines, first):
    high = lines.astype(BF16).astype(F32)
    middle_part = (lines - high).astype(BF16).astype(F32)
    low = lines - high - middle_part
    place = lax.broadcasted_iota(jnp.int32, lines.shape, 0) - first
    return jnp.where(place == 0, high, jnp.where(place == 1, middle_part, jnp.where(place == 2, low, 0.0)))


def join_lines(tail, first, rows):
    line = jnp.sum(tail[first : first + 3].astype(F32), axis=0, keepdims=True)
    return jnp.broadcast_to(line, (LANES, LANES)).T[:rows]


def project_keys_kernel(hidden, gain, weight, sent, key_tile, *rest):
    own, near, third, values, gained, value_tile = rest[:6]
    rows_in, gain_in, row_sem, gain_sem, tile_sem = rest[6:]
    shard = lax.axis_index("shard")
    rows = values.shape[0]
    half = weight.shape[1] // 2
    inner_block, outer_block = far_blocks(shard)
    blocks = [shard, jnp.bitwise_xor(shard, 1), jnp.where(is_inner(shard), inner_block, outer_block)]
    rows_here = row_copies(hidden, blocks, rows_in, row_sem)
    tile_copy = pltpu.make_async_copy(weight.at[:, pl.ds(half, half)], value_tile, tile_sem)
    gain_copy = pltpu.make_async_copy(gain, gain_in, gain_sem)
    gain_copy.start()
    for copy in rows_here + [tile_copy]:
        copy.start()
    gain_copy.wait()
    for copy in rows_here:
        copy.wait()
    scale_rows(rows_in, gained, gain_in, slice(None))
    for place, ref in enumerate((own, near, third)):
        span = slice(place * rows, (place + 1) * rows)
        put_squares(rows_in, span, ref, 2 if place == 2 else 0)
    product = jnp.dot(gained[...], key_tile[...], preferred_element_type=F32).astype(BF16)
    for place, ref in enumerate((own, near, third)):
        ref[:rows] = product[place * rows : (place + 1) * rows]
    tile_copy.wait()
    values[...] = jnp.dot(sent[...], value_tile[...], preferred_element_type=F32).astype(BF16)


def project_keys(hidden, gain, weight, sent, tile):
    stripes, blocks, page_len, features = hidden.shape
    half = weight.shape[1] // 2
    rows = stripes * page_len
    return pl.pallas_call(
        project_keys_kernel,
        in_specs=[whole(pl.ANY)] * 3 + [whole()] * 2,
        out_specs=[whole()] * 6,
        out_shape=[jax.ShapeDtypeStruct((rows + LINES, half), BF16)] * 3
        + [
            jax.ShapeDtypeStruct((rows, half), BF16),
            jax.ShapeDtypeStruct((3 * rows, features), BF16),
            jax.ShapeDtypeStruct((features, half), BF16),
        ],
        scratch_shapes=[
            pltpu.VMEM((3 * rows, features), BF16),
            pltpu.VMEM((features,), BF16),
            pltpu.SemaphoreType.DMA((3 * stripes,)),
            pltpu.SemaphoreType.DMA,
            pltpu.SemaphoreType.DMA,
        ],
        compiler_params=pltpu.CompilerParams(vmem_limit_bytes=LIMIT),
        cost_estimate=SMALL,
        name="project_keys",
    )(hidden, gain, weight, sent, tile)


def project_values_kernel(gained, tile, *rest):
    product = jnp.dot(gained[...], tile[...], preferred_element_type=F32).astype(BF16)
    rows = rest[-1].shape[0]
    for place, ref in enumerate(rest[-3:]):
        ref[...] = product[place * rows : (place + 1) * rows]


def project_values(gained, tile, after):
    return pl.pallas_call(
        project_values_kernel,
        in_specs=[whole()] * 2 + [whole(pl.ANY)] * len(after),
        out_specs=[whole()] * 3,
        out_shape=[jax.ShapeDtypeStruct((gained.shape[0] // 3, tile.shape[1]), BF16)] * 3,
        compiler_params=pltpu.CompilerParams(vmem_limit_bytes=LIMIT),
        cost_estimate=SMALL,
        name="project_values",
    )(gained, tile, *after)


def carry_kernel(mine, first, *rest):
    inner = is_inner(lax.axis_index("shard"))
    arrived = jnp.where(inner, first[...].astype(F32), 0.0)
    rest[-1][...] = (mine[...].astype(F32) + arrived).astype(BF16)


def carry(mine, first, after):
    return pl.pallas_call(
        carry_kernel,
        in_specs=[whole(), whole()] + [whole(pl.ANY)] * len(after),
        out_specs=whole(),
        out_shape=jax.ShapeDtypeStruct(mine.shape, BF16),
        compiler_params=pltpu.CompilerParams(vmem_limit_bytes=LIMIT),
        cost_estimate=SMALL,
        name="carry",
    )(mine, first, *after)


def rep_shapes(rows, width):
    return [jax.ShapeDtypeStruct((rows, width), BF16)] * 4


def ask_kernel(jobs, query, *rest):
    outs, marks = rest[-5:-1], rest[-1]
    slots = query.shape[0]
    replica = lax.axis_index("rep")
    line = lax.broadcasted_iota(jnp.int32, marks.shape, 0)
    found = jnp.zeros(marks.shape, jnp.int32)
    for step, out in enumerate(outs):
        hit, context, _ = job_from(jobs, step)
        out[...] = query[context]
        sent = jobs[0, replica * SENDS] == jnp.bitwise_xor(replica, step)
        found = found + jnp.where(line == step * slots + context, hit.astype(jnp.int32), 0)
        found = found + jnp.where(line == 4 * slots + step, sent.astype(jnp.int32), 0)
    marks[...] = found.astype(F32)


def ask(jobs, query, after):
    return pl.pallas_call(
        ask_kernel,
        in_specs=[whole(SMEM), whole()] + [whole(pl.ANY)] * len(after),
        out_specs=[whole()] * 5,
        out_shape=rep_shapes(*query.shape[1:])
        + [jax.ShapeDtypeStruct((4 * query.shape[0] + 8, LANES), F32)],
        compiler_params=pltpu.CompilerParams(vmem_limit_bytes=LIMIT),
        cost_estimate=SMALL,
        name="ask",
    )(jobs, query, *after)


def kept_kernel(jobs, table, lengths, query, pool, *rest, shards, after):
    outs = rest[after : after + 4]
    new_pool, pages, total, level, in_sem, out_sem = rest[after + 4 :]
    slots, heads, _ = query.shape
    here = heads // shards
    rows = slots * here
    replica = lax.axis_index("rep")
    shard = lax.axis_index("shard")
    page_len = pool.shape[1]
    half = pool.shape[2] // 2

    def copy_in(context, page):
        place = context * 2 + page
        return pltpu.make_async_copy(pool.at[table[page, context]], pages.at[place], in_sem.at[place])

    def copy_out(context, page):
        place = context * 2 + page
        return pltpu.make_async_copy(pages.at[place], new_pool.at[table[page, context]], out_sem.at[place])

    @pl.loop(0, slots)
    def _(context):
        for page in range(2):
            copy_in(context, page).start()

    lane = lax.broadcasted_iota(jnp.int32, (heads, 2 * page_len), 1)
    page_of = lane // page_len
    position = (page_of * shards + shard) * page_len + lane % page_len

    def context_part(context):
        gone = [jnp.int32(0), jnp.int32(0)]
        for job in range(jobs.shape[1]):
            hit = (jobs[0, job] == replica) & (jobs[1, job] == context)
            for page in range(2):
                gone[page] = gone[page] | (hit & (jobs[2, job] == page)).astype(jnp.int32)
        usable = (position < lengths[context]) & (jnp.where(page_of == 0, gone[0], gone[1]) == 0)
        both = pages[pl.ds(context * 2, 2)].reshape(2 * page_len, 2 * half)
        return attend(query[context], both[:, :half], both[:, half:], usable)

    @pl.loop(0, slots // GROUP)
    def _(index):
        contexts = [index * GROUP + member for member in range(GROUP)]
        for context in contexts:
            for page in range(2):
                copy_in(context, page).wait()
                copy_out(context, page).start()
        results = [context_part(context) for context in contexts]
        for context, (result, logarithm) in zip(contexts, results):
            total[context] = result
            level[context] = jnp.broadcast_to(logarithm, result.shape)

    for step, out in enumerate(outs):
        start = pl.multiple_of(jnp.bitwise_xor(shard, step) * here, here)
        out[:rows] = total[:, pl.ds(start, here), :].reshape(rows, LANES).astype(BF16)
        lines = level[:, pl.ds(start, here), :].reshape(rows, LANES).T[:16]
        out[rows:] = split_lines(lines, 0).astype(BF16)

    @pl.loop(0, slots)
    def _(context):
        for page in range(2):
            copy_out(context, page).wait()


def kept(jobs, table, lengths, query, pool, after, shards):
    slots, heads, size = query.shape
    return pl.pallas_call(
        functools.partial(kept_kernel, shards=shards, after=len(after)),
        in_specs=[whole(SMEM)] * 3 + [whole()] + [whole(pl.ANY)] * (1 + len(after)),
        out_specs=[whole()] * 4 + [whole(pl.ANY)],
        out_shape=[jax.ShapeDtypeStruct((slots * heads // shards + 16, size), BF16)] * 4
        + [jax.ShapeDtypeStruct(pool.shape, pool.dtype)],
        scratch_shapes=[
            pltpu.VMEM((slots * 2,) + pool.shape[1:], pool.dtype),
            pltpu.VMEM(query.shape, F32),
            pltpu.VMEM(query.shape, F32),
            pltpu.SemaphoreType.DMA((slots * 2,)),
            pltpu.SemaphoreType.DMA((slots * 2,)),
        ],
        compiler_params=pltpu.CompilerParams(vmem_limit_bytes=LIMIT),
        cost_estimate=SMALL,
        name="kept",
    )(jobs, table, lengths, query, pool, *after)


def route(jobs, finished, outs):
    replica = lax.axis_index("rep")
    page_len = finished.shape[0] // SENDS
    for step, out in enumerate(outs):
        chosen = jobs[0, replica * SENDS] == jnp.bitwise_xor(replica, step)

        @pl.when(chosen)
        def _():
            out[...] = finished[:page_len]

        @pl.when(jnp.logical_not(chosen))
        def _():
            out[...] = finished[page_len:]


def add_parts(own, near, first, third, rows, columns):
    direct = jnp.where(is_inner(lax.axis_index("shard")), 0.0, first[rows, columns].astype(F32))
    parts = [ref[rows, columns].astype(F32) for ref in (own, near, third)]
    return (parts[0] + parts[1]) + (parts[2] + direct)


def finish_keys_kernel(jobs, own, near, first, third, frequency, *rest, stripe):
    asked, outs = rest[:4], rest[4:8]
    scale, weights_out, share, tails, finished, level = rest[8:]
    replica = lax.axis_index("rep")
    shard = lax.axis_index("shard")
    rows, width = finished.shape
    page_len = rows // SENDS

    def added(span, columns):
        return add_parts(own, near, first, third, span, columns)

    squares = jnp.sum(added(slice(rows, rows + LINES), slice(0, LANES)), axis=0, keepdims=True)
    squares = jnp.broadcast_to(squares, (LANES, LANES)).T[:rows]
    inverse = lax.rsqrt(squares / D + EPS)
    scale[...] = inverse
    row = lax.broadcasted_iota(jnp.int32, (rows, LANES), 0)
    lane = lax.broadcasted_iota(jnp.int32, (rows, LANES), 1)
    index = jnp.where(row < page_len, jobs[2, replica * SENDS], jobs[2, replica * SENDS + 1])
    position = index * stripe + shard * page_len + row % page_len
    angle = position.astype(F32) * frequency[...]
    cosine = jnp.cos(angle) * inverse
    sine_part = jnp.where(lane < LANES // 2, -jnp.sin(angle), jnp.sin(angle)) * inverse
    for head in range(width // LANES):
        columns = slice(head * LANES, (head + 1) * LANES)
        value = added(slice(0, rows), columns)
        turned = value * cosine + pltpu.roll(value, LANES // 2, 1) * sine_part
        finished[:, columns] = turned.astype(BF16)
    route(jobs, finished, outs)
    for send in range(SENDS):
        step = jnp.bitwise_xor(jobs[0, replica * SENDS + send], replica)
        query = asked[0][...]
        for other in range(1, 4):
            query = jnp.where(step == other, asked[other][...], query)
        scores = score(query, finished[send * page_len : (send + 1) * page_len])
        largest = jnp.max(scores, axis=1, keepdims=True)
        weights = jnp.exp(scores - largest)
        total = jnp.sum(weights, axis=1, keepdims=True)
        weights_out[send] = weights.astype(BF16)
        share[send] = jnp.broadcast_to(1.0 / total, share.shape[1:])
        level[send] = jnp.broadcast_to(largest + jnp.log(total), level.shape[1:])
    here = level.shape[1] // tails.shape[0]
    count = SENDS * here
    for step in range(tails.shape[0]):
        start = pl.multiple_of(jnp.bitwise_xor(shard, step) * here, here)
        mine = level[:, pl.ds(start, here), :].reshape(count, LANES)
        around = [jnp.zeros((rows_, LANES), F32) for rows_ in (step * count, LANES - (step + 1) * count)]
        pieces = [piece for piece in (around[0], mine, around[1]) if piece.shape[0]]
        tails[step] = split_lines(jnp.concatenate(pieces, axis=0).T[:16], 3)


def finish_values_kernel(marks, own, near, first, third, scale, weights, share, tails, *rest, shards, after):
    kept_parts, outs = rest[:4], rest[4 + after : 8 + after]
    packed, finished, result = rest[8 + after : 12 + after], rest[12 + after], rest[13 + after]
    shard = lax.axis_index("shard")
    page_len = own.shape[0] // SENDS
    sent = [marks[marks.shape[0] - 8 + step : marks.shape[0] - 7 + step] > 0.0 for step in range(4)]
    for head in range(own.shape[1] // LANES):
        columns = slice(head * LANES, (head + 1) * LANES)
        total = add_parts(own, near, first, third, slice(None), columns) * scale[...]
        finished[:, columns] = total.astype(BF16)
        for step, out in enumerate(outs):
            out[:, columns] = jnp.where(sent[step], total[:page_len], total[page_len:]).astype(BF16)
    for send in range(SENDS):
        products = jnp.dot(
            weights[send], finished[send * page_len : (send + 1) * page_len], preferred_element_type=F32
        )
        result[send] = head_pick(products) * share[send]
    here = share.shape[1] // shards
    count = SENDS * here
    rows = kept_parts[0].shape[0] - 16
    for step in range(4):
        start = pl.multiple_of(jnp.bitwise_xor(shard, step) * here, here)
        packed[step][:rows] = kept_parts[step][:rows]
        packed[step][rows : rows + count] = result[:, pl.ds(start, here), :].reshape(count, LANES).astype(BF16)
        packed[step][rows + count :] = (kept_parts[step][rows:].astype(F32) + tails[step]).astype(BF16)


def finish_keys(jobs, parts, frequency, asked, stripe, shards):
    rows, width = parts[0].shape[0] - LINES, parts[0].shape[1]
    heads = asked[0].shape[0]
    page_len = rows // SENDS
    return pl.pallas_call(
        functools.partial(finish_keys_kernel, stripe=stripe),
        in_specs=[whole(SMEM)] + [whole()] * 9,
        out_specs=[whole()] * 8,
        out_shape=rep_shapes(page_len, width)
        + [
            jax.ShapeDtypeStruct((rows, LANES), F32),
            jax.ShapeDtypeStruct((SENDS, heads, page_len), BF16),
            jax.ShapeDtypeStruct((SENDS, heads, LANES), F32),
            jax.ShapeDtypeStruct((shards, 16, LANES), F32),
        ],
        scratch_shapes=[pltpu.VMEM((rows, width), BF16), pltpu.VMEM((SENDS, heads, LANES), F32)],
        compiler_params=pltpu.CompilerParams(vmem_limit_bytes=LIMIT),
        cost_estimate=SMALL,
        name="finish_keys",
    )(jobs, *parts, frequency, *asked)


def finish_values(marks, parts, scale, weights, share, tails, kept_parts, after, shards):
    rows, width = parts[0].shape
    heads = share.shape[1]
    page_len = rows // SENDS
    packed = kept_parts[0].shape[0] + SENDS * heads // shards
    return pl.pallas_call(
        functools.partial(finish_values_kernel, shards=shards, after=len(after)),
        in_specs=[whole()] * 13 + [whole(pl.ANY)] * len(after),
        out_specs=[whole()] * 8,
        out_shape=rep_shapes(page_len, width) + [jax.ShapeDtypeStruct((packed, LANES), BF16)] * 4,
        scratch_shapes=[pltpu.VMEM((rows, width), BF16), pltpu.VMEM((SENDS, heads, LANES), F32)],
        compiler_params=pltpu.CompilerParams(vmem_limit_bytes=LIMIT),
        cost_estimate=SMALL,
        name="finish_values",
    )(marks, *parts, scale, weights, share, tails, *kept_parts, *after)


def job_from(jobs, step):
    replica = lax.axis_index("rep")
    first = jnp.bitwise_xor(replica, step) * SENDS
    hit_first = jobs[0, first] == replica
    hit = hit_first | (jobs[0, first + 1] == replica)
    row = jnp.where(hit_first, first, first + 1)
    return hit, jobs[1, row], jobs[2, row]


def place_kernel(jobs, table, pool, *rest):
    key_pages, value_pages = rest[:4], rest[4:8]
    out, done, pages, sem = rest[8:]
    half = rest[0].shape[1]
    done[...] = jnp.zeros_like(done)
    for wait in (False, True):
        for step in range(4):
            hit, context, page = job_from(jobs, step)

            @pl.when(hit)
            def _():
                slot = table[page, context]
                copy = pltpu.make_async_copy(pages.at[step], out.at[slot], sem.at[step])
                if wait:
                    copy.wait()
                else:
                    pages[step, :, :half] = key_pages[step][...]
                    pages[step, :, half:] = value_pages[step][...]
                    copy.start()


def place_pages(jobs, table, pool, key_pages, value_pages):
    return pl.pallas_call(
        place_kernel,
        in_specs=[whole(SMEM)] * 2 + [whole(pl.ANY)] + [whole()] * 8,
        out_specs=[whole(pl.ANY), whole()],
        out_shape=[jax.ShapeDtypeStruct(pool.shape, pool.dtype), jax.ShapeDtypeStruct((16, LANES), BF16)],
        scratch_shapes=[pltpu.VMEM((4,) + pool.shape[1:], pool.dtype), pltpu.SemaphoreType.DMA((4,))],
        input_output_aliases={2: 0},
        compiler_params=pltpu.CompilerParams(vmem_limit_bytes=LIMIT),
        cost_estimate=SMALL,
        name="place_pages",
    )(jobs, table, pool, *key_pages, *value_pages)


def blend(parts, levels):
    top = functools.reduce(jnp.maximum, levels)
    shares = [jnp.exp(level - top) for level in levels]
    both = functools.reduce(jnp.add, shares)
    total = functools.reduce(jnp.add, [part * share for part, share in zip(parts, shares)])
    return total / both, top + jnp.log(both)


def gather_kernel(marks, *refs, rows, count):
    parts, page, outs, page_out = refs[:4], refs[4], refs[5:9], refs[9]
    page_out[...] = page[...]
    tail = functools.reduce(jnp.add, [ref[rows + count :].astype(F32) for ref in parts])
    levels = join_lines(tail, 3, LANES)
    mixed, level = blend(
        [ref[rows : rows + count].astype(F32) for ref in parts],
        [levels[step * count : (step + 1) * count] for step in (0, 3, 2, 1)],
    )
    here = count // SENDS
    lane = lax.broadcasted_iota(jnp.int32, (here, LANES), 1)
    for step, out in enumerate(outs):
        chosen = marks[marks.shape[0] - 8 + step : marks.shape[0] - 7 + step] > 0.0
        total = jnp.where(chosen, level[:here], level[here:])
        high = total.astype(BF16).astype(F32)
        middle_part = (total - high).astype(BF16).astype(F32)
        low = total - high - middle_part
        out[:, :LANES] = jnp.where(chosen, mixed[:here], mixed[here:]).astype(BF16)
        out[:, LANES:] = jnp.where(
            lane == 0, high, jnp.where(lane == 1, middle_part, jnp.where(lane == 2, low, 0.0))
        ).astype(BF16)


def gather_parts(marks, parts, page, rows, count):
    return pl.pallas_call(
        functools.partial(gather_kernel, rows=rows, count=count),
        in_specs=[whole()] * 6,
        out_specs=[whole()] * 5,
        out_shape=rep_shapes(count // SENDS, 2 * LANES) + [jax.ShapeDtypeStruct(page.shape, BF16)],
        compiler_params=pltpu.CompilerParams(vmem_limit_bytes=LIMIT),
        cost_estimate=SMALL,
        name="gather_parts",
    )(marks, *parts, page)


def blend_kernel(*refs, rows, count):
    parts, after, kept_out, kept_level = refs[:4], refs[4], refs[5], refs[6]
    mixed, level = blend(
        [ref[:rows].astype(F32) for ref in parts], [join_lines(ref[rows + count :], 0, rows) for ref in parts]
    )
    kept_out[...] = mixed
    kept_level[...] = level


def blend_kept(parts, after, rows, count):
    return pl.pallas_call(
        functools.partial(blend_kernel, rows=rows, count=count),
        in_specs=[whole()] * 4 + [whole(pl.ANY)],
        out_specs=[whole()] * 2,
        out_shape=[jax.ShapeDtypeStruct((rows, LANES), F32)] * 2,
        compiler_params=pltpu.CompilerParams(vmem_limit_bytes=LIMIT),
        cost_estimate=SMALL,
        name="blend_kept",
    )(*parts, after)


FRESH_ORDER = (0, 2, 3, 1)


def combine_kernel(marks, kept_out, kept_level, *refs):
    parts, out, mixed = refs[:4], refs[5], refs[6]
    slots, here, size = mixed.shape
    spans = [slice(context * here, (context + 1) * here) for context in range(slots)]
    blended = []
    for step, ref in zip(FRESH_ORDER, parts):
        hits = [marks[step * slots + context : step * slots + context + 1] > 0.0 for context in range(slots)]
        old, old_level = jnp.zeros((here, size), F32), jnp.zeros((here, size), F32)
        for hit, span in zip(hits, spans):
            old = jnp.where(hit, kept_out[span], old)
            old_level = jnp.where(hit, kept_level[span], old_level)
        fresh_level = jnp.sum(ref[:, LANES:].astype(F32), axis=1, keepdims=True)
        fresh_level = jnp.broadcast_to(fresh_level, (here, size))
        result, _ = blend([old, ref[:, :LANES].astype(F32)], [old_level, fresh_level])
        blended.append((hits, result))
    for context, span in enumerate(spans):
        total = kept_out[span]
        for hits, result in blended:
            total = jnp.where(hits[context], result, total)
        mixed[context] = total
    for head in range(here):
        out[:, head * size : (head + 1) * size] = mixed[:, head, :].astype(BF16)


def combine(marks, kept_out, kept_level, parts, after, slots):
    here = kept_out.shape[0] // slots
    return pl.pallas_call(
        combine_kernel,
        in_specs=[whole()] * 7 + [whole(pl.ANY)],
        out_specs=whole(),
        out_shape=jax.ShapeDtypeStruct((slots, here * LANES), BF16),
        scratch_shapes=[pltpu.VMEM((slots, here, LANES), F32)],
        compiler_params=pltpu.CompilerParams(vmem_limit_bytes=LIMIT),
        cost_estimate=SMALL,
        name="combine",
    )(marks, kept_out, kept_level, *parts, after)


def on_device(
    hidden, norm_gain, kv_weight, restore_jobs, page_table, context_lengths, queries, kv_pool
):
    shards = lax.axis_size("shard")
    replicas = lax.axis_size("rep")
    stripe = hidden.shape[0] // SENDS
    page_len = stripe // shards
    kv_weight = pltpu.with_memory_space_constraint(kv_weight, pltpu.HBM)
    kv_pool = pltpu.with_memory_space_constraint(kv_pool, pltpu.HBM)
    gain = pltpu.with_memory_space_constraint(norm_gain, pltpu.HBM)
    blocks = pltpu.with_memory_space_constraint(
        hidden.reshape(SENDS, shards, page_len, hidden.shape[1]), pltpu.HBM
    )
    jobs = restore_jobs.T
    table = page_table[:, :, 0].T
    slots = queries.shape[0]
    query = queries.reshape(slots, QH, HD)

    def along(array, pairs):
        return lax.ppermute(array, "shard", pairs)

    def across(array, step):
        return lax.ppermute(array, "rep", [(i, i ^ step) for i in range(replicas)])

    def between(arrays):
        return [arrays[0]] + [across(arrays[step], step) for step in range(1, replicas)]

    key_sent, gained_sent, key_tile = project_first(blocks, gain, kv_weight)
    key_first = along(key_sent, FIRST)
    key_0, key_1, key_2, value_sent, gained, tile = project_keys(
        blocks, gain, kv_weight, gained_sent, key_tile
    )
    value_first = along(value_sent, FIRST)
    key_near = along(key_1, NEAR)
    key_2 = carry(key_2, key_first, [])
    key_third = along(key_2, THIRD)
    *asked, marks = ask(jobs, query, [key_2])
    asked = between(asked)
    value_0, value_1, value_2 = project_values(gained, tile, [asked[0], value_first])
    value_near = along(value_1, NEAR)
    *kept_parts, new_pool = kept(jobs, table, context_lengths, query, kv_pool, [value_1] + asked[1:], shards)
    value_third = along(carry(value_2, value_first, [kept_parts[0]]), THIRD)
    frequency = THETA ** (-(jnp.arange(HD // 2, dtype=F32) * 2.0 / HD))
    frequency = jnp.concatenate([frequency, frequency])[None, :]
    *key_out, scale, weights, share, tails = finish_keys(
        jobs, (key_0, key_near, key_first, key_third), frequency, asked, stripe, shards
    )
    key_pages = between(key_out)
    finished = finish_values(
        marks,
        (value_0, value_near, value_first, value_third),
        scale,
        weights,
        share,
        tails,
        kept_parts,
        key_pages[1:],
        shards,
    )
    value_pages = [finished[0], None, across(finished[2], 2), across(finished[3], 3)]
    packed = finished[4:]
    parts = [packed[0]] + [
        along(packed[step], [(i, i ^ step) for i in range(shards)]) for step in range(shards - 1, 0, -1)
    ]
    here = QH // shards
    *gathered, near_page = gather_parts(marks, parts, finished[1], slots * here, SENDS * here)
    fresh = [gathered[0]] + [across(gathered[step], step) for step in FRESH_ORDER[1:]]
    value_pages[1] = across(near_page, 1)
    kept_out, kept_level = blend_kept(parts, gathered[0], slots * here, SENDS * here)
    new_pool, placed = place_pages(jobs, table, new_pool, key_pages, value_pages)
    return (new_pool, combine(marks, kept_out, kept_level, fresh, placed, slots))


def solution(mesh):
    in_specs = (
        P(("outer", "rep"), "shard"),
        P("shard"),
        P("shard", None),
        P("outer", None),
        P(("outer", "rep"), None, "shard"),
        P(("outer", "rep")),
        P(("outer", "rep"), None),
        P(("outer", "rep", "shard"), None, None),
    )
    out_specs = (P(("outer", "rep", "shard"), None, None), P(("outer", "rep"), "shard"))
    fast = mesh.shape["shard"] == 4 and mesh.shape["rep"] == 4
    return jax.shard_map(
        on_device if fast else on_device_general, mesh=mesh, in_specs=in_specs, out_specs=out_specs, check_vma=False
    )
```

```python
import functools
import math

import jax
import jax.numpy as jnp
from jax import lax
from jax.experimental import pallas as pl
from jax.experimental.pallas import tpu as pltpu
from jax.sharding import PartitionSpec as P

D = 8192
QH = 64
KVH = 8
HD = 128
SENDS = 2


THETA = 500000.0
EPS = 1e-05
FLOOR_SCORE = -1e30


def rotate(key_rows, positions):
    half_dim = key_rows.shape[-1] // 2
    frequency = THETA ** (-(jnp.arange(half_dim, dtype=jnp.float32) * 2.0 / key_rows.shape[-1]))
    angles = positions.astype(jnp.float32)[:, None] * frequency[None, :]
    cosine = jnp.cos(angles)[:, None, :]
    sine_part = jnp.sin(angles)[:, None, :]
    first_half = key_rows[..., :half_dim]
    second = key_rows[..., half_dim:]
    return jnp.concatenate(
        [first_half * cosine - second * sine_part, second * cosine + first_half * sine_part],
        axis=-1,
    )


def finish(projected, inverse, positions):
    row_count = projected.shape[0]
    half_width = projected.shape[1] // 2
    scaled = projected * inverse[:, None]
    key_rows = rotate(scaled[:, :half_width].reshape(row_count, KVH, HD), positions).reshape(
        row_count, half_width
    )
    return jnp.concatenate([key_rows, scaled[:, half_width:]], axis=1).astype(jnp.bfloat16)


def spread_out(pieces, targets, replicas):
    outgoing = jnp.zeros((replicas,) + pieces.shape[1:], pieces.dtype)
    for send_index in range(SENDS):
        hit = (jnp.arange(replicas, dtype=jnp.int32) == targets[send_index])[:, None, None]
        outgoing = jnp.where(hit, pieces[send_index][None], outgoing)
    return outgoing


def on_device_general(
    hidden, norm_gain, kv_weight, restore_jobs, page_table, context_lengths, queries, kv_pool
):
    shards = lax.axis_size("shard")
    replicas = lax.axis_size("rep")
    my_replica = lax.axis_index("rep")
    my_shard = lax.axis_index("shard")
    stripe = hidden.shape[0] // SENDS
    page_len = stripe // shards
    features = hidden.shape[1]
    kv_width = kv_weight.shape[1]
    pool_pages = kv_pool.shape[0]
    destination = restore_jobs[:, 0]
    context = restore_jobs[:, 1]
    stripe_index = restore_jobs[:, 2]
    my_targets = lax.dynamic_slice_in_dim(destination, my_replica * SENDS, SENDS, 0)
    is_mine = destination == my_replica
    gain_wide = norm_gain.astype(jnp.float32)[None, :]
    page_rows = jnp.arange(page_len, dtype=jnp.int32)
    wide = hidden.astype(jnp.float32)
    squares = lax.psum(jnp.sum(wide * wide, axis=1), "shard")
    inverse = lax.rsqrt(squares / D + EPS)
    gained = (wide * gain_wide).astype(jnp.bfloat16)
    arranged = gained.reshape(SENDS, shards, page_len, features).transpose(1, 0, 2, 3)
    arranged = arranged.reshape(shards * SENDS * page_len, features)
    owned = lax.psum_scatter(
        jnp.dot(arranged, kv_weight, preferred_element_type=jnp.float32).astype(jnp.bfloat16),
        "shard",
        scatter_dimension=0,
        tiled=True,
    ).astype(jnp.float32)
    owned_inverse = lax.dynamic_slice_in_dim(
        inverse.reshape(SENDS, stripe), my_shard * page_len, page_len, 1
    )
    my_stripes = lax.dynamic_slice_in_dim(stripe_index, my_replica * SENDS, SENDS, 0)
    positions = my_stripes[:, None] * stripe + my_shard * page_len + page_rows[None, :]
    finished = finish(owned, owned_inverse.reshape(-1), positions.reshape(-1)).reshape(
        SENDS, page_len, kv_width
    )
    outgoing = spread_out(finished, my_targets, replicas)
    arrived = lax.all_to_all(outgoing, "rep", split_axis=0, concat_axis=0, tiled=True)
    mine_grid = is_mine.reshape(replicas, SENDS)
    has_page = jnp.any(mine_grid, axis=1)
    which = jnp.argmax(mine_grid.astype(jnp.int32), axis=1)
    job_index = jnp.arange(replicas, dtype=jnp.int32) * SENDS + which
    physical = jnp.where(
        has_page, page_table[context[job_index], stripe_index[job_index], 0], pool_pages
    )
    new_pool = kv_pool.at[physical].set(arrived, mode="drop")
    slots = queries.shape[0]
    pages_dev = page_table.shape[1]
    group = QH // KVH
    scale = 1.0 / math.sqrt(HD)
    cached = new_pool[page_table[:, :, 0]]
    key_rows = cached[..., : KVH * HD].reshape(slots, pages_dev * page_len, KVH, HD)
    value_rows = cached[..., KVH * HD :].reshape(slots, pages_dev * page_len, KVH, HD)
    query_rows = queries.reshape(slots, KVH, group, HD)
    scores = (
        jnp.einsum("cgmd,cpgd->cgmp", query_rows, key_rows, preferred_element_type=jnp.float32)
        * scale
    )
    position = (
        (jnp.arange(pages_dev, dtype=jnp.int32)[:, None] * shards + my_shard) * page_len
        + page_rows[None, :]
    ).reshape(-1)
    usable = (position[None, :] < context_lengths[:, None])[:, None, None, :]
    local_max = jnp.max(jnp.where(usable, scores, FLOOR_SCORE), axis=-1)
    weights = jnp.where(usable, jnp.exp(scores - local_max[..., None]), 0.0)
    denominator = jnp.sum(weights, axis=-1).reshape(slots, QH)
    numerator = jnp.einsum(
        "cgmp,cpgd->cgmd",
        weights.astype(jnp.bfloat16),
        value_rows,
        preferred_element_type=jnp.float32,
    )
    numerator = numerator.reshape(slots, QH, HD)
    local_max = local_max.reshape(slots, QH)
    heads_here = QH // shards
    row_max = lax.pmax(local_max, "shard")
    factor = jnp.exp(local_max - row_max)
    scaled_num = (numerator * factor[..., None]).reshape(slots, QH * HD)
    numerator, denominator = (
        lax.psum(scaled_num.astype(jnp.bfloat16), "shard").astype(jnp.float32),
        lax.psum((denominator * factor).astype(jnp.bfloat16), "shard").astype(jnp.float32),
    )
    numerator = lax.dynamic_slice_in_dim(numerator, my_shard * heads_here * HD, heads_here * HD, 1)
    denominator = lax.dynamic_slice_in_dim(denominator, my_shard * heads_here, heads_here, 1)
    numerator = numerator.reshape(slots, heads_here, HD)
    attention_out = numerator / denominator[..., None]
    return (new_pool, attention_out.reshape(slots, heads_here * HD).astype(jnp.bfloat16))


FIRST = [(0, 1), (3, 2), (1, 3), (2, 0)]
NEAR = [(0, 1), (1, 0), (2, 3), (3, 2)]
THIRD = [(0, 3), (3, 0), (1, 2), (2, 1)]
LANES = 128
LINES = 8
GROUP = 2
BF16 = jnp.bfloat16
F32 = jnp.float32
SMEM = pltpu.SMEM
VMEM = pltpu.VMEM
SMALL = pl.CostEstimate(flops=1, bytes_accessed=1, transcendentals=0)
LIMIT = 24 * 1024 * 1024


def whole(space=VMEM):
    return pl.BlockSpec(memory_space=space)


def row_copies(hidden, blocks, rows_in, sem):
    stripes, _, page_len, _ = hidden.shape
    return [
        pltpu.make_async_copy(
            hidden.at[stripe, block],
            rows_in.at[pl.ds((place * stripes + stripe) * page_len, page_len)],
            sem.at[place * stripes + stripe],
        )
        for place, block in enumerate(blocks)
        for stripe in range(stripes)
    ]


def scale_rows(rows_in, gained, gain_in, span):
    wide_gain = gain_in[...].astype(F32).reshape(1, gain_in.shape[0])
    gained[span] = (rows_in[span].astype(F32) * wide_gain).astype(BF16)


def put_squares(rows_in, span, out, first):
    rows = out.shape[0] - LINES
    squares = jnp.zeros((rows, LANES), F32)
    for lane in range(rows_in.shape[1] // LANES):
        part = rows_in[span, lane * LANES : (lane + 1) * LANES].astype(F32)
        squares = squares + part * part
    total = jnp.sum(squares.T, axis=0, keepdims=True)
    high = total.astype(BF16).astype(F32)
    place = lax.broadcasted_iota(jnp.int32, (LINES, LANES), 0) - first
    lines = jnp.where(place == 0, high, jnp.where(place == 1, total - high, 0.0))
    rest = jnp.zeros((LINES, out.shape[1] - LANES), F32)
    out[rows:] = jnp.concatenate([lines, rest], axis=1).astype(BF16)


def is_inner(shard):
    return (shard == 1) | (shard == 2)


def far_blocks(shard):
    lower = shard < 2
    return jnp.where(lower, 2, 1), jnp.where(lower, 3, 0)


def first_kernel(hidden, gain, weight, out, gained, tile, rows_in, gain_in, row_sem, gain_sem, tile_sem):
    shard = lax.axis_index("shard")
    half = weight.shape[1] // 2
    inner_block, outer_block = far_blocks(shard)
    rows_here = row_copies(hidden, [jnp.where(is_inner(shard), outer_block, inner_block)], rows_in, row_sem)
    piece = half // 2
    pieces = [slice(index * piece, (index + 1) * piece) for index in range(2)]
    tile_copies = [
        pltpu.make_async_copy(weight.at[:, columns], tile.at[:, columns], tile_sem.at[index])
        for index, columns in enumerate(pieces)
    ]
    gain_copy = pltpu.make_async_copy(gain, gain_in, gain_sem)
    gain_copy.start()
    for copy in rows_here + tile_copies:
        copy.start()
    gain_copy.wait()
    for copy in rows_here:
        copy.wait()
    scale_rows(rows_in, gained, gain_in, slice(None))
    put_squares(rows_in, slice(None), out, 0)
    for copy, columns in zip(tile_copies, pieces):
        copy.wait()
        product = jnp.dot(gained[...], tile[:, columns], preferred_element_type=F32)
        out[: gained.shape[0], columns] = product.astype(BF16)


def project_first(hidden, gain, weight):
    stripes, blocks, page_len, features = hidden.shape
    half = weight.shape[1] // 2
    rows = stripes * page_len
    return pl.pallas_call(
        first_kernel,
        in_specs=[whole(pl.ANY)] * 3,
        out_specs=[whole()] * 3,
        out_shape=[
            jax.ShapeDtypeStruct((rows + LINES, half), BF16),
            jax.ShapeDtypeStruct((rows, features), BF16),
            jax.ShapeDtypeStruct((features, half), BF16),
        ],
        scratch_shapes=[
            pltpu.VMEM((rows, features), BF16),
            pltpu.VMEM((features,), BF16),
            pltpu.SemaphoreType.DMA((stripes,)),
            pltpu.SemaphoreType.DMA,
            pltpu.SemaphoreType.DMA((2,)),
        ],
        compiler_params=pltpu.CompilerParams(vmem_limit_bytes=LIMIT),
        cost_estimate=SMALL,
        name="project_first",
    )(hidden, gain, weight)


def head_spread(query, width):
    heads = query.shape[0]
    group = heads // (width // LANES)
    head = lax.broadcasted_iota(jnp.int32, (heads, LANES), 0)
    pieces = [jnp.where(head // group == g, query, jnp.zeros_like(query)) for g in range(width // LANES)]
    return jnp.concatenate(pieces, axis=1)


def head_pick(products):
    heads, width = products.shape
    group = heads // (width // LANES)
    head = lax.broadcasted_iota(jnp.int32, (heads, LANES), 0)
    picked = products[:, :LANES]
    for g in range(1, width // LANES):
        picked = jnp.where(head // group == g, products[:, g * LANES : (g + 1) * LANES], picked)
    return picked


def score(query, key_rows):
    spread = head_spread(query, key_rows.shape[1])
    scores = lax.dot_general(spread, key_rows, (((1,), (1,)), ((), ())), preferred_element_type=F32)
    return scores * (1.0 / math.sqrt(LANES))


def attend(query, key_rows, value_rows, usable):
    scores = jnp.where(usable, score(query, key_rows), FLOOR_SCORE)
    largest = jnp.max(scores, axis=1, keepdims=True)
    weights = jnp.where(usable, jnp.exp(scores - largest), 0.0)
    total = jnp.sum(weights, axis=1, keepdims=True)
    picked = head_pick(jnp.dot(weights.astype(BF16), value_rows, preferred_element_type=F32))
    some = total > 0.0
    safe = jnp.where(some, total, 1.0)
    return picked / safe, jnp.where(some, largest + jnp.log(safe), FLOOR_SCORE)


def split_lines(lines, first):
    high = lines.astype(BF16).astype(F32)
    middle_part = (lines - high).astype(BF16).astype(F32)
    low = lines - high - middle_part
    place = lax.broadcasted_iota(jnp.int32, lines.shape, 0) - first
    return jnp.where(place == 0, high, jnp.where(place == 1, middle_part, jnp.where(place == 2, low, 0.0)))


def join_lines(tail, first, rows):
    line = jnp.sum(tail[first : first + 3].astype(F32), axis=0, keepdims=True)
    return jnp.broadcast_to(line, (LANES, LANES)).T[:rows]


def project_keys_kernel(hidden, gain, weight, sent, key_tile, *rest):
    own, near, third, values, gained, value_tile = rest[:6]
    rows_in, gain_in, row_sem, gain_sem, tile_sem = rest[6:]
    shard = lax.axis_index("shard")
    rows = values.shape[0]
    half = weight.shape[1] // 2
    inner_block, outer_block = far_blocks(shard)
    blocks = [shard, jnp.bitwise_xor(shard, 1), jnp.where(is_inner(shard), inner_block, outer_block)]
    rows_here = row_copies(hidden, blocks, rows_in, row_sem)
    tile_copy = pltpu.make_async_copy(weight.at[:, pl.ds(half, half)], value_tile, tile_sem)
    gain_copy = pltpu.make_async_copy(gain, gain_in, gain_sem)
    gain_copy.start()
    for copy in rows_here + [tile_copy]:
        copy.start()
    gain_copy.wait()
    for copy in rows_here:
        copy.wait()
    scale_rows(rows_in, gained, gain_in, slice(None))
    for place, ref in enumerate((own, near, third)):
        span = slice(place * rows, (place + 1) * rows)
        put_squares(rows_in, span, ref, 2 if place == 2 else 0)
    product = jnp.dot(gained[...], key_tile[...], preferred_element_type=F32).astype(BF16)
    for place, ref in enumerate((own, near, third)):
        ref[:rows] = product[place * rows : (place + 1) * rows]
    tile_copy.wait()
    values[...] = jnp.dot(sent[...], value_tile[...], preferred_element_type=F32).astype(BF16)


def project_keys(hidden, gain, weight, sent, tile):
    stripes, blocks, page_len, features = hidden.shape
    half = weight.shape[1] // 2
    rows = stripes * page_len
    return pl.pallas_call(
        project_keys_kernel,
        in_specs=[whole(pl.ANY)] * 3 + [whole()] * 2,
        out_specs=[whole()] * 6,
        out_shape=[jax.ShapeDtypeStruct((rows + LINES, half), BF16)] * 3
        + [
            jax.ShapeDtypeStruct((rows, half), BF16),
            jax.ShapeDtypeStruct((3 * rows, features), BF16),
            jax.ShapeDtypeStruct((features, half), BF16),
        ],
        scratch_shapes=[
            pltpu.VMEM((3 * rows, features), BF16),
            pltpu.VMEM((features,), BF16),
            pltpu.SemaphoreType.DMA((3 * stripes,)),
            pltpu.SemaphoreType.DMA,
            pltpu.SemaphoreType.DMA,
        ],
        compiler_params=pltpu.CompilerParams(vmem_limit_bytes=LIMIT),
        cost_estimate=SMALL,
        name="project_keys",
    )(hidden, gain, weight, sent, tile)


def project_values_kernel(gained, tile, *rest):
    product = jnp.dot(gained[...], tile[...], preferred_element_type=F32).astype(BF16)
    rows = rest[-1].shape[0]
    for place, ref in enumerate(rest[-3:]):
        ref[...] = product[place * rows : (place + 1) * rows]


def project_values(gained, tile, after):
    return pl.pallas_call(
        project_values_kernel,
        in_specs=[whole()] * 2 + [whole(pl.ANY)] * len(after),
        out_specs=[whole()] * 3,
        out_shape=[jax.ShapeDtypeStruct((gained.shape[0] // 3, tile.shape[1]), BF16)] * 3,
        compiler_params=pltpu.CompilerParams(vmem_limit_bytes=LIMIT),
        cost_estimate=SMALL,
        name="project_values",
    )(gained, tile, *after)


def carry_kernel(mine, first, *rest):
    inner = is_inner(lax.axis_index("shard"))
    arrived = jnp.where(inner, first[...].astype(F32), 0.0)
    rest[-1][...] = (mine[...].astype(F32) + arrived).astype(BF16)


def carry(mine, first, after):
    return pl.pallas_call(
        carry_kernel,
        in_specs=[whole(), whole()] + [whole(pl.ANY)] * len(after),
        out_specs=whole(),
        out_shape=jax.ShapeDtypeStruct(mine.shape, BF16),
        compiler_params=pltpu.CompilerParams(vmem_limit_bytes=LIMIT),
        cost_estimate=SMALL,
        name="carry",
    )(mine, first, *after)


def rep_shapes(rows, width):
    return [jax.ShapeDtypeStruct((rows, width), BF16)] * 4


def ask_kernel(jobs, table, query, *rest):
    outs, marks, places = rest[-6:-2], rest[-2], rest[-1]
    slots = query.shape[0]
    replica = lax.axis_index("rep")
    line = lax.broadcasted_iota(jnp.int32, marks.shape, 0)
    found = jnp.zeros(marks.shape, jnp.int32)
    place_line = lax.broadcasted_iota(jnp.int32, places.shape, 0)
    spots = jnp.full(places.shape, -1, jnp.int32)
    for step, out in enumerate(outs):
        hit, context, page = job_from(jobs, step)
        out[...] = query[context]
        sent = jobs[0, replica * SENDS] == jnp.bitwise_xor(replica, step)
        found = found + jnp.where(line == step * slots + context, hit.astype(jnp.int32), 0)
        found = found + jnp.where(line == 4 * slots + step, sent.astype(jnp.int32), 0)
        spots = jnp.where(place_line == step, jnp.where(hit, table[page, context], -1), spots)
    marks[...] = found.astype(F32)
    places[...] = spots


def ask(jobs, table, query, after):
    return pl.pallas_call(
        ask_kernel,
        in_specs=[whole(SMEM)] * 2 + [whole()] + [whole(pl.ANY)] * len(after),
        out_specs=[whole()] * 6,
        out_shape=rep_shapes(*query.shape[1:])
        + [
            jax.ShapeDtypeStruct((4 * query.shape[0] + 8, LANES), F32),
            jax.ShapeDtypeStruct((8, LANES), jnp.int32),
        ],
        compiler_params=pltpu.CompilerParams(vmem_limit_bytes=LIMIT),
        cost_estimate=SMALL,
        name="ask",
    )(jobs, table, query, *after)


def kept_kernel(jobs, table, lengths, query, pool, *rest, shards, after):
    outs = rest[after : after + 4]
    new_pool, pages, total, level, in_sem, out_sem = rest[after + 4 :]
    slots, heads, _ = query.shape
    here = heads // shards
    rows = slots * here
    replica = lax.axis_index("rep")
    shard = lax.axis_index("shard")
    page_len = pool.shape[1]
    half = pool.shape[2] // 2

    def copy_in(context, page):
        place = context * 2 + page
        return pltpu.make_async_copy(pool.at[table[page, context]], pages.at[place], in_sem.at[place])

    def copy_out(context, page):
        place = context * 2 + page
        return pltpu.make_async_copy(pages.at[place], new_pool.at[table[page, context]], out_sem.at[place])

    @pl.loop(0, slots)
    def _(context):
        for page in range(2):
            copy_in(context, page).start()

    lane = lax.broadcasted_iota(jnp.int32, (heads, 2 * page_len), 1)
    page_of = lane // page_len
    position = (page_of * shards + shard) * page_len + lane % page_len

    def context_part(context):
        gone = [jnp.int32(0), jnp.int32(0)]
        for job in range(jobs.shape[1]):
            hit = (jobs[0, job] == replica) & (jobs[1, job] == context)
            for page in range(2):
                gone[page] = gone[page] | (hit & (jobs[2, job] == page)).astype(jnp.int32)
        usable = (position < lengths[context]) & (jnp.where(page_of == 0, gone[0], gone[1]) == 0)
        both = pages[pl.ds(context * 2, 2)].reshape(2 * page_len, 2 * half)
        return attend(query[context], both[:, :half], both[:, half:], usable)

    @pl.loop(0, slots // GROUP)
    def _(index):
        contexts = [index * GROUP + member for member in range(GROUP)]
        for context in contexts:
            for page in range(2):
                copy_in(context, page).wait()
                copy_out(context, page).start()
        results = [context_part(context) for context in contexts]
        for context, (result, logarithm) in zip(contexts, results):
            total[context] = result
            level[context] = jnp.broadcast_to(logarithm, result.shape)

    for step, out in enumerate(outs):
        start = pl.multiple_of(jnp.bitwise_xor(shard, step) * here, here)
        out[:rows] = total[:, pl.ds(start, here), :].reshape(rows, LANES).astype(BF16)
        lines = level[:, pl.ds(start, here), :].reshape(rows, LANES).T[:16]
        out[rows:] = split_lines(lines, 0).astype(BF16)

    @pl.loop(0, slots)
    def _(context):
        for page in range(2):
            copy_out(context, page).wait()


def kept(jobs, table, lengths, query, pool, after, shards):
    slots, heads, size = query.shape
    return pl.pallas_call(
        functools.partial(kept_kernel, shards=shards, after=len(after)),
        in_specs=[whole(SMEM)] * 3 + [whole()] + [whole(pl.ANY)] * (1 + len(after)),
        out_specs=[whole()] * 4 + [whole(pl.ANY)],
        out_shape=[jax.ShapeDtypeStruct((slots * heads // shards + 16, size), BF16)] * 4
        + [jax.ShapeDtypeStruct(pool.shape, pool.dtype)],
        scratch_shapes=[
            pltpu.VMEM((slots * 2,) + pool.shape[1:], pool.dtype),
            pltpu.VMEM(query.shape, F32),
            pltpu.VMEM(query.shape, F32),
            pltpu.SemaphoreType.DMA((slots * 2,)),
            pltpu.SemaphoreType.DMA((slots * 2,)),
        ],
        compiler_params=pltpu.CompilerParams(vmem_limit_bytes=LIMIT),
        cost_estimate=SMALL,
        name="kept",
    )(jobs, table, lengths, query, pool, *after)


def route(jobs, finished, outs):
    replica = lax.axis_index("rep")
    page_len = finished.shape[0] // SENDS
    for step, out in enumerate(outs):
        chosen = jobs[0, replica * SENDS] == jnp.bitwise_xor(replica, step)

        @pl.when(chosen)
        def _():
            out[...] = finished[:page_len]

        @pl.when(jnp.logical_not(chosen))
        def _():
            out[...] = finished[page_len:]


def add_parts(own, near, first, third, rows, columns):
    direct = jnp.where(is_inner(lax.axis_index("shard")), 0.0, first[rows, columns].astype(F32))
    parts = [ref[rows, columns].astype(F32) for ref in (own, near, third)]
    return (parts[0] + parts[1]) + (parts[2] + direct)


def finish_keys_kernel(jobs, own, near, first, third, frequency, *rest, stripe):
    asked, outs = rest[:4], rest[4:8]
    scale, weights_out, share, tails, finished, level = rest[8:]
    replica = lax.axis_index("rep")
    shard = lax.axis_index("shard")
    rows, width = finished.shape
    page_len = rows // SENDS

    def added(span, columns):
        return add_parts(own, near, first, third, span, columns)

    squares = jnp.sum(added(slice(rows, rows + LINES), slice(0, LANES)), axis=0, keepdims=True)
    squares = jnp.broadcast_to(squares, (LANES, LANES)).T[:rows]
    inverse = lax.rsqrt(squares / D + EPS)
    scale[...] = inverse
    row = lax.broadcasted_iota(jnp.int32, (rows, LANES), 0)
    lane = lax.broadcasted_iota(jnp.int32, (rows, LANES), 1)
    index = jnp.where(row < page_len, jobs[2, replica * SENDS], jobs[2, replica * SENDS + 1])
    position = index * stripe + shard * page_len + row % page_len
    angle = position.astype(F32) * frequency[...]
    cosine = jnp.cos(angle) * inverse
    sine_part = jnp.where(lane < LANES // 2, -jnp.sin(angle), jnp.sin(angle)) * inverse
    for head in range(width // LANES):
        columns = slice(head * LANES, (head + 1) * LANES)
        value = added(slice(0, rows), columns)
        turned = value * cosine + pltpu.roll(value, LANES // 2, 1) * sine_part
        finished[:, columns] = turned.astype(BF16)
    route(jobs, finished, outs)
    for send in range(SENDS):
        step = jnp.bitwise_xor(jobs[0, replica * SENDS + send], replica)
        query = asked[0][...]
        for other in range(1, 4):
            query = jnp.where(step == other, asked[other][...], query)
        scores = score(query, finished[send * page_len : (send + 1) * page_len])
        largest = jnp.max(scores, axis=1, keepdims=True)
        weights = jnp.exp(scores - largest)
        total = jnp.sum(weights, axis=1, keepdims=True)
        weights_out[send] = weights.astype(BF16)
        share[send] = jnp.broadcast_to(1.0 / total, share.shape[1:])
        level[send] = jnp.broadcast_to(largest + jnp.log(total), level.shape[1:])
    here = level.shape[1] // tails.shape[0]
    count = SENDS * here
    for step in range(tails.shape[0]):
        start = pl.multiple_of(jnp.bitwise_xor(shard, step) * here, here)
        mine = level[:, pl.ds(start, here), :].reshape(count, LANES)
        around = [jnp.zeros((rows_, LANES), F32) for rows_ in (step * count, LANES - (step + 1) * count)]
        pieces = [piece for piece in (around[0], mine, around[1]) if piece.shape[0]]
        tails[step] = split_lines(jnp.concatenate(pieces, axis=0).T[:16], 3)


def finish_values_kernel(marks, own, near, first, third, scale, weights, share, tails, *rest, shards, after):
    kept_parts, outs = rest[:4], rest[4 + after : 8 + after]
    packed, finished, result = rest[8 + after : 12 + after], rest[12 + after], rest[13 + after]
    shard = lax.axis_index("shard")
    page_len = own.shape[0] // SENDS
    sent = [marks[marks.shape[0] - 8 + step : marks.shape[0] - 7 + step] > 0.0 for step in range(4)]
    for head in range(own.shape[1] // LANES):
        columns = slice(head * LANES, (head + 1) * LANES)
        total = add_parts(own, near, first, third, slice(None), columns) * scale[...]
        finished[:, columns] = total.astype(BF16)
        for step, out in enumerate(outs):
            out[:, columns] = jnp.where(sent[step], total[:page_len], total[page_len:]).astype(BF16)
    for send in range(SENDS):
        products = jnp.dot(
            weights[send], finished[send * page_len : (send + 1) * page_len], preferred_element_type=F32
        )
        result[send] = head_pick(products) * share[send]
    here = share.shape[1] // shards
    count = SENDS * here
    rows = kept_parts[0].shape[0] - 16
    for step in range(4):
        start = pl.multiple_of(jnp.bitwise_xor(shard, step) * here, here)
        packed[step][:rows] = kept_parts[step][:rows]
        packed[step][rows : rows + count] = result[:, pl.ds(start, here), :].reshape(count, LANES).astype(BF16)
        packed[step][rows + count :] = (kept_parts[step][rows:].astype(F32) + tails[step]).astype(BF16)


def finish_keys(jobs, parts, frequency, asked, stripe, shards):
    rows, width = parts[0].shape[0] - LINES, parts[0].shape[1]
    heads = asked[0].shape[0]
    page_len = rows // SENDS
    return pl.pallas_call(
        functools.partial(finish_keys_kernel, stripe=stripe),
        in_specs=[whole(SMEM)] + [whole()] * 9,
        out_specs=[whole()] * 8,
        out_shape=rep_shapes(page_len, width)
        + [
            jax.ShapeDtypeStruct((rows, LANES), F32),
            jax.ShapeDtypeStruct((SENDS, heads, page_len), BF16),
            jax.ShapeDtypeStruct((SENDS, heads, LANES), F32),
            jax.ShapeDtypeStruct((shards, 16, LANES), F32),
        ],
        scratch_shapes=[pltpu.VMEM((rows, width), BF16), pltpu.VMEM((SENDS, heads, LANES), F32)],
        compiler_params=pltpu.CompilerParams(vmem_limit_bytes=LIMIT),
        cost_estimate=SMALL,
        name="finish_keys",
    )(jobs, *parts, frequency, *asked)


def finish_values(marks, parts, scale, weights, share, tails, kept_parts, after, shards):
    rows, width = parts[0].shape
    heads = share.shape[1]
    page_len = rows // SENDS
    packed = kept_parts[0].shape[0] + SENDS * heads // shards
    return pl.pallas_call(
        functools.partial(finish_values_kernel, shards=shards, after=len(after)),
        in_specs=[whole()] * 13 + [whole(pl.ANY)] * len(after),
        out_specs=[whole()] * 8,
        out_shape=rep_shapes(page_len, width) + [jax.ShapeDtypeStruct((packed, LANES), BF16)] * 4,
        scratch_shapes=[pltpu.VMEM((rows, width), BF16), pltpu.VMEM((SENDS, heads, LANES), F32)],
        compiler_params=pltpu.CompilerParams(vmem_limit_bytes=LIMIT),
        cost_estimate=SMALL,
        name="finish_values",
    )(marks, *parts, scale, weights, share, tails, *kept_parts, *after)


def job_from(jobs, step):
    replica = lax.axis_index("rep")
    first = jnp.bitwise_xor(replica, step) * SENDS
    hit_first = jobs[0, first] == replica
    hit = hit_first | (jobs[0, first + 1] == replica)
    row = jnp.where(hit_first, first, first + 1)
    return hit, jobs[1, row], jobs[2, row]


def place_kernel(places, pool, *rest):
    key_pages, value_pages = rest[:4], rest[4:8]
    out, done, pages, sem = rest[8:]
    half = key_pages[0].shape[1]
    spots = [jnp.max(places[step : step + 1]) for step in range(4)]
    done[...] = jnp.zeros_like(done)
    for wait in (False, True):
        for step, spot in enumerate(spots):

            @pl.when(spot >= 0)
            def _():
                copy = pltpu.make_async_copy(pages.at[step], out.at[spot], sem.at[step])
                if wait:
                    copy.wait()
                else:
                    pages[step, :, :half] = key_pages[step][...]
                    pages[step, :, half:] = value_pages[step][...]
                    copy.start()


def place_pages(places, pool, key_pages, value_pages):
    return pl.pallas_call(
        place_kernel,
        in_specs=[whole(), whole(pl.ANY)] + [whole()] * 8,
        out_specs=[whole(pl.ANY), whole()],
        out_shape=[jax.ShapeDtypeStruct(pool.shape, pool.dtype), jax.ShapeDtypeStruct((16, LANES), BF16)],
        scratch_shapes=[pltpu.VMEM((4,) + pool.shape[1:], pool.dtype), pltpu.SemaphoreType.DMA((4,))],
        input_output_aliases={1: 0},
        compiler_params=pltpu.CompilerParams(vmem_limit_bytes=LIMIT),
        cost_estimate=SMALL,
        name="place_pages",
    )(places, pool, *key_pages, *value_pages)


def blend(parts, levels):
    top = functools.reduce(jnp.maximum, levels)
    shares = [jnp.exp(level - top) for level in levels]
    both = functools.reduce(jnp.add, shares)
    total = functools.reduce(jnp.add, [part * share for part, share in zip(parts, shares)])
    return total / both, top + jnp.log(both)


def gather_kernel(marks, *refs, rows, count):
    parts, page, outs, page_out = refs[:4], refs[4], refs[5:9], refs[9]
    page_out[...] = page[...]
    tail = functools.reduce(jnp.add, [ref[rows + count :].astype(F32) for ref in parts])
    levels = join_lines(tail, 3, LANES)
    mixed, level = blend(
        [ref[rows : rows + count].astype(F32) for ref in parts],
        [levels[step * count : (step + 1) * count] for step in (0, 2, 3, 1)],
    )
    here = count // SENDS
    lane = lax.broadcasted_iota(jnp.int32, (here, LANES), 1)
    for step, out in enumerate(outs):
        chosen = marks[marks.shape[0] - 8 + step : marks.shape[0] - 7 + step] > 0.0
        total = jnp.where(chosen, level[:here], level[here:])
        high = total.astype(BF16).astype(F32)
        middle_part = (total - high).astype(BF16).astype(F32)
        low = total - high - middle_part
        out[:, :LANES] = jnp.where(chosen, mixed[:here], mixed[here:]).astype(BF16)
        out[:, LANES:] = jnp.where(
            lane == 0, high, jnp.where(lane == 1, middle_part, jnp.where(lane == 2, low, 0.0))
        ).astype(BF16)


def gather_parts(marks, parts, page, rows, count):
    return pl.pallas_call(
        functools.partial(gather_kernel, rows=rows, count=count),
        in_specs=[whole()] * 6,
        out_specs=[whole()] * 5,
        out_shape=rep_shapes(count // SENDS, 2 * LANES) + [jax.ShapeDtypeStruct(page.shape, BF16)],
        compiler_params=pltpu.CompilerParams(vmem_limit_bytes=LIMIT),
        cost_estimate=SMALL,
        name="gather_parts",
    )(marks, *parts, page)


def blend_kernel(*refs, rows, count):
    parts, after, kept_out, kept_level = refs[:4], refs[4], refs[5], refs[6]
    mixed, level = blend(
        [ref[:rows].astype(F32) for ref in parts], [join_lines(ref[rows + count :], 0, rows) for ref in parts]
    )
    kept_out[...] = mixed
    kept_level[...] = level


def blend_kept(parts, after, rows, count):
    return pl.pallas_call(
        functools.partial(blend_kernel, rows=rows, count=count),
        in_specs=[whole()] * 4 + [whole(pl.ANY)],
        out_specs=[whole()] * 2,
        out_shape=[jax.ShapeDtypeStruct((rows, LANES), F32)] * 2,
        compiler_params=pltpu.CompilerParams(vmem_limit_bytes=LIMIT),
        cost_estimate=SMALL,
        name="blend_kept",
    )(*parts, after)


FRESH_ORDER = (0, 2, 3, 1)


def combine_kernel(marks, kept_out, kept_level, *refs):
    parts, out, mixed = refs[:4], refs[5], refs[6]
    slots, here, size = mixed.shape
    spans = [slice(context * here, (context + 1) * here) for context in range(slots)]
    blended = []
    for step, ref in zip(FRESH_ORDER, parts):
        hits = [marks[step * slots + context : step * slots + context + 1] > 0.0 for context in range(slots)]
        old, old_level = jnp.zeros((here, size), F32), jnp.zeros((here, size), F32)
        for hit, span in zip(hits, spans):
            old = jnp.where(hit, kept_out[span], old)
            old_level = jnp.where(hit, kept_level[span], old_level)
        fresh_level = jnp.sum(ref[:, LANES:].astype(F32), axis=1, keepdims=True)
        fresh_level = jnp.broadcast_to(fresh_level, (here, size))
        result, _ = blend([old, ref[:, :LANES].astype(F32)], [old_level, fresh_level])
        blended.append((hits, result))
    for context, span in enumerate(spans):
        total = kept_out[span]
        for hits, result in blended:
            total = jnp.where(hits[context], result, total)
        mixed[context] = total
    for head in range(here):
        out[:, head * size : (head + 1) * size] = mixed[:, head, :].astype(BF16)


def combine(marks, kept_out, kept_level, parts, after, slots):
    here = kept_out.shape[0] // slots
    return pl.pallas_call(
        combine_kernel,
        in_specs=[whole()] * 7 + [whole(pl.ANY)],
        out_specs=whole(),
        out_shape=jax.ShapeDtypeStruct((slots, here * LANES), BF16),
        scratch_shapes=[pltpu.VMEM((slots, here, LANES), F32)],
        compiler_params=pltpu.CompilerParams(vmem_limit_bytes=LIMIT),
        cost_estimate=SMALL,
        name="combine",
    )(marks, kept_out, kept_level, *parts, after)


def on_device(
    hidden, norm_gain, kv_weight, restore_jobs, page_table, context_lengths, queries, kv_pool
):
    shards = lax.axis_size("shard")
    replicas = lax.axis_size("rep")
    stripe = hidden.shape[0] // SENDS
    page_len = stripe // shards
    kv_weight = pltpu.with_memory_space_constraint(kv_weight, pltpu.HBM)
    kv_pool = pltpu.with_memory_space_constraint(kv_pool, pltpu.HBM)
    gain = pltpu.with_memory_space_constraint(norm_gain, pltpu.HBM)
    blocks = pltpu.with_memory_space_constraint(
        hidden.reshape(SENDS, shards, page_len, hidden.shape[1]), pltpu.HBM
    )
    jobs = restore_jobs.T
    table = page_table[:, :, 0].T
    slots = queries.shape[0]
    query = queries.reshape(slots, QH, HD)

    def along(array, pairs):
        return lax.ppermute(array, "shard", pairs)

    def across(array, step):
        return lax.ppermute(array, "rep", [(i, i ^ step) for i in range(replicas)])

    def between(arrays):
        return [arrays[0]] + [across(arrays[step], step) for step in range(1, replicas)]

    key_sent, gained_sent, key_tile = project_first(blocks, gain, kv_weight)
    key_first = along(key_sent, FIRST)
    key_0, key_1, key_2, value_sent, gained, tile = project_keys(
        blocks, gain, kv_weight, gained_sent, key_tile
    )
    value_first = along(value_sent, FIRST)
    key_near = along(key_1, NEAR)
    key_2 = carry(key_2, key_first, [])
    key_third = along(key_2, THIRD)
    *asked, marks, places = ask(jobs, table, query, [key_2])
    asked = between(asked)
    value_0, value_1, value_2 = project_values(gained, tile, [asked[0], value_first])
    value_near = along(value_1, NEAR)
    value_2 = carry(value_2, value_first, asked[1:])
    value_third = along(value_2, THIRD)
    *kept_parts, new_pool = kept(jobs, table, context_lengths, query, kv_pool, [value_2], shards)
    frequency = THETA ** (-(jnp.arange(HD // 2, dtype=F32) * 2.0 / HD))
    frequency = jnp.concatenate([frequency, frequency])[None, :]
    *key_out, scale, weights, share, tails = finish_keys(
        jobs, (key_0, key_near, key_first, key_third), frequency, asked, stripe, shards
    )
    key_pages = between(key_out)
    finished = finish_values(
        marks,
        (value_0, value_near, value_first, value_third),
        scale,
        weights,
        share,
        tails,
        kept_parts,
        key_pages[1:],
        shards,
    )
    value_pages = [finished[0], None, across(finished[2], 2), across(finished[3], 3)]
    packed = finished[4:]
    parts = [packed[0]] + [
        along(packed[step], [(i, i ^ step) for i in range(shards)]) for step in (2, 3, 1)
    ]
    here = QH // shards
    *gathered, near_page = gather_parts(marks, parts, finished[1], slots * here, SENDS * here)
    fresh = [gathered[0]] + [across(gathered[step], step) for step in FRESH_ORDER[1:]]
    value_pages[1] = across(near_page, 1)
    kept_out, kept_level = blend_kept(parts, gathered[0], slots * here, SENDS * here)
    new_pool, placed = place_pages(places, new_pool, key_pages, value_pages)
    return (new_pool, combine(marks, kept_out, kept_level, fresh, placed, slots))


def solution(mesh):
    in_specs = (
        P(("outer", "rep"), "shard"),
        P("shard"),
        P("shard", None),
        P("outer", None),
        P(("outer", "rep"), None, "shard"),
        P(("outer", "rep")),
        P(("outer", "rep"), None),
        P(("outer", "rep", "shard"), None, None),
    )
    out_specs = (P(("outer", "rep", "shard"), None, None), P(("outer", "rep"), "shard"))
    fast = mesh.shape["shard"] == 4 and mesh.shape["rep"] == 4
    return jax.shard_map(
        on_device if fast else on_device_general, mesh=mesh, in_specs=in_specs, out_specs=out_specs, check_vma=False
    )
```

```python
import functools
import math

import jax
import jax.numpy as jnp
from jax import lax
from jax.experimental import pallas as pl
from jax.experimental.pallas import tpu as pltpu
from jax.sharding import PartitionSpec as P

D = 8192
QH = 64
KVH = 8
HD = 128
SENDS = 2


THETA = 500000.0
EPS = 1e-05
FLOOR_SCORE = -1e30


def rotate(key_rows, positions):
    half_dim = key_rows.shape[-1] // 2
    frequency = THETA ** (-(jnp.arange(half_dim, dtype=jnp.float32) * 2.0 / key_rows.shape[-1]))
    angles = positions.astype(jnp.float32)[:, None] * frequency[None, :]
    cosine = jnp.cos(angles)[:, None, :]
    sine_part = jnp.sin(angles)[:, None, :]
    first_half = key_rows[..., :half_dim]
    second = key_rows[..., half_dim:]
    return jnp.concatenate(
        [first_half * cosine - second * sine_part, second * cosine + first_half * sine_part],
        axis=-1,
    )


def finish(projected, inverse, positions):
    row_count = projected.shape[0]
    half_width = projected.shape[1] // 2
    scaled = projected * inverse[:, None]
    key_rows = rotate(scaled[:, :half_width].reshape(row_count, KVH, HD), positions).reshape(
        row_count, half_width
    )
    return jnp.concatenate([key_rows, scaled[:, half_width:]], axis=1).astype(jnp.bfloat16)


def spread_out(pieces, targets, replicas):
    outgoing = jnp.zeros((replicas,) + pieces.shape[1:], pieces.dtype)
    for send_index in range(SENDS):
        hit = (jnp.arange(replicas, dtype=jnp.int32) == targets[send_index])[:, None, None]
        outgoing = jnp.where(hit, pieces[send_index][None], outgoing)
    return outgoing


def on_device_general(
    hidden, norm_gain, kv_weight, restore_jobs, page_table, context_lengths, queries, kv_pool
):
    shards = lax.axis_size("shard")
    replicas = lax.axis_size("rep")
    my_replica = lax.axis_index("rep")
    my_shard = lax.axis_index("shard")
    stripe = hidden.shape[0] // SENDS
    page_len = stripe // shards
    features = hidden.shape[1]
    kv_width = kv_weight.shape[1]
    pool_pages = kv_pool.shape[0]
    destination = restore_jobs[:, 0]
    context = restore_jobs[:, 1]
    stripe_index = restore_jobs[:, 2]
    my_targets = lax.dynamic_slice_in_dim(destination, my_replica * SENDS, SENDS, 0)
    is_mine = destination == my_replica
    gain_wide = norm_gain.astype(jnp.float32)[None, :]
    page_rows = jnp.arange(page_len, dtype=jnp.int32)
    wide = hidden.astype(jnp.float32)
    squares = lax.psum(jnp.sum(wide * wide, axis=1), "shard")
    inverse = lax.rsqrt(squares / D + EPS)
    gained = (wide * gain_wide).astype(jnp.bfloat16)
    arranged = gained.reshape(SENDS, shards, page_len, features).transpose(1, 0, 2, 3)
    arranged = arranged.reshape(shards * SENDS * page_len, features)
    owned = lax.psum_scatter(
        jnp.dot(arranged, kv_weight, preferred_element_type=jnp.float32).astype(jnp.bfloat16),
        "shard",
        scatter_dimension=0,
        tiled=True,
    ).astype(jnp.float32)
    owned_inverse = lax.dynamic_slice_in_dim(
        inverse.reshape(SENDS, stripe), my_shard * page_len, page_len, 1
    )
    my_stripes = lax.dynamic_slice_in_dim(stripe_index, my_replica * SENDS, SENDS, 0)
    positions = my_stripes[:, None] * stripe + my_shard * page_len + page_rows[None, :]
    finished = finish(owned, owned_inverse.reshape(-1), positions.reshape(-1)).reshape(
        SENDS, page_len, kv_width
    )
    outgoing = spread_out(finished, my_targets, replicas)
    arrived = lax.all_to_all(outgoing, "rep", split_axis=0, concat_axis=0, tiled=True)
    mine_grid = is_mine.reshape(replicas, SENDS)
    has_page = jnp.any(mine_grid, axis=1)
    which = jnp.argmax(mine_grid.astype(jnp.int32), axis=1)
    job_index = jnp.arange(replicas, dtype=jnp.int32) * SENDS + which
    physical = jnp.where(
        has_page, page_table[context[job_index], stripe_index[job_index], 0], pool_pages
    )
    new_pool = kv_pool.at[physical].set(arrived, mode="drop")
    slots = queries.shape[0]
    pages_dev = page_table.shape[1]
    group = QH // KVH
    scale = 1.0 / math.sqrt(HD)
    cached = new_pool[page_table[:, :, 0]]
    key_rows = cached[..., : KVH * HD].reshape(slots, pages_dev * page_len, KVH, HD)
    value_rows = cached[..., KVH * HD :].reshape(slots, pages_dev * page_len, KVH, HD)
    query_rows = queries.reshape(slots, KVH, group, HD)
    scores = (
        jnp.einsum("cgmd,cpgd->cgmp", query_rows, key_rows, preferred_element_type=jnp.float32)
        * scale
    )
    position = (
        (jnp.arange(pages_dev, dtype=jnp.int32)[:, None] * shards + my_shard) * page_len
        + page_rows[None, :]
    ).reshape(-1)
    usable = (position[None, :] < context_lengths[:, None])[:, None, None, :]
    local_max = jnp.max(jnp.where(usable, scores, FLOOR_SCORE), axis=-1)
    weights = jnp.where(usable, jnp.exp(scores - local_max[..., None]), 0.0)
    denominator = jnp.sum(weights, axis=-1).reshape(slots, QH)
    numerator = jnp.einsum(
        "cgmp,cpgd->cgmd",
        weights.astype(jnp.bfloat16),
        value_rows,
        preferred_element_type=jnp.float32,
    )
    numerator = numerator.reshape(slots, QH, HD)
    local_max = local_max.reshape(slots, QH)
    heads_here = QH // shards
    row_max = lax.pmax(local_max, "shard")
    factor = jnp.exp(local_max - row_max)
    scaled_num = (numerator * factor[..., None]).reshape(slots, QH * HD)
    numerator, denominator = (
        lax.psum(scaled_num.astype(jnp.bfloat16), "shard").astype(jnp.float32),
        lax.psum((denominator * factor).astype(jnp.bfloat16), "shard").astype(jnp.float32),
    )
    numerator = lax.dynamic_slice_in_dim(numerator, my_shard * heads_here * HD, heads_here * HD, 1)
    denominator = lax.dynamic_slice_in_dim(denominator, my_shard * heads_here, heads_here, 1)
    numerator = numerator.reshape(slots, heads_here, HD)
    attention_out = numerator / denominator[..., None]
    return (new_pool, attention_out.reshape(slots, heads_here * HD).astype(jnp.bfloat16))


FIRST = [(0, 1), (3, 2), (1, 3), (2, 0)]
NEAR = [(0, 1), (1, 0), (2, 3), (3, 2)]
THIRD = [(0, 3), (3, 0), (1, 2), (2, 1)]
LANES = 128
LINES = 8
GROUP = 2
BF16 = jnp.bfloat16
F32 = jnp.float32
SMEM = pltpu.SMEM
VMEM = pltpu.VMEM
SMALL = pl.CostEstimate(flops=1, bytes_accessed=1, transcendentals=0)
LIMIT = 24 * 1024 * 1024


def whole(space=VMEM):
    return pl.BlockSpec(memory_space=space)


def row_copies(hidden, blocks, rows_in, sem):
    stripes, _, page_len, _ = hidden.shape
    return [
        pltpu.make_async_copy(
            hidden.at[stripe, block],
            rows_in.at[pl.ds((place * stripes + stripe) * page_len, page_len)],
            sem.at[place * stripes + stripe],
        )
        for place, block in enumerate(blocks)
        for stripe in range(stripes)
    ]


def scale_rows(rows_in, gained, gain_in, span):
    wide_gain = gain_in[...].astype(F32).reshape(1, gain_in.shape[0])
    gained[span] = (rows_in[span].astype(F32) * wide_gain).astype(BF16)


def put_squares(rows_in, span, out, first):
    rows = out.shape[0] - LINES
    squares = jnp.zeros((rows, LANES), F32)
    for lane in range(rows_in.shape[1] // LANES):
        part = rows_in[span, lane * LANES : (lane + 1) * LANES].astype(F32)
        squares = squares + part * part
    total = jnp.sum(squares.T, axis=0, keepdims=True)
    high = total.astype(BF16).astype(F32)
    place = lax.broadcasted_iota(jnp.int32, (LINES, LANES), 0) - first
    lines = jnp.where(place == 0, high, jnp.where(place == 1, total - high, 0.0))
    rest = jnp.zeros((LINES, out.shape[1] - LANES), F32)
    out[rows:] = jnp.concatenate([lines, rest], axis=1).astype(BF16)


def is_inner(shard):
    return (shard == 1) | (shard == 2)


def far_blocks(shard):
    lower = shard < 2
    return jnp.where(lower, 2, 1), jnp.where(lower, 3, 0)


def first_kernel(hidden, gain, weight, out, gained, tile, rows_in, gain_in, row_sem, gain_sem, tile_sem):
    shard = lax.axis_index("shard")
    half = weight.shape[1] // 2
    inner_block, outer_block = far_blocks(shard)
    rows_here = row_copies(hidden, [jnp.where(is_inner(shard), outer_block, inner_block)], rows_in, row_sem)
    piece = half // 2
    pieces = [slice(index * piece, (index + 1) * piece) for index in range(2)]
    tile_copies = [
        pltpu.make_async_copy(weight.at[:, columns], tile.at[:, columns], tile_sem.at[index])
        for index, columns in enumerate(pieces)
    ]
    gain_copy = pltpu.make_async_copy(gain, gain_in, gain_sem)
    gain_copy.start()
    for copy in rows_here + tile_copies:
        copy.start()
    gain_copy.wait()
    for copy in rows_here:
        copy.wait()
    scale_rows(rows_in, gained, gain_in, slice(None))
    put_squares(rows_in, slice(None), out, 0)
    for copy, columns in zip(tile_copies, pieces):
        copy.wait()
        product = jnp.dot(gained[...], tile[:, columns], preferred_element_type=F32)
        out[: gained.shape[0], columns] = product.astype(BF16)


def project_first(hidden, gain, weight):
    stripes, blocks, page_len, features = hidden.shape
    half = weight.shape[1] // 2
    rows = stripes * page_len
    return pl.pallas_call(
        first_kernel,
        in_specs=[whole(pl.ANY)] * 3,
        out_specs=[whole()] * 3,
        out_shape=[
            jax.ShapeDtypeStruct((rows + LINES, half), BF16),
            jax.ShapeDtypeStruct((rows, features), BF16),
            jax.ShapeDtypeStruct((features, half), BF16),
        ],
        scratch_shapes=[
            pltpu.VMEM((rows, features), BF16),
            pltpu.VMEM((features,), BF16),
            pltpu.SemaphoreType.DMA((stripes,)),
            pltpu.SemaphoreType.DMA,
            pltpu.SemaphoreType.DMA((2,)),
        ],
        compiler_params=pltpu.CompilerParams(vmem_limit_bytes=LIMIT),
        cost_estimate=SMALL,
        name="project_first",
    )(hidden, gain, weight)


def head_spread(query, width):
    heads = query.shape[0]
    group = heads // (width // LANES)
    head = lax.broadcasted_iota(jnp.int32, (heads, LANES), 0)
    pieces = [jnp.where(head // group == g, query, jnp.zeros_like(query)) for g in range(width // LANES)]
    return jnp.concatenate(pieces, axis=1)


def head_pick(products):
    heads, width = products.shape
    group = heads // (width // LANES)
    head = lax.broadcasted_iota(jnp.int32, (heads, LANES), 0)
    picked = products[:, :LANES]
    for g in range(1, width // LANES):
        picked = jnp.where(head // group == g, products[:, g * LANES : (g + 1) * LANES], picked)
    return picked


def score(query, key_rows):
    spread = head_spread(query, key_rows.shape[1])
    scores = lax.dot_general(spread, key_rows, (((1,), (1,)), ((), ())), preferred_element_type=F32)
    return scores * (1.0 / math.sqrt(LANES))


def attend(query, key_rows, value_rows, usable):
    scores = jnp.where(usable, score(query, key_rows), FLOOR_SCORE)
    largest = jnp.max(scores, axis=1, keepdims=True)
    weights = jnp.where(usable, jnp.exp(scores - largest), 0.0)
    total = jnp.sum(weights, axis=1, keepdims=True)
    picked = head_pick(jnp.dot(weights.astype(BF16), value_rows, preferred_element_type=F32))
    some = total > 0.0
    safe = jnp.where(some, total, 1.0)
    return picked / safe, jnp.where(some, largest + jnp.log(safe), FLOOR_SCORE)


def split_lines(lines, first):
    high = lines.astype(BF16).astype(F32)
    middle_part = (lines - high).astype(BF16).astype(F32)
    low = lines - high - middle_part
    place = lax.broadcasted_iota(jnp.int32, lines.shape, 0) - first
    return jnp.where(place == 0, high, jnp.where(place == 1, middle_part, jnp.where(place == 2, low, 0.0)))


def join_lines(tail, first, rows):
    line = jnp.sum(tail[first : first + 3].astype(F32), axis=0, keepdims=True)
    return jnp.broadcast_to(line, (LANES, LANES)).T[:rows]


def project_keys_kernel(hidden, gain, weight, sent, key_tile, *rest):
    own, near, third, values, gained, value_tile = rest[:6]
    rows_in, gain_in, row_sem, gain_sem, tile_sem = rest[6:]
    shard = lax.axis_index("shard")
    rows = values.shape[0]
    half = weight.shape[1] // 2
    inner_block, outer_block = far_blocks(shard)
    blocks = [shard, jnp.bitwise_xor(shard, 1), jnp.where(is_inner(shard), inner_block, outer_block)]
    rows_here = row_copies(hidden, blocks, rows_in, row_sem)
    tile_copy = pltpu.make_async_copy(weight.at[:, pl.ds(half, half)], value_tile, tile_sem)
    gain_copy = pltpu.make_async_copy(gain, gain_in, gain_sem)
    gain_copy.start()
    for copy in rows_here + [tile_copy]:
        copy.start()
    gain_copy.wait()
    for copy in rows_here:
        copy.wait()
    scale_rows(rows_in, gained, gain_in, slice(None))
    product = jnp.dot(gained[...], key_tile[...], preferred_element_type=F32).astype(BF16)
    for place, ref in enumerate((own, near, third)):
        ref[:rows] = product[place * rows : (place + 1) * rows]
    for place, ref in enumerate((own, near, third)):
        span = slice(place * rows, (place + 1) * rows)
        put_squares(rows_in, span, ref, 2 if place == 2 else 0)
    tile_copy.wait()
    values[...] = jnp.dot(sent[...], value_tile[...], preferred_element_type=F32).astype(BF16)


def project_keys(hidden, gain, weight, sent, tile):
    stripes, blocks, page_len, features = hidden.shape
    half = weight.shape[1] // 2
    rows = stripes * page_len
    return pl.pallas_call(
        project_keys_kernel,
        in_specs=[whole(pl.ANY)] * 3 + [whole()] * 2,
        out_specs=[whole()] * 6,
        out_shape=[jax.ShapeDtypeStruct((rows + LINES, half), BF16)] * 3
        + [
            jax.ShapeDtypeStruct((rows, half), BF16),
            jax.ShapeDtypeStruct((3 * rows, features), BF16),
            jax.ShapeDtypeStruct((features, half), BF16),
        ],
        scratch_shapes=[
            pltpu.VMEM((3 * rows, features), BF16),
            pltpu.VMEM((features,), BF16),
            pltpu.SemaphoreType.DMA((3 * stripes,)),
            pltpu.SemaphoreType.DMA,
            pltpu.SemaphoreType.DMA,
        ],
        compiler_params=pltpu.CompilerParams(vmem_limit_bytes=LIMIT),
        cost_estimate=SMALL,
        name="project_keys",
    )(hidden, gain, weight, sent, tile)


def project_values_kernel(gained, tile, *rest):
    product = jnp.dot(gained[...], tile[...], preferred_element_type=F32).astype(BF16)
    rows = rest[-1].shape[0]
    for place, ref in enumerate(rest[-3:]):
        ref[...] = product[place * rows : (place + 1) * rows]


def project_values(gained, tile, after):
    return pl.pallas_call(
        project_values_kernel,
        in_specs=[whole()] * 2 + [whole(pl.ANY)] * len(after),
        out_specs=[whole()] * 3,
        out_shape=[jax.ShapeDtypeStruct((gained.shape[0] // 3, tile.shape[1]), BF16)] * 3,
        compiler_params=pltpu.CompilerParams(vmem_limit_bytes=LIMIT),
        cost_estimate=SMALL,
        name="project_values",
    )(gained, tile, *after)


def carry_kernel(mine, first, *rest):
    inner = is_inner(lax.axis_index("shard"))
    arrived = jnp.where(inner, first[...].astype(F32), 0.0)
    rest[-1][...] = (mine[...].astype(F32) + arrived).astype(BF16)


def carry(mine, first, after):
    return pl.pallas_call(
        carry_kernel,
        in_specs=[whole(), whole()] + [whole(pl.ANY)] * len(after),
        out_specs=whole(),
        out_shape=jax.ShapeDtypeStruct(mine.shape, BF16),
        compiler_params=pltpu.CompilerParams(vmem_limit_bytes=LIMIT),
        cost_estimate=SMALL,
        name="carry",
    )(mine, first, *after)


def rep_shapes(rows, width):
    return [jax.ShapeDtypeStruct((rows, width), BF16)] * 4


def ask_kernel(jobs, table, query, *rest):
    outs, marks, places = rest[-6:-2], rest[-2], rest[-1]
    slots = query.shape[0]
    replica = lax.axis_index("rep")
    line = lax.broadcasted_iota(jnp.int32, marks.shape, 0)
    found = jnp.zeros(marks.shape, jnp.int32)
    place_line = lax.broadcasted_iota(jnp.int32, places.shape, 0)
    spots = jnp.full(places.shape, -1, jnp.int32)
    for step, out in enumerate(outs):
        hit, context, page = job_from(jobs, step)
        out[...] = query[context]
        sent = jobs[0, replica * SENDS] == jnp.bitwise_xor(replica, step)
        found = found + jnp.where(line == step * slots + context, hit.astype(jnp.int32), 0)
        found = found + jnp.where(line == 4 * slots + step, sent.astype(jnp.int32), 0)
        spots = jnp.where(place_line == step, jnp.where(hit, table[page, context], -1), spots)
    marks[...] = found.astype(F32)
    places[...] = spots


def ask(jobs, table, query, after):
    return pl.pallas_call(
        ask_kernel,
        in_specs=[whole(SMEM)] * 2 + [whole()] + [whole(pl.ANY)] * len(after),
        out_specs=[whole()] * 6,
        out_shape=rep_shapes(*query.shape[1:])
        + [
            jax.ShapeDtypeStruct((4 * query.shape[0] + 8, LANES), F32),
            jax.ShapeDtypeStruct((8, LANES), jnp.int32),
        ],
        compiler_params=pltpu.CompilerParams(vmem_limit_bytes=LIMIT),
        cost_estimate=SMALL,
        name="ask",
    )(jobs, table, query, *after)


def kept_kernel(jobs, table, lengths, query, pool, *rest, shards, after):
    outs = rest[after : after + 4]
    new_pool, pages, total, level, in_sem, out_sem = rest[after + 4 :]
    slots, heads, _ = query.shape
    here = heads // shards
    rows = slots * here
    replica = lax.axis_index("rep")
    shard = lax.axis_index("shard")
    page_len = pool.shape[1]
    half = pool.shape[2] // 2

    def copy_in(context, page):
        place = context * 2 + page
        return pltpu.make_async_copy(pool.at[table[page, context]], pages.at[place], in_sem.at[place])

    def copy_out(context, page):
        place = context * 2 + page
        return pltpu.make_async_copy(pages.at[place], new_pool.at[table[page, context]], out_sem.at[place])

    @pl.loop(0, slots)
    def _(context):
        for page in range(2):
            copy_in(context, page).start()

    lane = lax.broadcasted_iota(jnp.int32, (heads, 2 * page_len), 1)
    page_of = lane // page_len
    position = (page_of * shards + shard) * page_len + lane % page_len

    def context_part(context):
        gone = [jnp.int32(0), jnp.int32(0)]
        for job in range(jobs.shape[1]):
            hit = (jobs[0, job] == replica) & (jobs[1, job] == context)
            for page in range(2):
                gone[page] = gone[page] | (hit & (jobs[2, job] == page)).astype(jnp.int32)
        usable = (position < lengths[context]) & (jnp.where(page_of == 0, gone[0], gone[1]) == 0)
        both = pages[pl.ds(context * 2, 2)].reshape(2 * page_len, 2 * half)
        return attend(query[context], both[:, :half], both[:, half:], usable)

    @pl.loop(0, slots // GROUP)
    def _(index):
        contexts = [index * GROUP + member for member in range(GROUP)]
        for context in contexts:
            for page in range(2):
                copy_in(context, page).wait()
                copy_out(context, page).start()
        results = [context_part(context) for context in contexts]
        for context, (result, logarithm) in zip(contexts, results):
            total[context] = result
            level[context] = jnp.broadcast_to(logarithm, result.shape)

    for step, out in enumerate(outs):
        start = pl.multiple_of(jnp.bitwise_xor(shard, step) * here, here)
        out[:rows] = total[:, pl.ds(start, here), :].reshape(rows, LANES).astype(BF16)
        lines = level[:, pl.ds(start, here), :].reshape(rows, LANES).T[:16]
        out[rows:] = split_lines(lines, 0).astype(BF16)

    @pl.loop(0, slots)
    def _(context):
        for page in range(2):
            copy_out(context, page).wait()


def kept(jobs, table, lengths, query, pool, after, shards):
    slots, heads, size = query.shape
    return pl.pallas_call(
        functools.partial(kept_kernel, shards=shards, after=len(after)),
        in_specs=[whole(SMEM)] * 3 + [whole()] + [whole(pl.ANY)] * (1 + len(after)),
        out_specs=[whole()] * 4 + [whole(pl.ANY)],
        out_shape=[jax.ShapeDtypeStruct((slots * heads // shards + 16, size), BF16)] * 4
        + [jax.ShapeDtypeStruct(pool.shape, pool.dtype)],
        scratch_shapes=[
            pltpu.VMEM((slots * 2,) + pool.shape[1:], pool.dtype),
            pltpu.VMEM(query.shape, F32),
            pltpu.VMEM(query.shape, F32),
            pltpu.SemaphoreType.DMA((slots * 2,)),
            pltpu.SemaphoreType.DMA((slots * 2,)),
        ],
        compiler_params=pltpu.CompilerParams(vmem_limit_bytes=LIMIT),
        cost_estimate=SMALL,
        name="kept",
    )(jobs, table, lengths, query, pool, *after)


def route(jobs, finished, outs):
    replica = lax.axis_index("rep")
    page_len = finished.shape[0] // SENDS
    for step, out in enumerate(outs):
        chosen = jobs[0, replica * SENDS] == jnp.bitwise_xor(replica, step)

        @pl.when(chosen)
        def _():
            out[...] = finished[:page_len]

        @pl.when(jnp.logical_not(chosen))
        def _():
            out[...] = finished[page_len:]


def add_parts(own, near, first, third, rows, columns):
    direct = jnp.where(is_inner(lax.axis_index("shard")), 0.0, first[rows, columns].astype(F32))
    parts = [ref[rows, columns].astype(F32) for ref in (own, near, third)]
    return (parts[0] + parts[1]) + (parts[2] + direct)


def finish_keys_kernel(jobs, own, near, first, third, frequency, *rest, stripe):
    asked, outs = rest[:4], rest[4:8]
    scale, weights_out, share, tails, finished, level = rest[8:]
    replica = lax.axis_index("rep")
    shard = lax.axis_index("shard")
    rows, width = finished.shape
    page_len = rows // SENDS

    def added(span, columns):
        return add_parts(own, near, first, third, span, columns)

    squares = jnp.sum(added(slice(rows, rows + LINES), slice(0, LANES)), axis=0, keepdims=True)
    squares = jnp.broadcast_to(squares, (LANES, LANES)).T[:rows]
    inverse = lax.rsqrt(squares / D + EPS)
    scale[...] = inverse
    row = lax.broadcasted_iota(jnp.int32, (rows, LANES), 0)
    lane = lax.broadcasted_iota(jnp.int32, (rows, LANES), 1)
    index = jnp.where(row < page_len, jobs[2, replica * SENDS], jobs[2, replica * SENDS + 1])
    position = index * stripe + shard * page_len + row % page_len
    angle = position.astype(F32) * frequency[...]
    cosine = jnp.cos(angle) * inverse
    sine_part = jnp.where(lane < LANES // 2, -jnp.sin(angle), jnp.sin(angle)) * inverse
    for head in range(width // LANES):
        columns = slice(head * LANES, (head + 1) * LANES)
        value = added(slice(0, rows), columns)
        turned = value * cosine + pltpu.roll(value, LANES // 2, 1) * sine_part
        finished[:, columns] = turned.astype(BF16)
    route(jobs, finished, outs)
    for send in range(SENDS):
        step = jnp.bitwise_xor(jobs[0, replica * SENDS + send], replica)
        query = asked[0][...]
        for other in range(1, 4):
            query = jnp.where(step == other, asked[other][...], query)
        scores = score(query, finished[send * page_len : (send + 1) * page_len])
        largest = jnp.max(scores, axis=1, keepdims=True)
        weights = jnp.exp(scores - largest)
        total = jnp.sum(weights, axis=1, keepdims=True)
        weights_out[send] = weights.astype(BF16)
        share[send] = jnp.broadcast_to(1.0 / total, share.shape[1:])
        level[send] = jnp.broadcast_to(largest + jnp.log(total), level.shape[1:])
    here = level.shape[1] // tails.shape[0]
    count = SENDS * here
    for step in range(tails.shape[0]):
        start = pl.multiple_of(jnp.bitwise_xor(shard, step) * here, here)
        mine = level[:, pl.ds(start, here), :].reshape(count, LANES)
        around = [jnp.zeros((rows_, LANES), F32) for rows_ in (step * count, LANES - (step + 1) * count)]
        pieces = [piece for piece in (around[0], mine, around[1]) if piece.shape[0]]
        tails[step] = split_lines(jnp.concatenate(pieces, axis=0).T[:16], 3)


def finish_values_kernel(marks, own, near, first, third, scale, weights, share, tails, *rest, shards, after):
    kept_parts, outs = rest[:4], rest[4 + after : 8 + after]
    packed, finished, result = rest[8 + after : 12 + after], rest[12 + after], rest[13 + after]
    shard = lax.axis_index("shard")
    page_len = own.shape[0] // SENDS
    sent = [marks[marks.shape[0] - 8 + step : marks.shape[0] - 7 + step] > 0.0 for step in range(4)]
    for head in range(own.shape[1] // LANES):
        columns = slice(head * LANES, (head + 1) * LANES)
        total = add_parts(own, near, first, third, slice(None), columns) * scale[...]
        finished[:, columns] = total.astype(BF16)
        for step, out in enumerate(outs):
            out[:, columns] = jnp.where(sent[step], total[:page_len], total[page_len:]).astype(BF16)
    for send in range(SENDS):
        products = jnp.dot(
            weights[send], finished[send * page_len : (send + 1) * page_len], preferred_element_type=F32
        )
        result[send] = head_pick(products) * share[send]
    here = share.shape[1] // shards
    count = SENDS * here
    rows = kept_parts[0].shape[0] - 16
    for step in range(4):
        start = pl.multiple_of(jnp.bitwise_xor(shard, step) * here, here)
        packed[step][:rows] = kept_parts[step][:rows]
        packed[step][rows : rows + count] = result[:, pl.ds(start, here), :].reshape(count, LANES).astype(BF16)
        packed[step][rows + count :] = (kept_parts[step][rows:].astype(F32) + tails[step]).astype(BF16)


def finish_keys(jobs, parts, frequency, asked, stripe, shards):
    rows, width = parts[0].shape[0] - LINES, parts[0].shape[1]
    heads = asked[0].shape[0]
    page_len = rows // SENDS
    return pl.pallas_call(
        functools.partial(finish_keys_kernel, stripe=stripe),
        in_specs=[whole(SMEM)] + [whole()] * 9,
        out_specs=[whole()] * 8,
        out_shape=rep_shapes(page_len, width)
        + [
            jax.ShapeDtypeStruct((rows, LANES), F32),
            jax.ShapeDtypeStruct((SENDS, heads, page_len), BF16),
            jax.ShapeDtypeStruct((SENDS, heads, LANES), F32),
            jax.ShapeDtypeStruct((shards, 16, LANES), F32),
        ],
        scratch_shapes=[pltpu.VMEM((rows, width), BF16), pltpu.VMEM((SENDS, heads, LANES), F32)],
        compiler_params=pltpu.CompilerParams(vmem_limit_bytes=LIMIT),
        cost_estimate=SMALL,
        name="finish_keys",
    )(jobs, *parts, frequency, *asked)


def finish_values(marks, parts, scale, weights, share, tails, kept_parts, after, shards):
    rows, width = parts[0].shape
    heads = share.shape[1]
    page_len = rows // SENDS
    packed = kept_parts[0].shape[0] + SENDS * heads // shards
    return pl.pallas_call(
        functools.partial(finish_values_kernel, shards=shards, after=len(after)),
        in_specs=[whole()] * 13 + [whole(pl.ANY)] * len(after),
        out_specs=[whole()] * 8,
        out_shape=rep_shapes(page_len, width) + [jax.ShapeDtypeStruct((packed, LANES), BF16)] * 4,
        scratch_shapes=[pltpu.VMEM((rows, width), BF16), pltpu.VMEM((SENDS, heads, LANES), F32)],
        compiler_params=pltpu.CompilerParams(vmem_limit_bytes=LIMIT),
        cost_estimate=SMALL,
        name="finish_values",
    )(marks, *parts, scale, weights, share, tails, *kept_parts, *after)


def job_from(jobs, step):
    replica = lax.axis_index("rep")
    first = jnp.bitwise_xor(replica, step) * SENDS
    hit_first = jobs[0, first] == replica
    hit = hit_first | (jobs[0, first + 1] == replica)
    row = jnp.where(hit_first, first, first + 1)
    return hit, jobs[1, row], jobs[2, row]


def place_kernel(places, pool, *rest):
    key_pages, value_pages = rest[:4], rest[4:8]
    out, done, pages, sem = rest[8:]
    half = key_pages[0].shape[1]
    spots = [jnp.max(places[step : step + 1]) for step in range(4)]
    done[...] = jnp.zeros_like(done)
    for wait in (False, True):
        for step, spot in enumerate(spots):

            @pl.when(spot >= 0)
            def _():
                copy = pltpu.make_async_copy(pages.at[step], out.at[spot], sem.at[step])
                if wait:
                    copy.wait()
                else:
                    pages[step, :, :half] = key_pages[step][...]
                    pages[step, :, half:] = value_pages[step][...]
                    copy.start()


def place_pages(places, pool, key_pages, value_pages):
    return pl.pallas_call(
        place_kernel,
        in_specs=[whole(), whole(pl.ANY)] + [whole()] * 8,
        out_specs=[whole(pl.ANY), whole()],
        out_shape=[jax.ShapeDtypeStruct(pool.shape, pool.dtype), jax.ShapeDtypeStruct((16, LANES), BF16)],
        scratch_shapes=[pltpu.VMEM((4,) + pool.shape[1:], pool.dtype), pltpu.SemaphoreType.DMA((4,))],
        input_output_aliases={1: 0},
        compiler_params=pltpu.CompilerParams(vmem_limit_bytes=LIMIT),
        cost_estimate=SMALL,
        name="place_pages",
    )(places, pool, *key_pages, *value_pages)


def blend(parts, levels):
    top = functools.reduce(jnp.maximum, levels)
    shares = [jnp.exp(level - top) for level in levels]
    both = functools.reduce(jnp.add, shares)
    total = functools.reduce(jnp.add, [part * share for part, share in zip(parts, shares)])
    return total / both, top + jnp.log(both)


def gather_kernel(marks, *refs, rows, count):
    parts, page, outs, page_out = refs[:4], refs[4], refs[5:9], refs[9]
    page_out[...] = page[...]
    tail = functools.reduce(jnp.add, [ref[rows + count :].astype(F32) for ref in parts])
    levels = join_lines(tail, 3, LANES)
    mixed, level = blend(
        [ref[rows : rows + count].astype(F32) for ref in parts],
        [levels[step * count : (step + 1) * count] for step in (0, 2, 3, 1)],
    )
    here = count // SENDS
    lane = lax.broadcasted_iota(jnp.int32, (here, LANES), 1)
    for step, out in enumerate(outs):
        chosen = marks[marks.shape[0] - 8 + step : marks.shape[0] - 7 + step] > 0.0
        total = jnp.where(chosen, level[:here], level[here:])
        high = total.astype(BF16).astype(F32)
        middle_part = (total - high).astype(BF16).astype(F32)
        low = total - high - middle_part
        out[:, :LANES] = jnp.where(chosen, mixed[:here], mixed[here:]).astype(BF16)
        out[:, LANES:] = jnp.where(
            lane == 0, high, jnp.where(lane == 1, middle_part, jnp.where(lane == 2, low, 0.0))
        ).astype(BF16)


def gather_parts(marks, parts, page, rows, count):
    return pl.pallas_call(
        functools.partial(gather_kernel, rows=rows, count=count),
        in_specs=[whole()] * 6,
        out_specs=[whole()] * 5,
        out_shape=rep_shapes(count // SENDS, 2 * LANES) + [jax.ShapeDtypeStruct(page.shape, BF16)],
        compiler_params=pltpu.CompilerParams(vmem_limit_bytes=LIMIT),
        cost_estimate=SMALL,
        name="gather_parts",
    )(marks, *parts, page)


def blend_kernel(*refs, rows, count):
    parts, after, kept_out, kept_level = refs[:4], refs[4], refs[5], refs[6]
    mixed, level = blend(
        [ref[:rows].astype(F32) for ref in parts], [join_lines(ref[rows + count :], 0, rows) for ref in parts]
    )
    kept_out[...] = mixed
    kept_level[...] = level


def blend_kept(parts, after, rows, count):
    return pl.pallas_call(
        functools.partial(blend_kernel, rows=rows, count=count),
        in_specs=[whole()] * 4 + [whole(pl.ANY)],
        out_specs=[whole()] * 2,
        out_shape=[jax.ShapeDtypeStruct((rows, LANES), F32)] * 2,
        compiler_params=pltpu.CompilerParams(vmem_limit_bytes=LIMIT),
        cost_estimate=SMALL,
        name="blend_kept",
    )(*parts, after)


FRESH_ORDER = (0, 2, 3, 1)


def combine_kernel(marks, kept_out, kept_level, *refs):
    parts, out, mixed = refs[:4], refs[5], refs[6]
    slots, here, size = mixed.shape
    spans = [slice(context * here, (context + 1) * here) for context in range(slots)]
    blended = []
    for step, ref in zip(FRESH_ORDER, parts):
        hits = [marks[step * slots + context : step * slots + context + 1] > 0.0 for context in range(slots)]
        old, old_level = jnp.zeros((here, size), F32), jnp.zeros((here, size), F32)
        for hit, span in zip(hits, spans):
            old = jnp.where(hit, kept_out[span], old)
            old_level = jnp.where(hit, kept_level[span], old_level)
        fresh_level = jnp.sum(ref[:, LANES:].astype(F32), axis=1, keepdims=True)
        fresh_level = jnp.broadcast_to(fresh_level, (here, size))
        result, _ = blend([old, ref[:, :LANES].astype(F32)], [old_level, fresh_level])
        blended.append((hits, result))
    for context, span in enumerate(spans):
        total = kept_out[span]
        for hits, result in blended:
            total = jnp.where(hits[context], result, total)
        mixed[context] = total
    for head in range(here):
        out[:, head * size : (head + 1) * size] = mixed[:, head, :].astype(BF16)


def combine(marks, kept_out, kept_level, parts, after, slots):
    here = kept_out.shape[0] // slots
    return pl.pallas_call(
        combine_kernel,
        in_specs=[whole()] * 7 + [whole(pl.ANY)],
        out_specs=whole(),
        out_shape=jax.ShapeDtypeStruct((slots, here * LANES), BF16),
        scratch_shapes=[pltpu.VMEM((slots, here, LANES), F32)],
        compiler_params=pltpu.CompilerParams(vmem_limit_bytes=LIMIT),
        cost_estimate=SMALL,
        name="combine",
    )(marks, kept_out, kept_level, *parts, after)


def on_device(
    hidden, norm_gain, kv_weight, restore_jobs, page_table, context_lengths, queries, kv_pool
):
    shards = lax.axis_size("shard")
    replicas = lax.axis_size("rep")
    stripe = hidden.shape[0] // SENDS
    page_len = stripe // shards
    kv_weight = pltpu.with_memory_space_constraint(kv_weight, pltpu.HBM)
    kv_pool = pltpu.with_memory_space_constraint(kv_pool, pltpu.HBM)
    gain = pltpu.with_memory_space_constraint(norm_gain, pltpu.HBM)
    blocks = pltpu.with_memory_space_constraint(
        hidden.reshape(SENDS, shards, page_len, hidden.shape[1]), pltpu.HBM
    )
    jobs = restore_jobs.T
    table = page_table[:, :, 0].T
    slots = queries.shape[0]
    query = queries.reshape(slots, QH, HD)

    def along(array, pairs):
        return lax.ppermute(array, "shard", pairs)

    def across(array, step):
        return lax.ppermute(array, "rep", [(i, i ^ step) for i in range(replicas)])

    def between(arrays):
        return [arrays[0]] + [across(arrays[step], step) for step in range(1, replicas)]

    key_sent, gained_sent, key_tile = project_first(blocks, gain, kv_weight)
    key_first = along(key_sent, FIRST)
    key_0, key_1, key_2, value_sent, gained, tile = project_keys(
        blocks, gain, kv_weight, gained_sent, key_tile
    )
    value_first = along(value_sent, FIRST)
    key_near = along(key_1, NEAR)
    key_2 = carry(key_2, key_first, [])
    key_third = along(key_2, THIRD)
    *asked, marks, places = ask(jobs, table, query, [key_2])
    asked = between(asked)
    value_0, value_1, value_2 = project_values(gained, tile, [asked[0], value_first])
    value_near = along(value_1, NEAR)
    value_2 = carry(value_2, value_first, asked[1:])
    value_third = along(value_2, THIRD)
    *kept_parts, new_pool = kept(jobs, table, context_lengths, query, kv_pool, [value_2], shards)
    frequency = THETA ** (-(jnp.arange(HD // 2, dtype=F32) * 2.0 / HD))
    frequency = jnp.concatenate([frequency, frequency])[None, :]
    *key_out, scale, weights, share, tails = finish_keys(
        jobs, (key_0, key_near, key_first, key_third), frequency, asked, stripe, shards
    )
    key_pages = between(key_out)
    finished = finish_values(
        marks,
        (value_0, value_near, value_first, value_third),
        scale,
        weights,
        share,
        tails,
        kept_parts,
        key_pages[1:],
        shards,
    )
    value_pages = [finished[0], None, across(finished[2], 2), across(finished[3], 3)]
    packed = finished[4:]
    parts = [packed[0]] + [
        along(packed[step], [(i, i ^ step) for i in range(shards)]) for step in (2, 3, 1)
    ]
    here = QH // shards
    *gathered, near_page = gather_parts(marks, parts, finished[1], slots * here, SENDS * here)
    fresh = [gathered[0]] + [across(gathered[step], step) for step in FRESH_ORDER[1:]]
    value_pages[1] = across(near_page, 1)
    kept_out, kept_level = blend_kept(parts, gathered[0], slots * here, SENDS * here)
    new_pool, placed = place_pages(places, new_pool, key_pages, value_pages)
    return (new_pool, combine(marks, kept_out, kept_level, fresh, placed, slots))


def solution(mesh):
    in_specs = (
        P(("outer", "rep"), "shard"),
        P("shard"),
        P("shard", None),
        P("outer", None),
        P(("outer", "rep"), None, "shard"),
        P(("outer", "rep")),
        P(("outer", "rep"), None),
        P(("outer", "rep", "shard"), None, None),
    )
    out_specs = (P(("outer", "rep", "shard"), None, None), P(("outer", "rep"), "shard"))
    fast = mesh.shape["shard"] == 4 and mesh.shape["rep"] == 4
    return jax.shard_map(
        on_device if fast else on_device_general, mesh=mesh, in_specs=in_specs, out_specs=out_specs, check_vma=False
    )
```
